32 devices in a mesh: rows: 4 (over z), cols: 8 (over y, x, core).
Axes of the slice: x: 2, y: 2, z: 4, core: 2. Of those that a mesh axis runs over, the one named last changes fastest.
Arguments:
- tokens: bfloat16 [32, 256, 192], P('rows', 'cols'), may hold values from -60 to 60
- region_ids: int32 [32, 256], P('rows', 'cols'), may hold values from 0 to 2
- upper_rim: bfloat16 [4, 256, 192], P(None, 'cols'), may hold values from -60 to 60
- upper_ids: int32 [4, 256], P(None, 'cols'), may hold values from 0 to 2
- lower_rim: bfloat16 [4, 256, 192], P(None, 'cols'), may hold values from -60 to 60
- lower_ids: int32 [4, 256], P(None, 'cols'), may hold values from 0 to 2
- cotangent: bfloat16 [32, 256, 192], P('rows', 'cols'), may hold values from -6 to 6
- qkv_weight: bfloat16 [2, 192, 576], replicated, may hold values from -0.4375 to 0.4375
- proj_weight: bfloat16 [2, 192, 192], replicated, may hold values from -0.4375 to 0.4375
- inner_weight: bfloat16 [2, 192, 768], replicated, may hold values from -0.4375 to 0.4375
- outer_weight: bfloat16 [2, 768, 192], replicated, may hold values from -0.21875 to 0.21875
- bias_table: float32 [2, 225, 6], replicated, may hold values from -4 to 400
Outputs:
- token_grad: bfloat16 [32, 256, 192], P('rows', 'cols')
- qkv_grad: float32 [2, 192, 576], P(None, 'rows', 'cols')
- proj_grad: float32 [2, 192, 192], P(None, 'rows', 'cols')
- inner_grad: float32 [2, 192, 768], P(None, 'rows', 'cols')
- outer_grad: float32 [2, 768, 192], P(None, 'rows', 'cols')
- table_grad: float32 [2, 225, 6], replicated
The draws below stay inside these ranges and needn't reach their ends.
All inputs are finite; a program needn't handle non-finite values.
Results may differ from the reference program's by a relative error of at most 0.03.
Values may be sent and summed in bfloat16 or wider, within the bound.
No kernel may reach another device: no remote copies, remote signals or barrier semaphores. Data moves between devices by JAX's collectives and lax.ppermute only.
A program may use at most 64 MiB of HBM per device.

```python
import math
import jax
import jax.numpy as jnp
from jax import lax

C = 192
HEADS = 6
HID = 768
WIN = 8
HALF = 4
BIAS_LEN = 225
NROWS = 32
NCOL = 256
NTILES = 32


def feature_field(key, tag_number, shape):
    chan_key = jax.random.fold_in(key, 101)
    own_key = jax.random.fold_in(key, tag_number)
    scale_key, raw_key = jax.random.split(own_key)
    channel_scale = 0.5 * jnp.exp(jax.random.uniform(chan_key, (C,), jnp.float32) * math.log(10.0))
    token_scale = 0.3 * jnp.exp(jax.random.uniform(scale_key, shape[:-1] + (1,), jnp.float32) * math.log(10.0))
    raw_values = jnp.clip(jax.random.normal(raw_key, shape, jnp.float32), -4.0, 4.0)
    return raw_values * token_scale * channel_scale


def draw_tokens(key, part):
    return feature_field(key, 1, (NROWS, NCOL, C)).astype(jnp.bfloat16)


def draw_upper_rim(key, part):
    return feature_field(key, 2, (HALF, NCOL, C)).astype(jnp.bfloat16)


def draw_lower_rim(key, part):
    return feature_field(key, 3, (HALF, NCOL, C)).astype(jnp.bfloat16)


def draw_bias_table(key, part):
    table_key = jax.random.fold_in(key, 7)
    raw_values = jnp.clip(jax.random.normal(table_key, (2, BIAS_LEN, HEADS), jnp.float32), -4.0, 4.0)
    return raw_values


def place_ends(drawn, key, smallest, high):
    spot = [jax.random.randint(jax.random.fold_in(key, axis), (), 0, length) for axis, length in enumerate(drawn.shape)]
    widest = drawn.shape.index(max(drawn.shape))
    next_to = spot[:widest] + [(spot[widest] + 1) % drawn.shape[widest]] + spot[widest + 1:]
    return drawn.at[tuple(spot)].set(smallest).at[tuple(next_to)].set(high)


def raised(result, stream_key, source, target, blocks, factor):
    def block_of(position):
        return (jnp.arange(result.shape[position]) // (result.shape[position] // blocks)).reshape((-1,) + (1,) * (result.ndim - 1 - position))

    near = jax.random.permutation(stream_key, blocks)[block_of(target)]
    second = (block_of(target) + blocks // 2) % blocks
    return jnp.where((block_of(source) == near) | (block_of(source) == second), factor * result, result)


def shard_levels(stream_key, shape, shards, least, high):
    def one(axis_at, shards_of):
        draws = jax.random.uniform(jax.random.fold_in(jax.random.fold_in(stream_key, 6), axis_at), (shards_of,), jnp.float32, least / len(shards), high / len(shards))
        return jnp.repeat(jnp.exp(draws), shape[axis_at] // shards_of).reshape((-1,) + (1,) * (len(shape) - axis_at - 1))

    level = one(*shards[0])
    for cut in shards[1:]:
        level = level * one(*cut)
    return level


def normal_values(key, dims, width, reach, shards=(), kind=jnp.bfloat16):
    level = shard_levels(key, dims, shards, -0.22, 0.18) if shards else 1.0
    entries = jax.random.normal(key, dims, jnp.float32) * width * level
    return jnp.minimum(jnp.maximum(entries, -reach), reach).astype(kind)


def gaussian_with(key, extent, scale, bound, pieces, heavy, kind=jnp.bfloat16):
    array = scale * jax.random.normal(key, extent, jnp.float32)
    if pieces:
        array = array * shard_levels(key, extent, pieces, -0.22, 0.18)
    return jnp.clip(raised(array, jax.random.fold_in(key, 3), *heavy), -bound, bound).astype(kind)


def setup_inputs(seed: int = 0) -> dict:
    splits = jax.random.split(jax.random.key(seed), 13)
    return {
        "tokens": draw_tokens(jax.random.fold_in(splits[12], 71), 0),
        "region_ids": place_ends(jax.random.randint(splits[1], (NROWS, NCOL), 0, 3), jax.random.fold_in(splits[1], 1), 0, 2).astype(jnp.int32),
        "upper_rim": draw_upper_rim(jax.random.fold_in(splits[12], 71), 0),
        "upper_ids": place_ends(jax.random.randint(splits[3], (HALF, NCOL), 0, 3), jax.random.fold_in(splits[3], 1), 0, 2).astype(jnp.int32),
        "lower_rim": draw_lower_rim(jax.random.fold_in(splits[12], 71), 0),
        "lower_ids": place_ends(jax.random.randint(splits[5], (HALF, NCOL), 0, 3), jax.random.fold_in(splits[5], 1), 0, 2).astype(jnp.int32),
        "cotangent": gaussian_with(splits[6], (NROWS, NCOL, C), 1.0, 6.0, ((0, 4), (1, 8)), (1, 2, 8, 2.0)),
        "qkv_weight": normal_values(splits[7], (2, C, 3 * C), C ** -0.5, 0.4375),
        "proj_weight": normal_values(splits[8], (2, C, C), C ** -0.5, 0.4375),
        "inner_weight": normal_values(splits[9], (2, C, HID), C ** -0.5, 0.4375),
        "outer_weight": normal_values(splits[10], (2, HID, C), HID ** -0.5, 0.21875),
        "bias_table": draw_bias_table(jax.random.fold_in(splits[12], 71), 0),
    }


EPS = 1e-05
MASKED = -1000000000.0

def rounded(values):
    return lax.optimization_barrier(values.astype(jnp.bfloat16)).astype(jnp.float32)

def normalize(values):
    center = lax.optimization_barrier(jnp.mean(values, axis=-1, keepdims=True))
    shifted = values - center
    spread = lax.optimization_barrier(jnp.mean(shifted * shifted, axis=-1, keepdims=True))
    return shifted * lax.rsqrt(spread + EPS)

def norm_back(source, grad_norm):
    _, pullback = jax.vjp(normalize, source.astype(jnp.float32))
    return pullback(grad_norm)[0]

def by_transpose(left, right):
    return lax.dot_general(left, right, (((1,), (1,)), ((), ())), preferred_element_type=jnp.float32)

def over_rows(left, right):
    return lax.dot_general(left, right, (((0,), (0,)), ((), ())), preferred_element_type=jnp.float32)

def windows(surface):
    grid_rows, grid_cols = (surface.shape[0], surface.shape[1])
    trailing = surface.shape[2:]
    blocked = surface.reshape((grid_rows // WIN, WIN, grid_cols // WIN, WIN) + trailing)
    permute = (0, 2, 1, 3) + tuple(range(4, 4 + len(trailing)))
    return blocked.transpose(permute).reshape((grid_rows // WIN * (grid_cols // WIN), WIN * WIN) + trailing)

def unwindows(framed, grid_rows, grid_cols):
    trailing = framed.shape[2:]
    blocked = framed.reshape((grid_rows // WIN, grid_cols // WIN, WIN, WIN) + trailing)
    permute = (0, 2, 1, 3) + tuple(range(4, 4 + len(trailing)))
    return blocked.transpose(permute).reshape((grid_rows, grid_cols) + trailing)

def relative_onehot():
    places = jnp.arange(WIN * WIN, dtype=jnp.int32)
    pos_row = places // WIN
    pos_col = places % WIN
    lookup = (pos_row[:, None] - pos_row[None, :] + WIN - 1) * (2 * WIN - 1) + pos_col[:, None] - pos_col[None, :] + WIN - 1
    return (lookup[:, :, None] == jnp.arange(BIAS_LEN, dtype=jnp.int32)[None, None, :]).astype(jnp.float32)

def attend(normed_win, ids_win, qkv_weight, pos_bias):
    window_count, window_size, channels = normed_win.shape
    head_count = pos_bias.shape[0]
    head_size = channels // head_count
    score_scale = head_size ** (-0.5)
    qkv_all = jnp.dot(normed_win.reshape(window_count * window_size, channels), qkv_weight, preferred_element_type=jnp.float32)
    qkv_all = rounded(qkv_all).reshape(window_count, window_size, 3, head_count, head_size)
    scores = jnp.einsum('nqhd,nkhd->nhqk', qkv_all[:, :, 0], qkv_all[:, :, 1])
    scores = scores * score_scale + pos_bias[None]
    same_region = ids_win[:, :, None] == ids_win[:, None, :]
    scores = jnp.where(same_region[:, None], scores, MASKED)
    row_max = lax.optimization_barrier(jnp.max(scores, axis=-1, keepdims=True))
    exponent = jnp.exp(scores - row_max)
    attn_probs = exponent / lax.optimization_barrier(jnp.sum(exponent, axis=-1, keepdims=True))
    attn_out = jnp.einsum('nhqk,nkhd->nqhd', rounded(attn_probs), qkv_all[:, :, 2])
    return (qkv_all, attn_probs, attn_out.astype(jnp.bfloat16).reshape(window_count, window_size, channels))

def attend_back(normed_win, qkv_all, attn_probs, grad_out, qkv_weight):
    window_count, window_size, channels = normed_win.shape
    head_count, head_size = (qkv_all.shape[3], qkv_all.shape[4])
    score_scale = head_size ** (-0.5)
    grad_heads = grad_out.astype(jnp.float32).reshape(window_count, window_size, head_count, head_size)
    grad_probs = jnp.einsum('nqhd,nkhd->nhqk', grad_heads, qkv_all[:, :, 2])
    grad_scores = attn_probs * (grad_probs - lax.optimization_barrier(jnp.sum(grad_probs * attn_probs, axis=-1, keepdims=True)))
    grad_bias = lax.optimization_barrier(jnp.sum(grad_scores, axis=0))
    scores_low = rounded(grad_scores)
    grad_query = jnp.einsum('nhqk,nkhd->nqhd', scores_low, qkv_all[:, :, 1]) * score_scale
    grad_key = jnp.einsum('nhqk,nqhd->nkhd', scores_low, qkv_all[:, :, 0]) * score_scale
    grad_value = jnp.einsum('nhqk,nqhd->nkhd', rounded(attn_probs), grad_heads)
    grad_qkv = jnp.stack([grad_query, grad_key, grad_value], axis=2).astype(jnp.bfloat16)
    grad_qkv = grad_qkv.reshape(window_count * window_size, 3 * channels)
    flattened = normed_win.reshape(window_count * window_size, channels)
    grad_norm = by_transpose(grad_qkv, qkv_weight)
    grad_weight = over_rows(flattened, grad_qkv)
    return (grad_norm.reshape(window_count, window_size, channels), grad_weight, grad_bias)

def mixer_forward(surface, region, qkv_weight, table):
    grid_rows, grid_cols = (surface.shape[0], surface.shape[1])
    normed = normalize(surface.astype(jnp.float32)).astype(jnp.bfloat16)
    pos_bias = jnp.einsum('ijb,bh->hij', relative_onehot(), table, precision=lax.Precision.HIGHEST)
    qkv_all, attn_probs, attn_out = attend(windows(normed), windows(region), qkv_weight, pos_bias)
    return (normed, qkv_all, attn_probs, unwindows(attn_out, grid_rows, grid_cols))

def mixer_backward(surface, normed, qkv_all, attn_probs, grad_mix, qkv_weight):
    grid_rows, grid_cols = (surface.shape[0], surface.shape[1])
    grad_norm, grad_weight, grad_bias = attend_back(windows(normed), qkv_all, attn_probs, windows(grad_mix), qkv_weight)
    grad_surface = norm_back(surface, unwindows(grad_norm, grid_rows, grid_cols))
    grad_table = jnp.einsum('ijb,hij->bh', relative_onehot(), grad_bias, precision=lax.Precision.HIGHEST)
    return (grad_surface, grad_weight, grad_table)

def channel_forward(middle, inner_w, outer_w):
    normed = normalize(middle.astype(jnp.float32)).astype(jnp.bfloat16)
    hidden_pre = jnp.dot(normed, inner_w, preferred_element_type=jnp.float32)
    hidden_act = jax.nn.gelu(hidden_pre, approximate=False).astype(jnp.bfloat16)
    output = (middle.astype(jnp.float32) + jnp.dot(hidden_act, outer_w, preferred_element_type=jnp.float32)).astype(jnp.bfloat16)
    return (normed, hidden_pre, hidden_act, output)

def channel_backward(middle, normed, hidden_pre, hidden_act, grad_out, inner_w, outer_w):
    grad_act = by_transpose(grad_out, outer_w)
    grad_outer = over_rows(hidden_act, grad_out)
    _, pullback = jax.vjp(lambda inputs: jax.nn.gelu(inputs, approximate=False), hidden_pre)
    grad_pre = pullback(grad_act)[0].astype(jnp.bfloat16)
    grad_norm = by_transpose(grad_pre, inner_w)
    grad_inner = over_rows(normed, grad_pre)
    grad_middle = (grad_out.astype(jnp.float32) + norm_back(middle, grad_norm)).astype(jnp.bfloat16)
    return (grad_middle, grad_inner, grad_outer)

def reference(tokens, region_ids, upper_rim, upper_ids, lower_rim, lower_ids, cotangent, qkv_weight, proj_weight, inner_weight, outer_weight, bias_table):
    grid_rows, grid_cols, channels = tokens.shape
    normed_one, qkv_one, probs_one, mix_one = mixer_forward(tokens, region_ids, qkv_weight[0], bias_table[0])
    mix_flat_one = mix_one.reshape(grid_rows * grid_cols, channels)
    middle_one = (tokens.reshape(-1, channels).astype(jnp.float32) + jnp.dot(mix_flat_one, proj_weight[0], preferred_element_type=jnp.float32)).astype(jnp.bfloat16)
    chan_one = channel_forward(middle_one, inner_weight[0], outer_weight[0])
    first_out = chan_one[3].reshape(grid_rows, grid_cols, channels)
    extended = jnp.concatenate([upper_rim, first_out, lower_rim], axis=0)
    ext_region = jnp.concatenate([upper_ids, region_ids, lower_ids], axis=0)
    shifted = jnp.roll(extended, -HALF, axis=1)
    shifted_ids = jnp.roll(ext_region, -HALF, axis=1)
    normed_two, qkv_two, probs_two, mix_ext = mixer_forward(shifted, shifted_ids, qkv_weight[1], bias_table[1])
    mix_two = jnp.roll(mix_ext, HALF, axis=1)[HALF:HALF + grid_rows]
    mix_flat_two = mix_two.reshape(grid_rows * grid_cols, channels)
    middle_two = (chan_one[3].astype(jnp.float32) + jnp.dot(mix_flat_two, proj_weight[1], preferred_element_type=jnp.float32)).astype(jnp.bfloat16)
    chan_two = channel_forward(middle_two, inner_weight[1], outer_weight[1])
    grad_out = cotangent.reshape(-1, channels)
    grad_mid_two, inner_two, outer_two = channel_backward(middle_two, chan_two[0], chan_two[1], chan_two[2], grad_out, inner_weight[1], outer_weight[1])
    proj_two = over_rows(mix_flat_two, grad_mid_two)
    grad_mix_two = by_transpose(grad_mid_two, proj_weight[1]).astype(jnp.bfloat16).reshape(grid_rows, grid_cols, channels)
    grad_mix_ext = jnp.roll(jnp.pad(grad_mix_two, ((HALF, HALF), (0, 0), (0, 0))), -HALF, axis=1)
    grad_shift, qkv_two_grad, table_two = mixer_backward(shifted, normed_two, qkv_two, probs_two, grad_mix_ext, qkv_weight[1])
    folded = jnp.roll(grad_shift, HALF, axis=1)[HALF:HALF + grid_rows]
    grad_first = (grad_mid_two.reshape(grid_rows, grid_cols, channels).astype(jnp.float32) + folded).astype(jnp.bfloat16)
    grad_mid_one, inner_one, outer_one = channel_backward(middle_one, chan_one[0], chan_one[1], chan_one[2], grad_first.reshape(-1, channels), inner_weight[0], outer_weight[0])
    proj_one = over_rows(mix_flat_one, grad_mid_one)
    grad_mix_one = by_transpose(grad_mid_one, proj_weight[0]).astype(jnp.bfloat16).reshape(grid_rows, grid_cols, channels)
    grad_tokens, qkv_one_grad, table_one = mixer_backward(tokens, normed_one, qkv_one, probs_one, grad_mix_one, qkv_weight[0])
    token_grad = (grad_mid_one.reshape(grid_rows, grid_cols, channels).astype(jnp.float32) + grad_tokens).astype(jnp.bfloat16)
    tile_count = NTILES * 1.0
    qkv_grad = jnp.stack([qkv_one_grad, qkv_two_grad]) / tile_count
    proj_grad = jnp.stack([proj_one, proj_two]) / tile_count
    inner_grad = jnp.stack([inner_one, inner_two]) / tile_count
    outer_grad = jnp.stack([outer_one, outer_two]) / tile_count
    table_grad = jnp.stack([table_one, table_two]) / tile_count
    return (token_grad, qkv_grad, proj_grad, inner_grad, outer_grad, table_grad)
```

```python
import functools
import math

import jax
import jax.numpy as jnp
from jax import lax
from jax.experimental import pallas as pl
from jax.experimental.pallas import tpu as pltpu
from jax.sharding import PartitionSpec as P

WIN = 8
HALF = 4
TOK = WIN * WIN
SPAN = 2 * WIN - 1
LANES = 128
EPS = 1e-05
MASKED = -1000000000.0
F32 = jnp.float32
BF16 = jnp.bfloat16
VMEM_LIMIT = 40 * 1024 * 1024


def nn(left, right):
    return lax.dot_general(left, right, (((1,), (0,)), ((), ())), preferred_element_type=F32)


def nt(left, right):
    return lax.dot_general(left, right, (((1,), (1,)), ((), ())), preferred_element_type=F32)


def tn(left, right):
    return lax.dot_general(left, right, (((0,), (0,)), ((), ())), preferred_element_type=F32)


def iota(shape, dim):
    return lax.broadcasted_iota(jnp.int32, shape, dim)


def ones_where(condition):
    return jnp.where(condition, 1.0, 0.0).astype(BF16)


def norm(values):
    shifted = values - jnp.mean(values, axis=-1, keepdims=True)
    inverse = lax.rsqrt(jnp.mean(shifted * shifted, axis=-1, keepdims=True) + EPS)
    return shifted * inverse, inverse


def norm_back(unit, inverse, grad):
    mean_grad = jnp.mean(grad, axis=-1, keepdims=True)
    mean_unit = jnp.mean(grad * unit, axis=-1, keepdims=True)
    return inverse * (grad - mean_grad - unit * mean_unit)


def to_windows(grid):
    rows, cols, channels = grid.shape
    return jnp.concatenate(
        [
            grid[a : a + WIN, b : b + WIN].reshape(TOK, channels)
            for a in range(0, rows, WIN)
            for b in range(0, cols, WIN)
        ],
        axis=0,
    )


def from_windows(framed, rows, cols):
    per_band = cols // WIN
    bands = []
    for a in range(rows // WIN):
        pieces = [
            framed[(a * per_band + b) * TOK : (a * per_band + b + 1) * TOK].reshape(WIN, WIN, -1)
            for b in range(per_band)
        ]
        bands.append(jnp.concatenate(pieces, axis=1))
    return jnp.concatenate(bands, axis=0) if len(bands) > 1 else bands[0]


def lane_tiles(channels, size):
    tiles = []
    for start in range(0, channels, LANES):
        width = min(LANES, channels - start)
        tiles.append((start, width, start // size * TOK, (start + width) // size * TOK))
    return tiles


def spread(part, size):
    lane = iota((1, part.shape[1]), 1)
    copies = [
        part * ones_where((lane >= first) & (lane < first + size))
        for first in range(0, part.shape[1], size)
    ]
    return jnp.concatenate(copies, axis=0)


def collect(stacked, size):
    width = stacked.shape[1]
    heads = width // size
    lane = iota((TOK, width), 1)
    total = stacked[(heads - 1) * TOK :]
    for head in reversed(range(heads - 1)):
        total = jnp.where(lane < (head + 1) * size, stacked[head * TOK : (head + 1) * TOK], total)
    return total


def attend(query, key, value, bias, same, size):
    scale = size ** (-0.5)
    tiles = lane_tiles(query.shape[1], size)
    parts = []
    for start, width, first, last in tiles:
        scores = nt(key[:, start : start + width], spread(query[:, start : start + width], size))
        for at in range(first, last, LANES):
            part = scores[:, at - first : at - first + LANES] * scale + bias[:, at : at + LANES]
            part = jnp.where(same, part, MASKED)
            exponent = jnp.exp(part - jnp.max(part, axis=0, keepdims=True))
            parts.append(exponent * (1.0 / jnp.sum(exponent, axis=0, keepdims=True)))
    probs = jnp.concatenate(parts, axis=1)
    low = probs.astype(BF16)
    mix = [
        collect(tn(low[:, first:last], value[:, start : start + width]), size)
        for start, width, first, last in tiles
    ]
    return probs, jnp.concatenate(mix, axis=1).astype(BF16)


def attend_back(query, key, value, probs, grad_mix, size):
    scale = size ** (-0.5)
    grads = ([], [], [])
    terms = []
    for start, width, first, last in lane_tiles(query.shape[1], size):
        part = slice(start, start + width)
        grad_heads = spread(grad_mix[:, part], size)
        chance = probs[:, first:last]
        grad_probs = nt(value[:, part], grad_heads)
        term = chance * (grad_probs - jnp.sum(grad_probs * chance, axis=0, keepdims=True))
        low = term.astype(BF16)
        grads[0].append(collect(tn(low, key[:, part]), size) * scale)
        grads[1].append(nn(low, spread(query[:, part], size)) * scale)
        grads[2].append(nn(chance.astype(BF16), grad_heads))
        terms.append(term)
    return [jnp.concatenate(g, axis=1).astype(BF16) for g in grads], jnp.concatenate(terms, axis=1)


def same_region(ids):
    rows, cols = ids.shape
    masks = []
    row = iota((TOK, cols), 0)
    col = iota((TOK, cols), 1)
    lift = ones_where(iota((TOK, WIN), 0) // WIN == iota((TOK, WIN), 1))
    ones = jnp.ones((cols, LANES), BF16)
    for a in range(0, rows, WIN):
        band = ids[a : a + WIN].astype(BF16)
        lifted = nn(lift, band)
        for b in range(0, cols, WIN):
            picked = jnp.where(col == b + (row & (WIN - 1)), lifted, 0.0).astype(BF16)
            down = nn(picked, ones)
            tiled = nn(
                band,
                ones_where(iota((cols, LANES), 0) == b + (iota((cols, LANES), 1) & (WIN - 1))),
            )
            own = iota((WIN, LANES), 0) == ((iota((WIN, LANES), 1) // WIN) & (WIN - 1))
            across = jnp.sum(jnp.where(own, tiled, 0.0), axis=0, keepdims=True)
            masks.append(down == across)
    return masks


def split(values, count):
    parts = []
    for _ in range(count):
        low = values.astype(BF16)
        parts.append(low)
        values = values - low.astype(F32)
    return parts


def offset_rows(length):
    place = iota((length, 2 * LANES), 0)
    row = (place * 4370) >> 16
    return ones_where(iota((length, 2 * LANES), 1) == 2 * WIN * row + place - SPAN * row)


def offset_places():
    lane = iota((2 * LANES, WIN * LANES), 1)
    row = ((lane >> 3) & (WIN - 1)) - (lane >> 7) + WIN - 1
    return ones_where(iota((2 * LANES, WIN * LANES), 0) == 2 * WIN * row + (lane & (WIN - 1)))


def expand_bias(table):
    length, heads = table.shape
    onehot = offset_rows(length)
    rows = sum(tn(part, onehot) for part in split(table, 3))
    base = jnp.concatenate(
        [jnp.broadcast_to(rows[h : h + 1], (WIN, 2 * LANES)) for h in range(heads)], axis=0
    )
    place = iota(base.shape, 0) & (WIN - 1)
    rolled = base
    for c in range(WIN - 1):
        rolled = jnp.where(place == c, pltpu.roll(base, c + 2 * LANES - WIN + 1, 1), rolled)
    places = offset_places()
    spreaded = sum(nn(part, places) for part in split(rolled, 3))
    left = iota((WIN, LANES), 1) < TOK
    columns = []
    for h in range(0, heads, 2):
        pieces = [
            jnp.where(
                left,
                spreaded[h * WIN : (h + 1) * WIN, r * LANES : (r + 1) * LANES],
                spreaded[(h + 1) * WIN : (h + 2) * WIN, r * LANES : (r + 1) * LANES],
            )
            for r in range(WIN)
        ]
        columns.append(jnp.concatenate(pieces, axis=0))
    return jnp.concatenate(columns, axis=1)


def fold_bias(grad):
    heads = grad.shape[1] // TOK
    left = iota((WIN, LANES), 1) < TOK
    rows = []
    for h in range(heads):
        at = h // 2 * LANES
        pieces = []
        for r in range(WIN):
            piece = grad[r * WIN : (r + 1) * WIN, at : at + LANES]
            pieces.append(jnp.where(left, piece, 0.0) if h % 2 == 0 else jnp.where(left, 0.0, piece))
        rows.append(jnp.concatenate(pieces, axis=1))
    stacked = jnp.concatenate(rows, axis=0)
    places = offset_places()
    folded = sum(nt(part, places) for part in split(stacked, 3))
    place = iota(folded.shape, 0) & (WIN - 1)
    rolled = folded
    for c in range(WIN - 1):
        rolled = jnp.where(place == c, pltpu.roll(folded, WIN - 1 - c, 1), rolled)
    sums = [
        jnp.sum(rolled[h * WIN : (h + 1) * WIN], axis=0, keepdims=True) for h in range(heads)
    ]
    sums.append(jnp.zeros((WIN - heads, 2 * LANES), F32))
    return jnp.concatenate(sums, axis=0)


def table_rows(table, width):
    parts = [part.astype(F32) for part in split(table, 2)]
    if width == LANES:
        return jnp.concatenate([p[:, a : a + LANES] for p in parts for a in (0, LANES)], axis=0)
    pad = jnp.zeros((WIN, width - 2 * LANES), F32)
    return jnp.concatenate([jnp.concatenate([p, pad], axis=1) for p in parts], axis=0)


def rows_table(rows):
    if rows.shape[1] == LANES:
        rows = jnp.concatenate(
            [
                jnp.concatenate([rows[:WIN], rows[WIN : 2 * WIN]], axis=1),
                jnp.concatenate([rows[2 * WIN : 3 * WIN], rows[3 * WIN :]], axis=1),
            ],
            axis=0,
        )
    return rows[:WIN, : 2 * LANES] + rows[WIN : 2 * WIN, : 2 * LANES]


def halved(blocks, bit, table, send_ref, keep_ref):
    tail = table_rows(table, blocks[0].shape[1])
    low = bit == 0
    send = [jnp.where(low, blocks[i + 1], blocks[i]) for i in range(0, len(blocks), 2)]
    keep = [jnp.where(low, blocks[i], blocks[i + 1]) for i in range(0, len(blocks), 2)]
    send_ref[...] = jnp.concatenate(send + [tail], axis=0).astype(BF16)
    keep_ref[...] = jnp.concatenate(keep + [tail], axis=0).astype(BF16)


def pack_terms(qkv, inner, proj, outer, count):
    blocks = []
    for c in range(count):
        parts = []
        for term in (qkv, inner, proj):
            size = term.shape[0] // count
            parts.append(term[c * size : (c + 1) * size])
        block = jnp.concatenate(parts, axis=0)
        half = block.shape[0] // 2
        block = jnp.concatenate([block[:half], block[half:]], axis=1)
        size = outer.shape[0] // count
        wide = outer[c * size : (c + 1) * size]
        parts = [wide[:, a : a + block.shape[1]] for a in range(0, wide.shape[1], block.shape[1])]
        blocks.append(jnp.concatenate([block] + parts, axis=0))
    return blocks


def row_blocks(block, half, channels, hidden, count):
    low = block[:half]
    size = (block.shape[0] - half) * block.shape[1] // hidden
    wide = jnp.concatenate(
        [block[half + a : half + a + size] for a in range(0, block.shape[0] - half, size)], axis=1
    )
    thin = channels // count
    broad = hidden // count
    blocks = []
    for r in range(count):
        pair = jnp.concatenate(
            [
                low[:, r * thin : (r + 1) * thin],
                low[:, channels + r * thin : channels + (r + 1) * thin],
            ],
            axis=1,
        )
        parts = [
            wide[:, r * broad + a : r * broad + a + 2 * thin] for a in range(0, broad, 2 * thin)
        ]
        out = jnp.concatenate([pair] + parts, axis=0)
        blocks.append(
            jnp.concatenate([out, jnp.zeros((out.shape[0], LANES - 2 * thin), F32)], axis=1)
        )
    return blocks


def first_kernel(
    tokens,
    ids,
    cotangent,
    qkv_w,
    proj_w,
    inner_w,
    outer_w,
    table,
    first_out,
    up,
    down,
    query_out,
    key_out,
    value_out,
    probs_out,
    mix_out,
    middle_out,
    pre_out,
    act_out,
    edge,
):
    rows, cols, channels = tokens.shape
    heads = table.shape[2]
    size = channels // heads
    count = rows * cols
    surface = to_windows(tokens[...].astype(F32))
    normed = norm(surface)[0].astype(BF16)
    bias = expand_bias(table[0])
    masks = same_region(ids[...].astype(F32))
    query, key, value = (
        nn(normed, qkv_w[0, :, i * channels : (i + 1) * channels]).astype(BF16) for i in range(3)
    )
    query_out[...] = query
    key_out[...] = key
    value_out[...] = value
    mixes = []
    for w in range(count // TOK):
        at = slice(w * TOK, (w + 1) * TOK)
        probs, mix = attend(query[at], key[at], value[at], bias, masks[w], size)
        probs_out[w] = probs
        mixes.append(mix)
    mix = jnp.concatenate(mixes, axis=0)
    mix_out[...] = mix
    middle = (surface + nn(mix, proj_w[0])).astype(BF16)
    middle_out[...] = middle
    normed = norm(middle.astype(F32))[0].astype(BF16)
    outs = []
    for at in range(0, count, 2 * TOK):
        pre = nn(normed[at : at + 2 * TOK], inner_w[0])
        pre_out[at : at + 2 * TOK] = pre
        act = (0.5 * pre * (1.0 + lax.erf(pre * math.sqrt(0.5)))).astype(BF16)
        act_out[at : at + 2 * TOK] = act
        outs.append(nn(act, outer_w[0]))
    result = (middle.astype(F32) + jnp.concatenate(outs, axis=0)).astype(BF16).astype(F32)
    grid = from_windows(result, rows, cols)
    first_out[...] = grid.astype(BF16)
    grads = cotangent[...].astype(F32)
    marks = ids[...].astype(F32)
    for ref, start in ((up, 0), (down, rows - HALF)):
        edge[...] = jnp.zeros(edge.shape, F32)
        for i in range(HALF):
            edge[i * cols : (i + 1) * cols, :channels] = grid[start + i]
            edge[i * cols : (i + 1) * cols, channels:] = grads[start + i]
        edge[HALF * cols : HALF * cols + HALF, :cols] = marks[start : start + HALF]
        ref[...] = edge[...].astype(BF16)


def edge_kernel(
    first_out,
    cotangent,
    ids,
    upper_rim,
    upper_ids,
    lower_rim,
    lower_ids,
    from_up,
    from_down,
    up,
    down,
    to_left,
    to_right,
    ext_ids,
    edge,
    marks,
):
    rows, cols, channels = first_out.shape
    index = lax.axis_index("rows")
    at_top = index == 0
    at_bottom = index == lax.axis_size("rows") - 1
    grid = first_out[...].astype(F32)
    grads = cotangent[...].astype(F32)
    marks[HALF : HALF + rows, :] = ids[...].astype(F32)
    bands = []
    for at_end, rim, rim_ids, source, target, place in (
        (at_top, upper_rim, upper_ids, from_up, up, 0),
        (at_bottom, lower_rim, lower_ids, from_down, down, HALF + rows),
    ):
        got = source[...].astype(F32)
        wide = HALF * cols
        tokens = jnp.where(at_end, rim[...].astype(F32).reshape(wide, channels), got[:wide, :channels])
        rest = jnp.where(at_end, 0.0, got[:wide, channels:])
        band = jnp.concatenate([tokens, rest], axis=1)
        target[...] = band.astype(BF16)
        marks[place : place + HALF, :] = jnp.where(
            at_end, rim_ids[...].astype(F32), got[wide : wide + HALF, :cols]
        )
        bands.append(band)
    ext_ids[...] = marks[...]
    total = rows + 2 * HALF
    for ref, start in ((to_left, 0), (to_right, cols - HALF)):
        edge[...] = jnp.zeros(edge.shape, F32)
        for i in range(total):
            here = slice(i * HALF, (i + 1) * HALF)
            if HALF <= i < HALF + rows:
                edge[here, :channels] = grid[i - HALF, start : start + HALF]
                edge[here, channels:] = grads[i - HALF, start : start + HALF]
            else:
                band, row = (bands[0], i) if i < HALF else (bands[1], i - HALF - rows)
                edge[here, :] = band[row * cols + start : row * cols + start + HALF]
        edge[total * HALF : total * HALF + total, :cols] = marks[...]
        ref[...] = edge[...].astype(BF16)


def side_kernel(table, pre, bias, slope, keeps):
    bias[...] = expand_bias(table[1])
    count = pre.shape[0]
    for at in range(0, count, TOK):
        x = pre[at : at + TOK]
        slope[at : at + TOK] = 0.5 * (1.0 + lax.erf(x * math.sqrt(0.5))) + x * (
            jnp.exp(-0.5 * x * x) * (1.0 / math.sqrt(2.0 * math.pi))
        )


def own_windows(rows, cols, channels, low, high):
    per_band = (cols + 2 * HALF) // WIN
    masks = []
    for a in range((rows + 2 * HALF) // WIN):
        for b in range(per_band):
            token = iota((TOK, channels), 0)
            row = a * WIN + (token >> 3)
            col = b * WIN + (token & (WIN - 1))
            masks.append((row >= low) & (row < high) & (col >= HALF) & (col < HALF + cols))
    return jnp.concatenate([ones_where(mask) for mask in masks], axis=0)


def second_kernel(
    first_out,
    cotangent,
    up,
    down,
    left,
    right,
    ext_ids,
    bias_ref,
    qkv_w,
    proj_w,
    inner_w,
    outer_w,
    grad_out,
    send,
    keep,
    xs,
    cs,
    probs_s,
):
    rows, cols, channels = first_out.shape
    total, wide = rows + 2 * HALF, cols + 2 * HALF
    width = bias_ref.shape[1]
    size = channels // (width // TOK)
    hidden = inner_w.shape[2]
    for ref, source, at in ((xs, first_out, 0), (cs, cotangent, channels)):
        part = slice(at, at + channels)
        ref[HALF : HALF + rows, HALF : HALF + cols, :] = source[...].astype(F32)
        for edge, place in ((up, 0), (down, HALF + rows)):
            band = edge[...].astype(F32)[:, part]
            for i in range(HALF):
                ref[place + i, HALF : HALF + cols, :] = band[i * cols : (i + 1) * cols]
        for edge, place in ((left, 0), (right, HALF + cols)):
            band = edge[...].astype(F32)[:, part]
            for i in range(total):
                ref[i, place : place + HALF, :] = band[i * HALF : (i + 1) * HALF]
    tail = slice(total * HALF, total * HALF + total)
    source_col = iota((cols, wide), 0)
    target_col = iota((cols, wide), 1)
    marks = sum(
        nn(values.astype(BF16), ones_where(target_col == source_col + shift))
        for values, shift in (
            (left[...].astype(F32)[tail, :cols], HALF - cols),
            (ext_ids[...], HALF),
            (right[...].astype(F32)[tail, :cols], HALF + cols),
        )
    )
    masks = same_region(marks)
    bias = bias_ref[...]
    surface = to_windows(xs[...])
    grad = to_windows(cs[...]).astype(BF16)
    count = surface.shape[0]
    unit_one, inverse_one = norm(surface)
    normed_one = unit_one.astype(BF16)
    weights = [qkv_w[1, :, i * channels : (i + 1) * channels] for i in range(3)]
    query, key, value = (nn(normed_one, w).astype(BF16) for w in weights)
    mixes = []
    for w in range(count // TOK):
        at = slice(w * TOK, (w + 1) * TOK)
        probs, mix = attend(query[at], key[at], value[at], bias, masks[w], size)
        probs_s[w] = probs
        mixes.append(mix)
    mix = jnp.concatenate(mixes, axis=0)
    middle = (surface + nn(mix, proj_w[1])).astype(BF16).astype(F32)
    unit_two, inverse_two = norm(middle)
    normed_two = unit_two.astype(BF16)
    acts, grad_pres, grad_norms = [], [], []
    for at in range(0, count, 2 * TOK):
        here = slice(at, at + 2 * TOK)
        pre = nn(normed_two[here], inner_w[1])
        cdf = 0.5 * (1.0 + lax.erf(pre * math.sqrt(0.5)))
        acts.append((pre * cdf).astype(BF16))
        slope = cdf + pre * (jnp.exp(-0.5 * pre * pre) * (1.0 / math.sqrt(2.0 * math.pi)))
        grad_pre = (slope * nt(grad[here], outer_w[1])).astype(BF16)
        grad_pres.append(grad_pre)
        grad_norms.append(nt(grad_pre, inner_w[1]))
    act = jnp.concatenate(acts, axis=0)
    grad_pre = jnp.concatenate(grad_pres, axis=0)
    grad_norm = jnp.concatenate(grad_norms, axis=0)
    grad_middle = (grad.astype(F32) + norm_back(unit_two, inverse_two, grad_norm)).astype(BF16)
    index = lax.axis_index("rows")
    last = lax.axis_size("rows") - 1
    per_band = wide // WIN
    raw = nt(grad_middle, proj_w[1])
    grad_mixes = []
    for w in range(count // TOK):
        row = w // per_band * WIN + (iota((TOK, channels), 0) >> 3)
        low = jnp.where(index == 0, HALF, 0)
        high = jnp.where(index == last, HALF + rows, total)
        part = jnp.where((row >= low) & (row < high), raw[w * TOK : (w + 1) * TOK], 0.0)
        grad_mixes.append(part.astype(BF16))
    grads = ([], [], [])
    bias_sum = jnp.zeros((TOK, width), F32)
    for w in range(count // TOK):
        at = slice(w * TOK, (w + 1) * TOK)
        parts, term = attend_back(query[at], key[at], value[at], probs_s[w], grad_mixes[w], size)
        for total_list, part in zip(grads, parts):
            total_list.append(part)
        lane = iota((1, width), 1)
        row = w // per_band * WIN + ((lane >> 3) & (WIN - 1))
        col = w % per_band * WIN + (lane & (WIN - 1))
        own = (row >= HALF) & (row < HALF + rows) & (col >= HALF) & (col < HALF + cols)
        bias_sum = bias_sum + term * jnp.where(own, 1.0, 0.0)
    grads = [jnp.concatenate(g, axis=0) for g in grads]
    grad_norm = sum(nt(g, w) for g, w in zip(grads, weights))
    grad_surface = grad_middle.astype(F32) + norm_back(unit_one, inverse_one, grad_norm)
    xs[...] = from_windows(grad_surface, total, wide)
    grad_out[...] = to_windows(xs[HALF : HALF + rows, HALF : HALF + cols, :]).astype(BF16)
    own = own_windows(rows, cols, channels, HALF, HALF + rows)
    low = jnp.where(index == 0, 0, HALF)
    high = jnp.where(index == last, total, HALF + rows)
    normed_one = normed_one * own_windows(rows, cols, channels, low, high)
    blocks = pack_terms(
        jnp.concatenate([tn(g, normed_one) for g in grads], axis=0),
        tn(grad_pre, normed_two * own),
        tn(grad_middle, mix * own),
        tn(grad * own, act),
        lax.axis_size("cols"),
    )
    halved(blocks, lax.axis_index("cols") & 1, fold_bias(bias_sum), send, keep)


def third_kernel(
    tokens,
    grad_ref,
    query,
    key,
    value,
    probs_ref,
    mix,
    middle_ref,
    act,
    slope,
    qkv_w,
    proj_w,
    inner_w,
    outer_w,
    token_grad,
    send,
    keep,
):
    rows, cols, channels = tokens.shape
    width = probs_ref.shape[2]
    size = channels // (width // TOK)
    count = rows * cols
    grad = grad_ref[...]
    unit_one, inverse_one = norm(to_windows(tokens[...].astype(F32)))
    normed_one = unit_one.astype(BF16)
    unit_two, inverse_two = norm(middle_ref[...].astype(F32))
    normed_two = unit_two.astype(BF16)
    grad_pres, grad_norms = [], []
    for at in range(0, count, 2 * TOK):
        here = slice(at, at + 2 * TOK)
        grad_pre = (slope[here] * nt(grad[here], outer_w[0])).astype(BF16)
        grad_pres.append(grad_pre)
        grad_norms.append(nt(grad_pre, inner_w[0]))
    grad_pre = jnp.concatenate(grad_pres, axis=0)
    grad_norm = jnp.concatenate(grad_norms, axis=0)
    grad_middle = (grad.astype(F32) + norm_back(unit_two, inverse_two, grad_norm)).astype(BF16)
    grad_mix = nt(grad_middle, proj_w[0]).astype(BF16)
    grads = ([], [], [])
    bias_sum = jnp.zeros((TOK, width), F32)
    for w in range(count // TOK):
        at = slice(w * TOK, (w + 1) * TOK)
        parts, term = attend_back(query[at], key[at], value[at], probs_ref[w], grad_mix[at], size)
        for total_list, part in zip(grads, parts):
            total_list.append(part)
        bias_sum = bias_sum + term
    grads = [jnp.concatenate(g, axis=0) for g in grads]
    weights = [qkv_w[0, :, i * channels : (i + 1) * channels] for i in range(3)]
    grad_norm = sum(nt(g, w) for g, w in zip(grads, weights))
    grad_surface = grad_middle.astype(F32) + norm_back(unit_one, inverse_one, grad_norm)
    token_grad[...] = from_windows(grad_surface, rows, cols).astype(BF16)
    blocks = pack_terms(
        jnp.concatenate([tn(g, normed_one) for g in grads], axis=0),
        tn(grad_pre, normed_two),
        tn(grad_middle, mix[...]),
        tn(grad, act[...]),
        lax.axis_size("cols"),
    )
    halved(blocks, lax.axis_index("cols") & 1, fold_bias(bias_sum), send, keep)


def summed(keep, got, tail):
    both = keep[...].astype(F32) + got[...].astype(F32)
    edge = both.shape[0] - tail
    return both[:edge], rows_table(both[edge:])


def cols_kernel(count, bit, keep_in, got, send, keep):
    both, table = summed(keep_in, got, 2 * WIN)
    rows = both.shape[0] // count
    blocks = [both[i * rows : (i + 1) * rows] for i in range(count)]
    halved(blocks, (lax.axis_index("cols") >> bit) & 1, table, send, keep)


def turn_kernel(half, channels, hidden, keep_in, got, send, keep):
    both, table = summed(keep_in, got, 2 * WIN)
    blocks = row_blocks(both, half, channels, hidden, lax.axis_size("rows"))
    halved(blocks, lax.axis_index("rows") & 1, table, send, keep)


def rows_kernel(count, bit, keep_in, got, send, keep):
    both, table = summed(keep_in, got, 4 * WIN)
    rows = both.shape[0] // count
    blocks = [both[i * rows : (i + 1) * rows] for i in range(count)]
    halved(blocks, (lax.axis_index("rows") >> bit) & 1, table, send, keep)


def last_kernel(
    sizes, scale, keep_one, got_one, keep_two, got_two, qkv, proj, inner, outer, table
):
    (qkv_cols, inner_cols, proj_cols), thin, broad = sizes
    for b, (keep, got) in enumerate(((keep_one, got_one), (keep_two, got_two))):
        both, sums = summed(keep, got, 4 * WIN)
        both = both * scale
        half = (qkv_cols + inner_cols + proj_cols) // 2
        low = jnp.concatenate([both[:half, :thin], both[:half, thin : 2 * thin]], axis=0)
        qkv[b] = low[:qkv_cols].T
        inner[b] = low[qkv_cols : qkv_cols + inner_cols].T
        proj[b] = low[qkv_cols + inner_cols :].T
        wide = jnp.concatenate(
            [
                both[half + i * proj_cols : half + (i + 1) * proj_cols, : 2 * thin]
                for i in range(broad // (2 * thin))
            ],
            axis=1,
        )
        outer[b] = wide.T
        heads = table.shape[2]
        onehot = offset_rows(table.shape[1])
        table[b] = sum(nt(onehot, part) for part in split(sums * scale, 3))[:, :heads]


def call(kernel, outs, scratch, *operands):
    return pl.pallas_call(
        kernel,
        out_shape=[jax.ShapeDtypeStruct(shape, kind) for shape, kind in outs],
        scratch_shapes=scratch,
        compiler_params=pltpu.CompilerParams(vmem_limit_bytes=VMEM_LIMIT),
    )(*operands)


def flip(values, axis, bit):
    count = lax.axis_size(axis)
    return lax.ppermute(values, axis, [(i, i ^ (1 << bit)) for i in range(count)])


def ring(values, axis, step, periodic):
    count = lax.axis_size(axis)
    pairs = [(i, (i + step) % count) for i in range(count) if periodic or 0 <= i + step < count]
    return lax.ppermute(values, axis, pairs)


def reduce_terms(send, keep, channels, hidden, half):
    col_count = lax.axis_size("cols")
    row_count = lax.axis_size("rows")
    got = flip(send, "cols", 0)
    left = col_count // 2
    bit = 1
    tail = 2 * WIN
    rows = (keep.shape[0] - tail) // left
    while left > 1:
        shape = ((left // 2 * rows + tail, keep.shape[1]), BF16)
        send, keep = call(functools.partial(cols_kernel, left, bit), [shape, shape], [], keep, got)
        got = flip(send, "cols", bit)
        left //= 2
        bit += 1
    thin = channels // row_count
    broad = hidden // row_count
    rows = half + (rows - half) * keep.shape[1] // hidden * (broad // (2 * thin))
    tail = 4 * WIN
    left = row_count
    shape = ((left // 2 * rows + tail, LANES), BF16)
    send, keep = call(
        functools.partial(turn_kernel, half, channels, hidden), [shape, shape], [], keep, got
    )
    got = flip(send, "rows", 0)
    left //= 2
    bit = 1
    while left > 1:
        shape = ((left // 2 * rows + tail, LANES), BF16)
        send, keep = call(functools.partial(rows_kernel, left, bit), [shape, shape], [], keep, got)
        got = flip(send, "rows", bit)
        left //= 2
        bit += 1
    return keep, got


def local(
    tokens,
    region_ids,
    upper_rim,
    upper_ids,
    lower_rim,
    lower_ids,
    cotangent,
    qkv_weight,
    proj_weight,
    inner_weight,
    outer_weight,
    bias_table,
):
    rows, cols, channels = tokens.shape
    hidden = inner_weight.shape[2]
    length, heads = bias_table.shape[1:]
    col_count = lax.axis_size("cols")
    row_count = lax.axis_size("rows")
    count = rows * cols
    width = heads * TOK
    total = rows + 2 * HALF
    flat = ((count, channels), BF16)
    band = (HALF * cols + 2 * WIN, 2 * channels)
    first_out, up, down, query, key, value, probs, mix, middle, pre, act = call(
        first_kernel,
        [
            ((rows, cols, channels), BF16),
            (band, BF16),
            (band, BF16),
            flat,
            flat,
            flat,
            ((count // TOK, TOK, width), F32),
            flat,
            flat,
            ((count, hidden), F32),
            ((count, hidden), BF16),
        ],
        [pltpu.VMEM(band, F32)],
        tokens,
        region_ids,
        cotangent,
        qkv_weight,
        proj_weight,
        inner_weight,
        outer_weight,
        bias_table,
    )
    from_up = ring(down, "rows", 1, False)
    from_down = ring(up, "rows", -1, False)
    bias, slope = call(
        lambda t, p, b, s: side_kernel(t, p, b, s, None),
        [((TOK, width), F32), ((count, hidden), F32)],
        [],
        bias_table,
        pre,
    )
    strip = (total * HALF + total, 2 * channels)
    up, down, to_left, to_right, ext_ids = call(
        edge_kernel,
        [
            ((HALF * cols, 2 * channels), BF16),
            ((HALF * cols, 2 * channels), BF16),
            (strip, BF16),
            (strip, BF16),
            ((total, cols), F32),
        ],
        [pltpu.VMEM(strip, F32), pltpu.VMEM((total, cols), F32)],
        first_out,
        cotangent,
        region_ids,
        upper_rim,
        upper_ids,
        lower_rim,
        lower_ids,
        from_up,
        from_down,
    )
    left = ring(to_right, "cols", 1, True)
    right = ring(to_left, "cols", -1, True)
    half = (4 * channels + hidden) // col_count // 2
    block_rows = half + channels // col_count * hidden // (2 * channels)
    packed = ((col_count // 2 * block_rows + 2 * WIN, 2 * channels), BF16)
    grid = (total, cols + 2 * HALF, channels)
    grad_first, send_two, keep_two = call(
        second_kernel,
        [flat, packed, packed],
        [
            pltpu.VMEM(grid, F32),
            pltpu.VMEM(grid, F32),
            pltpu.VMEM((grid[0] * grid[1] // TOK, TOK, width), F32),
        ],
        first_out,
        cotangent,
        up,
        down,
        left,
        right,
        ext_ids,
        bias,
        qkv_weight,
        proj_weight,
        inner_weight,
        outer_weight,
    )
    token_grad, send_one, keep_one = call(
        third_kernel,
        [((rows, cols, channels), BF16), packed, packed],
        [],
        tokens,
        grad_first,
        query,
        key,
        value,
        probs,
        mix,
        middle,
        act,
        slope,
        qkv_weight,
        proj_weight,
        inner_weight,
        outer_weight,
    )
    keep_two, got_two = reduce_terms(send_two, keep_two, channels, hidden, half)
    keep_one, got_one = reduce_terms(send_one, keep_one, channels, hidden, half)
    thin = channels // row_count
    broad = hidden // row_count
    sizes = (
        (3 * channels // col_count, hidden // col_count, channels // col_count),
        thin,
        broad,
    )
    qkv_grad, proj_grad, inner_grad, outer_grad, table_grad = call(
        functools.partial(last_kernel, sizes, 1.0 / (row_count * col_count)),
        [
            ((2, thin, sizes[0][0]), F32),
            ((2, thin, sizes[0][2]), F32),
            ((2, thin, sizes[0][1]), F32),
            ((2, broad, sizes[0][2]), F32),
            ((2, length, heads), F32),
        ],
        [],
        keep_one,
        got_one,
        keep_two,
        got_two,
    )
    return token_grad, qkv_grad, proj_grad, inner_grad, outer_grad, table_grad


def solution(mesh):
    return jax.shard_map(
        local,
        mesh=mesh,
        in_specs=(
            P("rows", "cols", None),
            P("rows", "cols"),
            P(None, "cols", None),
            P(None, "cols"),
            P(None, "cols", None),
            P(None, "cols"),
            P("rows", "cols", None),
            P(),
            P(),
            P(),
            P(),
            P(),
        ),
        out_specs=(
            P("rows", "cols", None),
            P(None, "rows", "cols"),
            P(None, "rows", "cols"),
            P(None, "rows", "cols"),
            P(None, "rows", "cols"),
            P(),
        ),
        check_vma=False,
    )
```

```python
import functools
import math

import jax
import jax.numpy as jnp
from jax import lax
from jax.experimental import pallas as pl
from jax.experimental.pallas import tpu as pltpu
from jax.sharding import PartitionSpec as P

WIN = 8
HALF = 4
TOK = WIN * WIN
SPAN = 2 * WIN - 1
LANES = 128
EPS = 1e-05
MASKED = -1000000000.0
F32 = jnp.float32
BF16 = jnp.bfloat16
ARRIVAL = (0, 3, 2, 1)
ORDERED = (0, 3, 2, 1)
VMEM_LIMIT = 40 * 1024 * 1024


def nn(left, right):
    return lax.dot_general(left, right, (((1,), (0,)), ((), ())), preferred_element_type=F32)


def nt(left, right):
    return lax.dot_general(left, right, (((1,), (1,)), ((), ())), preferred_element_type=F32)


def tn(left, right):
    return lax.dot_general(left, right, (((0,), (0,)), ((), ())), preferred_element_type=F32)


def iota(shape, dim):
    return lax.broadcasted_iota(jnp.int32, shape, dim)


def ones_where(condition):
    return jnp.where(condition, 1.0, 0.0).astype(BF16)


def norm(values):
    shifted = values - jnp.mean(values, axis=-1, keepdims=True)
    inverse = lax.rsqrt(jnp.mean(shifted * shifted, axis=-1, keepdims=True) + EPS)
    return shifted * inverse, inverse


def norm_back(unit, inverse, grad):
    mean_grad = jnp.mean(grad, axis=-1, keepdims=True)
    mean_unit = jnp.mean(grad * unit, axis=-1, keepdims=True)
    return inverse * (grad - mean_grad - unit * mean_unit)


def to_windows(grid):
    rows, cols, channels = grid.shape
    return jnp.concatenate(
        [
            grid[a : a + WIN, b : b + WIN].reshape(TOK, channels)
            for a in range(0, rows, WIN)
            for b in range(0, cols, WIN)
        ],
        axis=0,
    )


def from_windows(framed, rows, cols):
    per_band = cols // WIN
    bands = []
    for a in range(rows // WIN):
        pieces = [
            framed[(a * per_band + b) * TOK : (a * per_band + b + 1) * TOK].reshape(WIN, WIN, -1)
            for b in range(per_band)
        ]
        bands.append(jnp.concatenate(pieces, axis=1))
    return jnp.concatenate(bands, axis=0) if len(bands) > 1 else bands[0]


def lane_tiles(channels, size):
    tiles = []
    for start in range(0, channels, LANES):
        width = min(LANES, channels - start)
        tiles.append((start, width, start // size * TOK, (start + width) // size * TOK))
    return tiles


def spread(part, size):
    lane = iota((1, part.shape[1]), 1)
    copies = [
        part * ones_where((lane >= first) & (lane < first + size))
        for first in range(0, part.shape[1], size)
    ]
    return jnp.concatenate(copies, axis=0)


def paired(stacks, sides, size):
    both = []
    for n, part in enumerate(stacks):
        zeros = jnp.zeros(part.shape, part.dtype)
        both.append(jnp.concatenate([part, zeros] if n == 0 else [zeros, part], axis=0))
    wide = nn(sides, jnp.concatenate(both, axis=1))
    left = iota((size, LANES), 1) < TOK
    half = stacks[0].shape[1]
    rows = []
    for h in range(sides.shape[0] // size):
        at = h // 2 * LANES
        own = slice(h * size, (h + 1) * size)
        first = wide[own, at : at + LANES]
        second = wide[own, half + at : half + at + LANES]
        if h % 2 == 0:
            rows.append(jnp.where(left, first, pltpu.roll(second, TOK, 1)))
        else:
            rows.append(jnp.where(left, pltpu.roll(first, TOK, 1), second))
    return jnp.concatenate(rows, axis=0)


def pair_up(stacks, sides, size):
    channels = sides.shape[0]
    return jnp.concatenate(
        [
            paired([stack[:, first:last] for stack in stacks], sides[start : start + width], size)
            for start, width, first, last in lane_tiles(channels, size)
        ],
        axis=0,
    )


def attend(query, key, bias, same, size):
    scale = size ** (-0.5)
    parts = []
    for start, width, first, last in lane_tiles(query.shape[1], size):
        scores = nt(key[:, start : start + width], spread(query[:, start : start + width], size))
        for at in range(first, last, LANES):
            part = scores[:, at - first : at - first + LANES] * scale + bias[:, at : at + LANES]
            part = jnp.where(same, part, MASKED)
            exponent = jnp.exp(part - jnp.max(part, axis=0, keepdims=True))
            parts.append(exponent * (1.0 / jnp.sum(exponent, axis=0, keepdims=True)))
    return jnp.concatenate(parts, axis=1)


def attend_all(query, key, value_t, bias, masks, size, probs_ref):
    mixes = []
    for w in range(0, len(masks), 2):
        lows = []
        for v in (w, w + 1):
            at = slice(v * TOK, (v + 1) * TOK)
            probs = attend(query[at], key[at], bias, masks[v], size)
            probs_ref[v] = probs
            lows.append(probs.astype(BF16))
        mixes.append(pair_up(lows, value_t[:, w * TOK : (w + 2) * TOK], size).astype(BF16))
    return jnp.concatenate(mixes, axis=1)


def attend_back(query, value, probs, grad_mix, size):
    scale = size ** (-0.5)
    keys, values = [], []
    terms = []
    for start, width, first, last in lane_tiles(query.shape[1], size):
        part = slice(start, start + width)
        grad_heads = spread(grad_mix[:, part], size)
        chance = probs[:, first:last]
        grad_probs = nt(value[:, part], grad_heads)
        term = chance * (grad_probs - jnp.sum(grad_probs * chance, axis=0, keepdims=True))
        keys.append(nn(term.astype(BF16), spread(query[:, part], size)) * scale)
        values.append(nn(chance.astype(BF16), grad_heads))
        terms.append(term)
    return (
        jnp.concatenate(keys, axis=1).astype(BF16),
        jnp.concatenate(values, axis=1).astype(BF16),
        jnp.concatenate(terms, axis=1),
    )


def attend_all_back(query, key_t, value, probs_ref, grad_mixes, size, weigh):
    scale = size ** (-0.5)
    queries, keys, values = [], [], []
    bias_sum = None
    for w in range(0, len(grad_mixes), 2):
        lows = []
        for v in (w, w + 1):
            at = slice(v * TOK, (v + 1) * TOK)
            key, val, term = attend_back(query[at], value[at], probs_ref[v], grad_mixes[v], size)
            keys.append(key)
            values.append(val)
            lows.append(term.astype(BF16))
            term = weigh(v, term)
            bias_sum = term if bias_sum is None else bias_sum + term
        part = pair_up(lows, key_t[:, w * TOK : (w + 2) * TOK], size)
        queries.append((part * scale).astype(BF16))
    return (
        jnp.concatenate(queries, axis=1),
        jnp.concatenate(keys, axis=0),
        jnp.concatenate(values, axis=0),
        bias_sum,
    )


def same_region(ids):
    rows, cols = ids.shape
    masks = []
    row = iota((TOK, cols), 0)
    col = iota((TOK, cols), 1)
    lift = ones_where(iota((TOK, WIN), 0) // WIN == iota((TOK, WIN), 1))
    ones = jnp.ones((cols, LANES), BF16)
    for a in range(0, rows, WIN):
        band = ids[a : a + WIN].astype(BF16)
        lifted = nn(lift, band)
        for b in range(0, cols, WIN):
            picked = jnp.where(col == b + (row & (WIN - 1)), lifted, 0.0).astype(BF16)
            down = nn(picked, ones)
            tiled = nn(
                band,
                ones_where(iota((cols, LANES), 0) == b + (iota((cols, LANES), 1) & (WIN - 1))),
            )
            own = iota((WIN, LANES), 0) == ((iota((WIN, LANES), 1) // WIN) & (WIN - 1))
            across = jnp.sum(jnp.where(own, tiled, 0.0), axis=0, keepdims=True)
            masks.append(down == across)
    return masks


def split(values, count):
    parts = []
    for _ in range(count):
        low = values.astype(BF16)
        parts.append(low)
        values = values - low.astype(F32)
    return parts


def offset_rows(length):
    place = iota((length, 2 * LANES), 0)
    row = (place * 4370) >> 16
    return ones_where(iota((length, 2 * LANES), 1) == 2 * WIN * row + place - SPAN * row)


def offset_places():
    lane = iota((2 * LANES, WIN * LANES), 1)
    row = ((lane >> 3) & (WIN - 1)) - (lane >> 7) + WIN - 1
    return ones_where(iota((2 * LANES, WIN * LANES), 0) == 2 * WIN * row + (lane & (WIN - 1)))


def expand_bias(table):
    heads, length = table.shape
    onehot = offset_rows(length)
    rows = sum(nn(part, onehot) for part in split(table, 3))
    base = jnp.concatenate(
        [jnp.broadcast_to(rows[h : h + 1], (WIN, 2 * LANES)) for h in range(heads)], axis=0
    )
    place = iota(base.shape, 0) & (WIN - 1)
    rolled = base
    for c in range(WIN - 1):
        rolled = jnp.where(place == c, pltpu.roll(base, c + 2 * LANES - WIN + 1, 1), rolled)
    places = offset_places()
    spreaded = sum(nn(part, places) for part in split(rolled, 3))
    left = iota((WIN, LANES), 1) < TOK
    columns = []
    for h in range(0, heads, 2):
        pieces = [
            jnp.where(
                left,
                spreaded[h * WIN : (h + 1) * WIN, r * LANES : (r + 1) * LANES],
                spreaded[(h + 1) * WIN : (h + 2) * WIN, r * LANES : (r + 1) * LANES],
            )
            for r in range(WIN)
        ]
        columns.append(jnp.concatenate(pieces, axis=0))
    return jnp.concatenate(columns, axis=1)


def fold_bias(grad):
    heads = grad.shape[1] // TOK
    left = iota((WIN, LANES), 1) < TOK
    rows = []
    for h in range(heads):
        at = h // 2 * LANES
        pieces = []
        for r in range(WIN):
            piece = grad[r * WIN : (r + 1) * WIN, at : at + LANES]
            pieces.append(jnp.where(left, piece, 0.0) if h % 2 == 0 else jnp.where(left, 0.0, piece))
        rows.append(jnp.concatenate(pieces, axis=1))
    stacked = jnp.concatenate(rows, axis=0)
    places = offset_places()
    folded = sum(nt(part, places) for part in split(stacked, 3))
    place = iota(folded.shape, 0) & (WIN - 1)
    rolled = folded
    for c in range(WIN - 1):
        rolled = jnp.where(place == c, pltpu.roll(folded, WIN - 1 - c, 1), rolled)
    sums = [
        jnp.sum(rolled[h * WIN : (h + 1) * WIN], axis=0, keepdims=True) for h in range(heads)
    ]
    sums.append(jnp.zeros((WIN - heads, 2 * LANES), F32))
    return jnp.concatenate(sums, axis=0)


def table_rows(table, width):
    if width == LANES:
        return jnp.concatenate([table[:, :LANES], table[:, LANES:]], axis=0)
    return jnp.concatenate([table, jnp.zeros((WIN, width - 2 * LANES), F32)], axis=1)


def rows_table(rows):
    if rows.shape[1] == LANES:
        return jnp.concatenate([rows[:WIN], rows[WIN:]], axis=1)
    return rows[:WIN, : 2 * LANES]


def sort_by(blocks, place, ways):
    bit = 1
    while bit < ways:
        low = (place & bit) == 0
        blocks = [
            jnp.where(low, blocks[i], blocks[i ^ bit]) for i in range(len(blocks))
        ]
        bit *= 2
    return [blocks[i::ways] for i in range(ways)]


def tree_sum(values):
    while len(values) > 1:
        values = [values[i] + values[i + 1] for i in range(0, len(values), 2)]
    return values[0]


def write_parts(parts, tails, refs):
    for ref, part in zip(refs, parts):
        ref[...] = jnp.concatenate(part + tails, axis=0).astype(BF16)


def table_tail(tables, width):
    rows = jnp.concatenate([table_rows(table, width) for table in tables], axis=0)
    pad = -rows.shape[0] % (2 * WIN)
    if pad:
        rows = jnp.concatenate([rows, jnp.zeros((pad, width), F32)], axis=0)
    return rows


def narrow_units(terms, count):
    units = []
    for c in range(count):
        parts = []
        for term in terms:
            size = term.shape[0] // count
            parts.append(term[c * size : (c + 1) * size])
        block = jnp.concatenate(parts, axis=0) if len(parts) > 1 else parts[0]
        half = block.shape[0] // 2
        units.append(jnp.concatenate([block[:half], block[half:]], axis=1))
    return units


def wide_units(outer, width, count):
    units = []
    size = outer.shape[0] // count
    for c in range(count):
        wide = outer[c * size : (c + 1) * size]
        units.append(
            jnp.concatenate([wide[:, a : a + width] for a in range(0, wide.shape[1], width)], axis=0)
        )
    return units


def joined(*units):
    return [jnp.concatenate(parts, axis=0) for parts in zip(*units)]


def row_pieces(block, wide, channels, hidden, count):
    thin = channels // count
    broad = hidden // count
    if wide:
        size = block.shape[0] * block.shape[1] // hidden
        full = jnp.concatenate(
            [block[a : a + size] for a in range(0, block.shape[0], size)], axis=1
        )
        return [
            jnp.concatenate(
                [full[:, r * broad + a : r * broad + a + 2 * thin] for a in range(0, broad, 2 * thin)],
                axis=0,
            )
            for r in range(count)
        ]
    return [
        jnp.concatenate(
            [
                block[:, r * thin : (r + 1) * thin],
                block[:, channels + r * thin : channels + (r + 1) * thin],
            ],
            axis=1,
        )
        for r in range(count)
    ]


def bias_kernel(table, first, second):
    first[...] = expand_bias(table[:, 0])
    second[...] = expand_bias(table[:, 1])


def first_kernel(
    tokens,
    ids,
    cotangent,
    qkv_w,
    proj_w,
    inner_w,
    outer_w,
    bias_ref,
    first_out,
    near,
    far,
    query_out,
    key_out,
    value_out,
    probs_out,
    mix_out,
    middle_out,
    pre_out,
    act_out,
    edge,
):
    rows, cols, channels = tokens.shape
    size = channels // (bias_ref.shape[1] // TOK)
    count = rows * cols
    surface = to_windows(tokens[...].astype(F32))
    normed = norm(surface)[0].astype(BF16)
    bias = bias_ref[...]
    masks = same_region(ids[...].astype(F32))
    query, key, value = (
        nn(normed, qkv_w[0, :, i * channels : (i + 1) * channels]).astype(BF16) for i in range(3)
    )
    query_out[...] = query
    key_out[...] = key
    value_out[...] = value
    mix_t = attend_all(query, key, value.T, bias, masks, size, probs_out)
    mix_out[...] = mix_t
    middle = (surface + tn(mix_t, proj_w[0])).astype(BF16)
    middle_out[...] = middle
    normed = norm(middle.astype(F32))[0].astype(BF16)
    outs = []
    for at in range(0, count, 2 * TOK):
        pre = nn(normed[at : at + 2 * TOK], inner_w[0])
        pre_out[at : at + 2 * TOK] = pre
        act = (0.5 * pre * (1.0 + lax.erf(pre * math.sqrt(0.5)))).astype(BF16)
        act_out[at : at + 2 * TOK] = act
        outs.append(nt(act, outer_w[0]))
    result = (middle.astype(F32) + jnp.concatenate(outs, axis=0)).astype(BF16).astype(F32)
    grid = from_windows(result, rows, cols)
    first_out[...] = grid.astype(BF16)
    grads = cotangent[...].astype(F32)
    marks = ids[...].astype(F32)
    even = (lax.axis_index("rows") & 1) == 0
    for ref, down in ((near, even), (far, jnp.logical_not(even))):
        edge[...] = jnp.zeros(edge.shape, F32)
        for i in range(HALF):
            low = rows - HALF + i
            here = slice(i * cols, (i + 1) * cols)
            edge[here, :channels] = jnp.where(down, grid[low], grid[i])
            edge[here, channels:] = jnp.where(down, grads[low], grads[i])
        edge[HALF * cols : HALF * cols + HALF, :cols] = jnp.where(
            down, marks[rows - HALF :], marks[:HALF]
        )
        ref[...] = edge[...].astype(BF16)


def edge_kernel(
    first_out,
    cotangent,
    ids,
    upper_rim,
    upper_ids,
    lower_rim,
    lower_ids,
    from_near,
    from_far,
    up,
    down,
    near,
    far,
    ext_ids,
    edge,
    marks,
):
    rows, cols, channels = first_out.shape
    index = lax.axis_index("rows")
    at_top = index == 0
    at_bottom = index == lax.axis_size("rows") - 1
    grid = first_out[...].astype(F32)
    grads = cotangent[...].astype(F32)
    marks[HALF : HALF + rows, :] = ids[...].astype(F32)
    bands = []
    even = (index & 1) == 0
    got_near = from_near[...].astype(F32)
    got_far = from_far[...].astype(F32)
    for at_end, rim, rim_ids, got, target, place in (
        (at_top, upper_rim, upper_ids, jnp.where(even, got_far, got_near), up, 0),
        (at_bottom, lower_rim, lower_ids, jnp.where(even, got_near, got_far), down, HALF + rows),
    ):
        wide = HALF * cols
        tokens = jnp.where(at_end, rim[...].astype(F32).reshape(wide, channels), got[:wide, :channels])
        rest = jnp.where(at_end, 0.0, got[:wide, channels:])
        band = jnp.concatenate([tokens, rest], axis=1)
        target[...] = band.astype(BF16)
        marks[place : place + HALF, :] = jnp.where(
            at_end, rim_ids[...].astype(F32), got[wide : wide + HALF, :cols]
        )
        bands.append(band)
    ext_ids[...] = marks[...]
    total = rows + 2 * HALF
    even = (lax.axis_index("cols") & 1) == 0
    last = cols - HALF
    for ref, right in ((near, even), (far, jnp.logical_not(even))):
        edge[...] = jnp.zeros(edge.shape, F32)
        for i in range(total):
            here = slice(i * HALF, (i + 1) * HALF)
            if HALF <= i < HALF + rows:
                for values, part in ((grid, slice(0, channels)), (grads, slice(channels, None))):
                    row = values[i - HALF]
                    edge[here, part] = jnp.where(right, row[last:], row[:HALF])
            else:
                band, row = (bands[0], i) if i < HALF else (bands[1], i - HALF - rows)
                row = band[row * cols : (row + 1) * cols]
                edge[here, :] = jnp.where(right, row[last:], row[:HALF])
        edge[total * HALF : total * HALF + total, :cols] = marks[...]
        ref[...] = edge[...].astype(BF16)


def side_kernel(pre, key, slope, key_t):
    key_t[...] = key[...].T
    for at in range(0, pre.shape[0], TOK):
        x = pre[at : at + TOK]
        slope[at : at + TOK] = 0.5 * (1.0 + lax.erf(x * math.sqrt(0.5))) + x * (
            jnp.exp(-0.5 * x * x) * (1.0 / math.sqrt(2.0 * math.pi))
        )


def own_windows(rows, cols, channels, low, high):
    per_band = (cols + 2 * HALF) // WIN
    masks = []
    for a in range((rows + 2 * HALF) // WIN):
        for b in range(per_band):
            token = iota((TOK, channels), 0)
            row = a * WIN + (token >> 3)
            col = b * WIN + (token & (WIN - 1))
            masks.append((row >= low) & (row < high) & (col >= HALF) & (col < HALF + cols))
    return jnp.concatenate([ones_where(mask) for mask in masks], axis=0)


def second_kernel(
    first_out,
    cotangent,
    up,
    down,
    near,
    far,
    ext_ids,
    bias_ref,
    qkv_w,
    proj_w,
    inner_w,
    outer_w,
    grad_out,
    keep,
    send,
    xs,
    cs,
    probs_s,
):
    rows, cols, channels = first_out.shape
    total, wide = rows + 2 * HALF, cols + 2 * HALF
    width = bias_ref.shape[1]
    size = channels // (width // TOK)
    even = (lax.axis_index("cols") & 1) == 0
    got_near = near[...].astype(F32)
    got_far = far[...].astype(F32)
    left = jnp.where(even, got_far, got_near)
    right = jnp.where(even, got_near, got_far)
    for ref, source, at in ((xs, first_out, 0), (cs, cotangent, channels)):
        part = slice(at, at + channels)
        ref[HALF : HALF + rows, HALF : HALF + cols, :] = source[...].astype(F32)
        for edge, place in ((up, 0), (down, HALF + rows)):
            band = edge[...].astype(F32)[:, part]
            for i in range(HALF):
                ref[place + i, HALF : HALF + cols, :] = band[i * cols : (i + 1) * cols]
        for edge, place in ((left, 0), (right, HALF + cols)):
            band = edge[:, part]
            for i in range(total):
                ref[i, place : place + HALF, :] = band[i * HALF : (i + 1) * HALF]
    tail = slice(total * HALF, total * HALF + total)
    source_col = iota((cols, wide), 0)
    target_col = iota((cols, wide), 1)
    marks = sum(
        nn(values.astype(BF16), ones_where(target_col == source_col + shift))
        for values, shift in (
            (left[tail, :cols], HALF - cols),
            (ext_ids[...], HALF),
            (right[tail, :cols], HALF + cols),
        )
    )
    masks = same_region(marks)
    bias = bias_ref[...]
    surface = to_windows(xs[...])
    grad = to_windows(cs[...]).astype(BF16)
    count = surface.shape[0]
    unit_one, inverse_one = norm(surface)
    normed_one = unit_one.astype(BF16)
    weights = [qkv_w[1, :, i * channels : (i + 1) * channels] for i in range(3)]
    query, key, value = (nn(normed_one, w).astype(BF16) for w in weights)
    key_t, value_t = (nt(w.T, normed_one).astype(BF16) for w in weights[1:])
    mix_t = attend_all(query, key, value_t, bias, masks, size, probs_s)
    middle = (surface + tn(mix_t, proj_w[1])).astype(BF16).astype(F32)
    unit_two, inverse_two = norm(middle)
    normed_two = unit_two.astype(BF16)
    acts, grad_pres, grad_norms = [], [], []
    for at in range(0, count, 2 * TOK):
        here = slice(at, at + 2 * TOK)
        pre = nn(normed_two[here], inner_w[1])
        cdf = 0.5 * (1.0 + lax.erf(pre * math.sqrt(0.5)))
        acts.append((pre * cdf).astype(BF16))
        slope = cdf + pre * (jnp.exp(-0.5 * pre * pre) * (1.0 / math.sqrt(2.0 * math.pi)))
        grad_pre = (slope * nn(grad[here], outer_w[1])).astype(BF16)
        grad_pres.append(grad_pre)
        grad_norms.append(nt(grad_pre, inner_w[1]))
    act = jnp.concatenate(acts, axis=0)
    grad_pre = jnp.concatenate(grad_pres, axis=0)
    grad_norm = jnp.concatenate(grad_norms, axis=0)
    grad_middle = (grad.astype(F32) + norm_back(unit_two, inverse_two, grad_norm)).astype(BF16)
    index = lax.axis_index("rows")
    last = lax.axis_size("rows") - 1
    per_band = wide // WIN
    raw = nt(grad_middle, proj_w[1])
    grad_mixes = []
    for w in range(count // TOK):
        row = w // per_band * WIN + (iota((TOK, channels), 0) >> 3)
        low = jnp.where(index == 0, HALF, 0)
        high = jnp.where(index == last, HALF + rows, total)
        part = jnp.where((row >= low) & (row < high), raw[w * TOK : (w + 1) * TOK], 0.0)
        grad_mixes.append(part.astype(BF16))

    def weigh(w, term):
        lane = iota((1, width), 1)
        row = w // per_band * WIN + ((lane >> 3) & (WIN - 1))
        col = w % per_band * WIN + (lane & (WIN - 1))
        own = (row >= HALF) & (row < HALF + rows) & (col >= HALF) & (col < HALF + cols)
        return term * jnp.where(own, 1.0, 0.0)

    grad_query, grad_key, grad_value, bias_sum = attend_all_back(
        query, key_t, value, probs_s, grad_mixes, size, weigh
    )
    grad_norm = (
        nt(grad_query.T, weights[0]) + nt(grad_key, weights[1]) + nt(grad_value, weights[2])
    )
    grad_surface = grad_middle.astype(F32) + norm_back(unit_one, inverse_one, grad_norm)
    xs[...] = from_windows(grad_surface, total, wide)
    grad_out[...] = to_windows(xs[HALF : HALF + rows, HALF : HALF + cols, :]).astype(BF16)
    own = own_windows(rows, cols, channels, HALF, HALF + rows)
    low = jnp.where(index == 0, 0, HALF)
    high = jnp.where(index == last, total, HALF + rows)
    normed_one = normed_one * own_windows(rows, cols, channels, low, high)
    count = lax.axis_size("cols")
    qkv = [nn(grad_query, normed_one), tn(grad_key, normed_one), tn(grad_value, normed_one)]
    blocks = joined(
        narrow_units(
            [jnp.concatenate(qkv, axis=0), nn(mix_t, grad_middle * own).T], count
        ),
        narrow_units([tn(grad_pre, normed_two * own)], count),
        wide_units(tn(grad * own, act), 2 * channels, count),
    )
    tails = [table_tail([fold_bias(bias_sum)], 2 * channels)]
    write_parts(sort_by(blocks, lax.axis_index("cols") & 1, 2), tails, (keep, send))


def third_kernel(
    grad_ref, middle_ref, act, slope, inner_w, outer_w, grad_out, keep, send
):
    count = grad_ref.shape[0]
    grad = grad_ref[...]
    unit, inverse = norm(middle_ref[...].astype(F32))
    grad_pres, grad_norms = [], []
    for at in range(0, count, 2 * TOK):
        here = slice(at, at + 2 * TOK)
        grad_pre = (slope[here] * nn(grad[here], outer_w[0])).astype(BF16)
        grad_pres.append(grad_pre)
        grad_norms.append(nt(grad_pre, inner_w[0]))
    grad_pre = jnp.concatenate(grad_pres, axis=0)
    grad_norm = jnp.concatenate(grad_norms, axis=0)
    grad_out[...] = (grad.astype(F32) + norm_back(unit, inverse, grad_norm)).astype(BF16)
    number = lax.axis_size("cols")
    blocks = joined(
        narrow_units([tn(grad_pre, unit.astype(BF16))], number),
        wide_units(tn(grad, act[...]), 2 * grad.shape[1], number),
    )
    write_parts(sort_by(blocks, lax.axis_index("cols") & 1, 2), [], (keep, send))


def fourth_kernel(
    tokens,
    grad_ref,
    query,
    key_t,
    value,
    probs_ref,
    mix_t,
    qkv_w,
    proj_w,
    token_grad,
    keep,
    send,
):
    rows, cols, channels = tokens.shape
    width = probs_ref.shape[2]
    size = channels // (width // TOK)
    count = rows * cols
    unit_one, inverse_one = norm(to_windows(tokens[...].astype(F32)))
    normed_one = unit_one.astype(BF16)
    grad_middle = grad_ref[...]
    grad_mix = nt(grad_middle, proj_w[0]).astype(BF16)
    grad_mixes = [grad_mix[at : at + TOK] for at in range(0, count, TOK)]
    grad_query, grad_key, grad_value, bias_sum = attend_all_back(
        query, key_t, value, probs_ref, grad_mixes, size, lambda w, term: term
    )
    weights = [qkv_w[0, :, i * channels : (i + 1) * channels] for i in range(3)]
    grad_norm = (
        nt(grad_query.T, weights[0]) + nt(grad_key, weights[1]) + nt(grad_value, weights[2])
    )
    grad_surface = grad_middle.astype(F32) + norm_back(unit_one, inverse_one, grad_norm)
    token_grad[...] = from_windows(grad_surface, rows, cols).astype(BF16)
    number = lax.axis_size("cols")
    qkv = [nn(grad_query, normed_one), tn(grad_key, normed_one), tn(grad_value, normed_one)]
    blocks = narrow_units(
        [jnp.concatenate(qkv, axis=0), nn(mix_t[...], grad_middle).T], number
    )
    tails = [table_tail([fold_bias(bias_sum)], 2 * channels)]
    write_parts(sort_by(blocks, lax.axis_index("cols") & 1, 2), tails, (keep, send))


def summed(refs):
    values = [ref[...].astype(F32) for ref in refs]
    if len(values) == 4:
        values = [values[i] for i in ORDERED]
    return tree_sum(values)


def cut(values, count):
    rows = values.shape[0] // count
    return [values[i * rows : (i + 1) * rows] for i in range(count)]


def ordered(parts):
    return [parts[i] for i in ARRIVAL] if len(parts) == 4 else parts


def join_kernel(count, bit, ways, *refs):
    two, ffn, att = (summed(refs[i : i + 2]) for i in (0, 2, 4))
    tail = 2 * WIN
    blocks = joined(
        cut(att[: att.shape[0] - tail], count), cut(ffn, count), cut(two[: two.shape[0] - tail], count)
    )
    tables = [rows_table(part[part.shape[0] - tail :]) for part in (att, two)]
    place = (lax.axis_index("cols") >> bit) & (ways - 1)
    tails = [table_tail(tables, att.shape[1])]
    write_parts(ordered(sort_by(blocks, place, ways)), tails, refs[6:])


def step_kernel(axis, count, bit, before, ways, tail, *refs):
    both = summed(refs[:before])
    edge = both.shape[0] - tail
    place = (lax.axis_index(axis) >> bit) & (ways - 1)
    parts = sort_by(cut(both[:edge], count), place, ways)
    write_parts(ordered(parts), [both[edge:]], refs[before:])


def dense(block, used):
    if used * 4 != LANES * 3:
        pad = jnp.zeros((block.shape[0], LANES - used), F32)
        return jnp.concatenate([block, pad], axis=1)
    cut_at = block.shape[0] // 4
    side = jnp.concatenate(
        [block[3 * cut_at :, a : a + LANES // 4] for a in range(0, used, LANES // 4)], axis=0
    )
    return jnp.concatenate([block[: 3 * cut_at], side], axis=1)


def undense(block, used):
    if used * 4 != LANES * 3:
        return block
    cut_at = block.shape[0] // 3
    side = [block[i * cut_at : (i + 1) * cut_at, used:] for i in range(3)]
    return jnp.concatenate([block[:, :used], jnp.concatenate(side, axis=1)], axis=0)


def turn_kernel(channels, hidden, before, ways, *refs):
    both = summed(refs[:before])
    count = lax.axis_size("rows")
    edge = both.shape[0] - 2 * WIN
    used = 2 * channels // count
    pieces = [
        row_pieces(unit, n % 3 == 2, channels, hidden, count)
        for n, unit in enumerate(cut(both[:edge], 6))
    ]
    halves = [[dense(b, used) for b in joined(*pieces[n : n + 3])] for n in (0, 3)]
    parts = sort_by(joined(*halves), lax.axis_index("rows") & (ways - 1), ways)
    tables = [rows_table(both[edge + n * WIN : edge + (n + 1) * WIN]) for n in range(2)]
    write_parts(ordered(parts), [table_tail(tables, LANES)], refs[before:])


def last_kernel(sizes, scale, before, *refs):
    (qkv_cols, inner_cols, proj_cols), thin, broad = sizes
    qkv, proj, inner, outer, table = refs[before:]
    total = summed(refs[:before]) * scale
    edge = total.shape[0] - 4 * WIN
    heads = table.shape[0]
    onehot = offset_rows(table.shape[2])
    for b in range(2):
        both = undense(total[b * edge // 2 : (b + 1) * edge // 2], 2 * thin)
        low, mid, wide = cut(both, 3)
        low = jnp.concatenate([low[:, :thin], low[:, thin : 2 * thin]], axis=0)
        mid = jnp.concatenate([mid[:, :thin], mid[:, thin : 2 * thin]], axis=0)
        qkv[b] = low[:qkv_cols].T
        proj[b] = low[qkv_cols:]
        inner[b] = mid.T
        outer[b] = jnp.concatenate(
            [part[:, : 2 * thin] for part in cut(wide, broad // (2 * thin))], axis=1
        )
        sums = rows_table(total[edge + 2 * b * WIN : edge + 2 * (b + 1) * WIN])
        table[:, b] = sum(nt(part, onehot) for part in split(sums, 2))[:heads]


def call(kernel, outs, scratch, *operands, cost=0.2):
    return pl.pallas_call(
        kernel,
        out_shape=[jax.ShapeDtypeStruct(shape, kind) for shape, kind in outs],
        scratch_shapes=scratch,
        cost_estimate=pl.CostEstimate(
            flops=int(cost * 1e9), bytes_accessed=1024, transcendentals=0
        ),
        compiler_params=pltpu.CompilerParams(vmem_limit_bytes=VMEM_LIMIT),
    )(*operands)


def flip(values, axis, bit):
    count = lax.axis_size(axis)
    return lax.ppermute(values, axis, [(i, i ^ bit) for i in range(count)])


def swap(values, axis, offset, periodic):
    count = lax.axis_size(axis)
    pairs = []
    for i in range(offset, count, 2):
        j = (i + 1) % count
        if periodic or i + 1 < count:
            pairs += [(i, j), (j, i)]
    return lax.ppermute(values, axis, pairs)


def spread_parts(parts, axis, bit):
    ways = len(parts)
    order = ARRIVAL if ways == 4 else range(ways)
    return [flip(part, axis, j << bit) if j else part for j, part in zip(order, parts)]


def bit_groups(bits, size):
    return [min(size, bits - at) for at in range(0, bits, size)]


def reduce_terms(pairs, channels, hidden, units):
    got = []
    for keep, send in pairs:
        got += [keep, flip(send, "cols", 1)]
    count = lax.axis_size("cols") // 2
    tail = 2 * WIN
    bit = 1
    for size in bit_groups(count.bit_length() - 1, 2):
        ways = 1 << size
        shape = ((count // ways * units * 6 + tail, 2 * channels), BF16)
        if bit == 1:
            kernel = functools.partial(join_kernel, count, bit, ways)
        else:
            kernel = functools.partial(step_kernel, "cols", count, bit, len(got), ways, tail)
        got = spread_parts(call(kernel, [shape] * ways, [], *got), "cols", bit)
        bit += size
        count //= ways
    count = lax.axis_size("rows")
    thin = channels // count
    rows = units * 3 // 4 * 3 if 8 * thin == 3 * LANES else units * 3
    tail = 4 * WIN
    bit = 0
    for size in bit_groups(count.bit_length() - 1, 2):
        ways = 1 << size
        shape = ((count // ways * rows * 2 + tail, LANES), BF16)
        if bit == 0:
            kernel = functools.partial(turn_kernel, channels, hidden, len(got), ways)
        else:
            kernel = functools.partial(step_kernel, "rows", count, bit, len(got), ways, tail)
        got = spread_parts(call(kernel, [shape] * ways, [], *got), "rows", bit)
        bit += size
        count //= ways
    return got


def local(
    tokens,
    region_ids,
    upper_rim,
    upper_ids,
    lower_rim,
    lower_ids,
    cotangent,
    qkv_weight,
    proj_weight,
    inner_weight,
    outer_weight,
    bias_table,
):
    rows, cols, channels = tokens.shape
    hidden = inner_weight.shape[2]
    length, heads = bias_table.shape[1:]
    outer_weight = jnp.swapaxes(outer_weight, 1, 2)
    bias_table = jnp.transpose(bias_table, (2, 0, 1))
    col_count = lax.axis_size("cols")
    row_count = lax.axis_size("rows")
    count = rows * cols
    width = heads * TOK
    total = rows + 2 * HALF
    flat = ((count, channels), BF16)
    band = (HALF * cols + 2 * WIN, 2 * channels)
    pair = ((TOK, width), F32)
    bias_one, bias_two = call(bias_kernel, [pair, pair], [], bias_table, cost=6.0)
    first_out, near, far, query, key, value, probs, mix, middle, pre, act = call(
        first_kernel,
        [
            ((rows, cols, channels), BF16),
            (band, BF16),
            (band, BF16),
            flat,
            flat,
            flat,
            ((count // TOK, TOK, width), F32),
            ((channels, count), BF16),
            flat,
            ((count, hidden), F32),
            ((count, hidden), BF16),
        ],
        [pltpu.VMEM(band, F32)],
        tokens,
        region_ids,
        cotangent,
        qkv_weight,
        proj_weight,
        inner_weight,
        outer_weight,
        bias_one,
        cost=3.0,
    )
    from_near = swap(near, "rows", 0, False)
    from_far = swap(far, "rows", 1, False)
    slope, key_t = call(
        side_kernel, [((count, hidden), F32), ((channels, count), BF16)], [], pre, key, cost=1.0
    )
    strip = (total * HALF + total, 2 * channels)
    up, down, near, far, ext_ids = call(
        edge_kernel,
        [
            ((HALF * cols, 2 * channels), BF16),
            ((HALF * cols, 2 * channels), BF16),
            (strip, BF16),
            (strip, BF16),
            ((total, cols), F32),
        ],
        [pltpu.VMEM(strip, F32), pltpu.VMEM((total, cols), F32)],
        first_out,
        cotangent,
        region_ids,
        upper_rim,
        upper_ids,
        lower_rim,
        lower_ids,
        from_near,
        from_far,
    )
    near = swap(near, "cols", 0, True)
    far = swap(far, "cols", 1, True)
    units = 4 * channels // col_count // 2
    slots = col_count // 2

    def packed(number, tail):
        return ((slots * number * units + tail, 2 * channels), BF16)

    grid = (total, cols + 2 * HALF, channels)
    grad_first, keep_two, send_two = call(
        second_kernel,
        [flat, packed(3, 2 * WIN), packed(3, 2 * WIN)],
        [
            pltpu.VMEM(grid, F32),
            pltpu.VMEM(grid, F32),
            pltpu.VMEM((grid[0] * grid[1] // TOK, TOK, width), F32),
        ],
        first_out,
        cotangent,
        up,
        down,
        near,
        far,
        ext_ids,
        bias_two,
        qkv_weight,
        proj_weight,
        inner_weight,
        outer_weight,
        cost=12.0,
    )
    grad_middle, keep_ffn, send_ffn = call(
        third_kernel,
        [flat, packed(2, 0), packed(2, 0)],
        [],
        grad_first,
        middle,
        act,
        slope,
        inner_weight,
        outer_weight,
        cost=1.0,
    )
    token_grad, keep_one, send_one = call(
        fourth_kernel,
        [((rows, cols, channels), BF16), packed(1, 2 * WIN), packed(1, 2 * WIN)],
        [],
        tokens,
        grad_middle,
        query,
        key_t,
        value,
        probs,
        mix,
        qkv_weight,
        proj_weight,
        cost=4.0,
    )
    pairs = [(keep_two, send_two), (keep_ffn, send_ffn), (keep_one, send_one)]
    got = reduce_terms(pairs, channels, hidden, units)
    thin = channels // row_count
    broad = hidden // row_count
    sizes = (
        (3 * channels // col_count, hidden // col_count, channels // col_count),
        thin,
        broad,
    )
    qkv_grad, proj_grad, inner_grad, outer_grad, table_grad = call(
        functools.partial(last_kernel, sizes, 1.0 / (row_count * col_count), len(got)),
        [
            ((2, thin, sizes[0][0]), F32),
            ((2, sizes[0][2], thin), F32),
            ((2, thin, sizes[0][1]), F32),
            ((2, sizes[0][2], broad), F32),
            ((heads, 2, length), F32),
        ],
        [],
        *got,
    )
    proj_grad = jnp.swapaxes(proj_grad, 1, 2)
    outer_grad = jnp.swapaxes(outer_grad, 1, 2)
    table_grad = jnp.transpose(table_grad, (1, 2, 0))
    return token_grad, qkv_grad, proj_grad, inner_grad, outer_grad, table_grad


def solution(mesh):
    return jax.shard_map(
        local,
        mesh=mesh,
        in_specs=(
            P("rows", "cols", None),
            P("rows", "cols"),
            P(None, "cols", None),
            P(None, "cols"),
            P(None, "cols", None),
            P(None, "cols"),
            P("rows", "cols", None),
            P(),
            P(),
            P(),
            P(),
            P(),
        ),
        out_specs=(
            P("rows", "cols", None),
            P(None, "rows", "cols"),
            P(None, "rows", "cols"),
            P(None, "rows", "cols"),
            P(None, "rows", "cols"),
            P(),
        ),
        check_vma=False,
    )
```

```python
import functools
import math

import jax
import jax.numpy as jnp
from jax import lax
from jax.experimental import pallas as pl
from jax.experimental.pallas import tpu as pltpu
from jax.sharding import PartitionSpec as P

WIN = 8
HALF = 4
TOK = WIN * WIN
SPAN = 2 * WIN - 1
LANES = 128
EPS = 1e-05
MASKED = -1000000000.0
F32 = jnp.float32
BF16 = jnp.bfloat16
ARRIVAL = (0, 3, 2, 1)
ORDERED = (0, 3, 2, 1)
TURN_COST = 20.0
FILL = 1
VMEM_LIMIT = 40 * 1024 * 1024


def nn(left, right):
    return lax.dot_general(left, right, (((1,), (0,)), ((), ())), preferred_element_type=F32)


def nt(left, right):
    return lax.dot_general(left, right, (((1,), (1,)), ((), ())), preferred_element_type=F32)


def tn(left, right):
    return lax.dot_general(left, right, (((0,), (0,)), ((), ())), preferred_element_type=F32)


def iota(shape, dim):
    return lax.broadcasted_iota(jnp.int32, shape, dim)


def ones_where(condition):
    return jnp.where(condition, 1.0, 0.0).astype(BF16)


def norm(values):
    shifted = values - jnp.mean(values, axis=-1, keepdims=True)
    inverse = lax.rsqrt(jnp.mean(shifted * shifted, axis=-1, keepdims=True) + EPS)
    return shifted * inverse, inverse


def norm_back(unit, inverse, grad):
    mean_grad = jnp.mean(grad, axis=-1, keepdims=True)
    mean_unit = jnp.mean(grad * unit, axis=-1, keepdims=True)
    return inverse * (grad - mean_grad - unit * mean_unit)


def to_windows(grid):
    rows, cols, channels = grid.shape
    return jnp.concatenate(
        [
            grid[a : a + WIN, b : b + WIN].reshape(TOK, channels)
            for a in range(0, rows, WIN)
            for b in range(0, cols, WIN)
        ],
        axis=0,
    )


def from_windows(framed, rows, cols):
    per_band = cols // WIN
    bands = []
    for a in range(rows // WIN):
        pieces = [
            framed[(a * per_band + b) * TOK : (a * per_band + b + 1) * TOK].reshape(WIN, WIN, -1)
            for b in range(per_band)
        ]
        bands.append(jnp.concatenate(pieces, axis=1))
    return jnp.concatenate(bands, axis=0) if len(bands) > 1 else bands[0]


def lane_tiles(channels, size):
    tiles = []
    for start in range(0, channels, LANES):
        width = min(LANES, channels - start)
        tiles.append((start, width, start // size * TOK, (start + width) // size * TOK))
    return tiles


def spread(part, size):
    lane = iota((1, part.shape[1]), 1)
    copies = [
        part * ones_where((lane >= first) & (lane < first + size))
        for first in range(0, part.shape[1], size)
    ]
    return jnp.concatenate(copies, axis=0)


def paired(stacks, sides, size):
    both = []
    for n, part in enumerate(stacks):
        zeros = jnp.zeros(part.shape, part.dtype)
        both.append(jnp.concatenate([part, zeros] if n == 0 else [zeros, part], axis=0))
    wide = nn(sides, jnp.concatenate(both, axis=1))
    left = iota((size, LANES), 1) < TOK
    half = stacks[0].shape[1]
    rows = []
    for h in range(sides.shape[0] // size):
        at = h // 2 * LANES
        own = slice(h * size, (h + 1) * size)
        first = wide[own, at : at + LANES]
        second = wide[own, half + at : half + at + LANES]
        if h % 2 == 0:
            rows.append(jnp.where(left, first, pltpu.roll(second, TOK, 1)))
        else:
            rows.append(jnp.where(left, pltpu.roll(first, TOK, 1), second))
    return jnp.concatenate(rows, axis=0)


def pair_up(stacks, sides, size):
    channels = sides.shape[0]
    return jnp.concatenate(
        [
            paired([stack[:, first:last] for stack in stacks], sides[start : start + width], size)
            for start, width, first, last in lane_tiles(channels, size)
        ],
        axis=0,
    )


def attend(query, key, bias, same, size):
    scale = size ** (-0.5)
    parts = []
    for start, width, first, last in lane_tiles(query.shape[1], size):
        scores = nt(key[:, start : start + width], spread(query[:, start : start + width], size))
        for at in range(first, last, LANES):
            part = scores[:, at - first : at - first + LANES] * scale + bias[:, at : at + LANES]
            part = jnp.where(same, part, MASKED)
            exponent = jnp.exp(part - jnp.max(part, axis=0, keepdims=True))
            parts.append(exponent * (1.0 / jnp.sum(exponent, axis=0, keepdims=True)))
    return jnp.concatenate(parts, axis=1)


def attend_all(query, key, value_t, bias, masks, size, probs_ref):
    mixes = []
    for w in range(0, len(masks), 2):
        lows = []
        for v in (w, w + 1):
            at = slice(v * TOK, (v + 1) * TOK)
            probs = attend(query[at], key[at], bias, masks[v], size)
            probs_ref[v] = probs
            lows.append(probs.astype(BF16))
        mixes.append(pair_up(lows, value_t[:, w * TOK : (w + 2) * TOK], size).astype(BF16))
    return jnp.concatenate(mixes, axis=1)


def attend_back(query, value, probs, grad_mix, size):
    scale = size ** (-0.5)
    keys, values = [], []
    terms = []
    for start, width, first, last in lane_tiles(query.shape[1], size):
        part = slice(start, start + width)
        grad_heads = spread(grad_mix[:, part], size)
        chance = probs[:, first:last]
        grad_probs = nt(value[:, part], grad_heads)
        term = chance * (grad_probs - jnp.sum(grad_probs * chance, axis=0, keepdims=True))
        keys.append(nn(term.astype(BF16), spread(query[:, part], size)) * scale)
        values.append(nn(chance.astype(BF16), grad_heads))
        terms.append(term)
    return (
        jnp.concatenate(keys, axis=1).astype(BF16),
        jnp.concatenate(values, axis=1).astype(BF16),
        jnp.concatenate(terms, axis=1),
    )


def attend_all_back(query, key_t, value, probs_ref, grad_mixes, size, weigh):
    scale = size ** (-0.5)
    queries, keys, values = [], [], []
    bias_sum = None
    for w in range(0, len(grad_mixes), 2):
        lows = []
        for v in (w, w + 1):
            at = slice(v * TOK, (v + 1) * TOK)
            key, val, term = attend_back(query[at], value[at], probs_ref[v], grad_mixes[v], size)
            keys.append(key)
            values.append(val)
            lows.append(term.astype(BF16))
            term = weigh(v, term)
            bias_sum = term if bias_sum is None else bias_sum + term
        part = pair_up(lows, key_t[:, w * TOK : (w + 2) * TOK], size)
        queries.append((part * scale).astype(BF16))
    return (
        jnp.concatenate(queries, axis=1),
        jnp.concatenate(keys, axis=0),
        jnp.concatenate(values, axis=0),
        bias_sum,
    )


def same_region(ids):
    rows, cols = ids.shape
    masks = []
    row = iota((TOK, cols), 0)
    col = iota((TOK, cols), 1)
    lift = ones_where(iota((TOK, WIN), 0) // WIN == iota((TOK, WIN), 1))
    ones = jnp.ones((cols, LANES), BF16)
    for a in range(0, rows, WIN):
        band = ids[a : a + WIN].astype(BF16)
        lifted = nn(lift, band)
        for b in range(0, cols, WIN):
            picked = jnp.where(col == b + (row & (WIN - 1)), lifted, 0.0).astype(BF16)
            down = nn(picked, ones)
            tiled = nn(
                band,
                ones_where(iota((cols, LANES), 0) == b + (iota((cols, LANES), 1) & (WIN - 1))),
            )
            own = iota((WIN, LANES), 0) == ((iota((WIN, LANES), 1) // WIN) & (WIN - 1))
            across = jnp.sum(jnp.where(own, tiled, 0.0), axis=0, keepdims=True)
            masks.append(down == across)
    return masks


def split(values, count):
    parts = []
    for _ in range(count):
        low = values.astype(BF16)
        parts.append(low)
        values = values - low.astype(F32)
    return parts


def offset_rows(length):
    place = iota((length, 2 * LANES), 0)
    row = (place * 4370) >> 16
    return ones_where(iota((length, 2 * LANES), 1) == 2 * WIN * row + place - SPAN * row)


def offset_places():
    lane = iota((2 * LANES, LANES), 1)
    return ones_where(iota((2 * LANES, LANES), 0) == 2 * WIN * (lane >> 3) + (lane & (WIN - 1)))


def shifted(values, first, last):
    place = iota(values.shape, 0) & (WIN - 1)
    result = values
    for c in range(WIN):
        shift = (first + (last - first) // (WIN - 1) * c) % values.shape[1]
        if shift:
            result = jnp.where(place == c, pltpu.roll(values, shift, 1), result)
    return result


def expand_bias(table):
    heads, length = table.shape
    onehot = offset_rows(length)
    rows = sum(nn(part, onehot) for part in split(table, 3))
    base = jnp.concatenate(
        [jnp.broadcast_to(rows[h : h + 1], (WIN, 2 * LANES)) for h in range(heads)], axis=0
    )
    places = offset_places()
    spreaded = sum(nn(part, places) for part in split(shifted(base, 1 - WIN, 0), 3))
    left = iota((WIN, LANES), 1) < TOK
    columns = []
    for h in range(0, heads, 2):
        first = spreaded[h * WIN : (h + 1) * WIN]
        second = spreaded[(h + 1) * WIN : (h + 2) * WIN]
        pieces = []
        for r in range(WIN):
            back = LANES - WIN * (WIN - 1 - r)
            one = pltpu.roll(first, back % LANES, 1) if back % LANES else first
            two = pltpu.roll(second, (back + TOK) % LANES, 1)
            pieces.append(jnp.where(left, one, two))
        columns.append(jnp.concatenate(pieces, axis=0))
    return jnp.concatenate(columns, axis=1)


def fold_bias(grad):
    heads = grad.shape[1] // TOK
    left = iota((WIN, LANES), 1) < TOK
    rows = []
    for h in range(heads):
        at = h // 2 * LANES
        total = None
        for r in range(WIN):
            piece = grad[r * WIN : (r + 1) * WIN, at : at + LANES]
            piece = jnp.where(left, piece, 0.0) if h % 2 == 0 else jnp.where(left, 0.0, piece)
            shift = (WIN * (WIN - 1 - r) + h % 2 * TOK) % LANES
            piece = pltpu.roll(piece, shift, 1) if shift else piece
            total = piece if total is None else total + piece
        rows.append(total)
    places = offset_places()
    stacked = jnp.concatenate(rows, axis=0)
    folded = shifted(sum(nt(part, places) for part in split(stacked, 2)), WIN - 1, 0)
    sums = [
        jnp.sum(folded[h * WIN : (h + 1) * WIN], axis=0, keepdims=True) for h in range(heads)
    ]
    sums.append(jnp.zeros((WIN - heads, 2 * LANES), F32))
    return jnp.concatenate(sums, axis=0)


def wide_places():
    lane = iota((2 * LANES, WIN * LANES), 1)
    row = ((lane >> 3) & (WIN - 1)) - (lane >> 7) + WIN - 1
    return ones_where(iota((2 * LANES, WIN * LANES), 0) == 2 * WIN * row + (lane & (WIN - 1)))


def fold_wide(grad):
    heads = grad.shape[1] // TOK
    left = iota((WIN, LANES), 1) < TOK
    rows = []
    for h in range(heads):
        at = h // 2 * LANES
        pieces = []
        for r in range(WIN):
            piece = grad[r * WIN : (r + 1) * WIN, at : at + LANES]
            pieces.append(jnp.where(left, piece, 0.0) if h % 2 == 0 else jnp.where(left, 0.0, piece))
        rows.append(jnp.concatenate(pieces, axis=1))
    stacked = jnp.concatenate(rows, axis=0)
    places = wide_places()
    folded = sum(nt(part, places) for part in split(stacked, 2))
    place = iota(folded.shape, 0) & (WIN - 1)
    rolled = folded
    for c in range(WIN - 1):
        rolled = jnp.where(place == c, pltpu.roll(folded, WIN - 1 - c, 1), rolled)
    sums = [
        jnp.sum(rolled[h * WIN : (h + 1) * WIN], axis=0, keepdims=True) for h in range(heads)
    ]
    sums.append(jnp.zeros((WIN - heads, 2 * LANES), F32))
    return jnp.concatenate(sums, axis=0)


def table_rows(table, width):
    if width == LANES:
        return jnp.concatenate([table[:, :LANES], table[:, LANES:]], axis=0)
    return jnp.concatenate([table, jnp.zeros((WIN, width - 2 * LANES), F32)], axis=1)


def rows_table(rows):
    if rows.shape[1] == LANES:
        return jnp.concatenate([rows[:WIN], rows[WIN:]], axis=1)
    return rows[:WIN, : 2 * LANES]


def sort_by(blocks, place, ways):
    bit = 1
    while bit < ways:
        low = (place & bit) == 0
        blocks = [
            jnp.where(low, blocks[i], blocks[i ^ bit]) for i in range(len(blocks))
        ]
        bit *= 2
    return [blocks[i::ways] for i in range(ways)]


def tree_sum(values):
    while len(values) > 1:
        values = [values[i] + values[i + 1] for i in range(0, len(values), 2)]
    return values[0]


def write_parts(parts, tails, refs):
    for ref, part in zip(refs, parts):
        ref[...] = jnp.concatenate(part + tails, axis=0).astype(BF16)


def table_tail(tables, width):
    rows = jnp.concatenate([table_rows(table, width) for table in tables], axis=0)
    pad = -rows.shape[0] % (2 * WIN)
    if pad:
        rows = jnp.concatenate([rows, jnp.zeros((pad, width), F32)], axis=0)
    return rows


def narrow_units(terms, count):
    units = []
    for c in range(count):
        parts = []
        for term in terms:
            size = term.shape[0] // count
            parts.append(term[c * size : (c + 1) * size])
        block = jnp.concatenate(parts, axis=0) if len(parts) > 1 else parts[0]
        half = block.shape[0] // 2
        units.append(jnp.concatenate([block[:half], block[half:]], axis=1))
    return units


def wide_units(outer, width, count):
    units = []
    size = outer.shape[0] // count
    for c in range(count):
        wide = outer[c * size : (c + 1) * size]
        units.append(
            jnp.concatenate([wide[:, a : a + width] for a in range(0, wide.shape[1], width)], axis=0)
        )
    return units


def joined(*units):
    return [jnp.concatenate(parts, axis=0) for parts in zip(*units)]


def row_pieces(block, wide, channels, hidden, count):
    thin = channels // count
    broad = hidden // count
    if wide:
        size = block.shape[0] * block.shape[1] // hidden
        full = jnp.concatenate(
            [block[a : a + size] for a in range(0, block.shape[0], size)], axis=1
        )
        return [
            jnp.concatenate(
                [full[:, r * broad + a : r * broad + a + 2 * thin] for a in range(0, broad, 2 * thin)],
                axis=0,
            )
            for r in range(count)
        ]
    return [
        jnp.concatenate(
            [
                block[:, r * thin : (r + 1) * thin],
                block[:, channels + r * thin : channels + (r + 1) * thin],
            ],
            axis=1,
        )
        for r in range(count)
    ]


def bias_kernel(table, first, second):
    first[...] = expand_bias(table[:, 0])
    second[...] = expand_bias(table[:, 1])


def first_kernel(
    tokens,
    ids,
    cotangent,
    qkv_w,
    proj_w,
    inner_w,
    outer_w,
    bias_ref,
    first_out,
    near,
    far,
    query_out,
    key_out,
    value_out,
    probs_out,
    mix_out,
    middle_out,
    pre_out,
    act_out,
    edge,
):
    rows, cols, channels = tokens.shape
    size = channels // (bias_ref.shape[1] // TOK)
    count = rows * cols
    surface = to_windows(tokens[...].astype(F32))
    normed = norm(surface)[0].astype(BF16)
    bias = bias_ref[...]
    masks = same_region(ids[...].astype(F32))
    query, key, value = (
        nn(normed, qkv_w[0, :, i * channels : (i + 1) * channels]).astype(BF16) for i in range(3)
    )
    query_out[...] = query
    key_out[...] = key
    value_out[...] = value
    mix_t = attend_all(query, key, value.T, bias, masks, size, probs_out)
    mix_out[...] = mix_t
    middle = (surface + tn(mix_t, proj_w[0])).astype(BF16)
    middle_out[...] = middle
    normed = norm(middle.astype(F32))[0].astype(BF16)
    outs = []
    for at in range(0, count, 2 * TOK):
        pre = nn(normed[at : at + 2 * TOK], inner_w[0])
        pre_out[at : at + 2 * TOK] = pre
        act = (0.5 * pre * (1.0 + lax.erf(pre * math.sqrt(0.5)))).astype(BF16)
        act_out[at : at + 2 * TOK] = act
        outs.append(nt(act, outer_w[0]))
    result = (middle.astype(F32) + jnp.concatenate(outs, axis=0)).astype(BF16).astype(F32)
    grid = from_windows(result, rows, cols)
    first_out[...] = grid.astype(BF16)
    grads = cotangent[...].astype(F32)
    marks = ids[...].astype(F32)
    even = (lax.axis_index("rows") & 1) == 0
    for ref, down in ((near, even), (far, jnp.logical_not(even))):
        edge[...] = jnp.zeros(edge.shape, F32)
        for i in range(HALF):
            low = rows - HALF + i
            here = slice(i * cols, (i + 1) * cols)
            edge[here, :channels] = jnp.where(down, grid[low], grid[i])
            edge[here, channels:] = jnp.where(down, grads[low], grads[i])
        edge[HALF * cols : HALF * cols + HALF, :cols] = jnp.where(
            down, marks[rows - HALF :], marks[:HALF]
        )
        ref[...] = edge[...].astype(BF16)


def edge_kernel(
    first_out,
    cotangent,
    ids,
    upper_rim,
    upper_ids,
    lower_rim,
    lower_ids,
    from_near,
    from_far,
    up,
    down,
    near,
    far,
    ext_ids,
    edge,
    marks,
):
    rows, cols, channels = first_out.shape
    index = lax.axis_index("rows")
    at_top = index == 0
    at_bottom = index == lax.axis_size("rows") - 1
    grid = first_out[...].astype(F32)
    grads = cotangent[...].astype(F32)
    marks[HALF : HALF + rows, :] = ids[...].astype(F32)
    bands = []
    even = (index & 1) == 0
    got_near = from_near[...].astype(F32)
    got_far = from_far[...].astype(F32)
    for at_end, rim, rim_ids, got, target, place in (
        (at_top, upper_rim, upper_ids, jnp.where(even, got_far, got_near), up, 0),
        (at_bottom, lower_rim, lower_ids, jnp.where(even, got_near, got_far), down, HALF + rows),
    ):
        wide = HALF * cols
        tokens = jnp.where(at_end, rim[...].astype(F32).reshape(wide, channels), got[:wide, :channels])
        rest = jnp.where(at_end, 0.0, got[:wide, channels:])
        band = jnp.concatenate([tokens, rest], axis=1)
        target[...] = band.astype(BF16)
        marks[place : place + HALF, :] = jnp.where(
            at_end, rim_ids[...].astype(F32), got[wide : wide + HALF, :cols]
        )
        bands.append(band)
    ext_ids[...] = marks[...]
    total = rows + 2 * HALF
    even = (lax.axis_index("cols") & 1) == 0
    last = cols - HALF
    for ref, right in ((near, even), (far, jnp.logical_not(even))):
        edge[...] = jnp.zeros(edge.shape, F32)
        for i in range(total):
            here = slice(i * HALF, (i + 1) * HALF)
            if HALF <= i < HALF + rows:
                for values, part in ((grid, slice(0, channels)), (grads, slice(channels, None))):
                    row = values[i - HALF]
                    edge[here, part] = jnp.where(right, row[last:], row[:HALF])
            else:
                band, row = (bands[0], i) if i < HALF else (bands[1], i - HALF - rows)
                row = band[row * cols : (row + 1) * cols]
                edge[here, :] = jnp.where(right, row[last:], row[:HALF])
        edge[total * HALF : total * HALF + total, :cols] = marks[...]
        ref[...] = edge[...].astype(BF16)


def side_kernel(pre, key, slope, key_t):
    key_t[...] = key[...].T
    for at in range(0, pre.shape[0], TOK):
        x = pre[at : at + TOK]
        slope[at : at + TOK] = 0.5 * (1.0 + lax.erf(x * math.sqrt(0.5))) + x * (
            jnp.exp(-0.5 * x * x) * (1.0 / math.sqrt(2.0 * math.pi))
        )


def own_windows(rows, cols, channels, low, high):
    per_band = (cols + 2 * HALF) // WIN
    masks = []
    for a in range((rows + 2 * HALF) // WIN):
        for b in range(per_band):
            token = iota((TOK, channels), 0)
            row = a * WIN + (token >> 3)
            col = b * WIN + (token & (WIN - 1))
            masks.append((row >= low) & (row < high) & (col >= HALF) & (col < HALF + cols))
    return jnp.concatenate([ones_where(mask) for mask in masks], axis=0)


def second_kernel(
    first_out,
    cotangent,
    up,
    down,
    near,
    far,
    ext_ids,
    bias_ref,
    qkv_w,
    proj_w,
    inner_w,
    outer_w,
    after,
    grad_out,
    keep,
    send,
    xs,
    cs,
    probs_s,
):
    rows, cols, channels = first_out.shape
    total, wide = rows + 2 * HALF, cols + 2 * HALF
    width = bias_ref.shape[1]
    size = channels // (width // TOK)
    even = (lax.axis_index("cols") & 1) == 0
    got_near = near[...].astype(F32)
    got_far = far[...].astype(F32)
    left = jnp.where(even, got_far, got_near)
    right = jnp.where(even, got_near, got_far)
    for ref, source, at in ((xs, first_out, 0), (cs, cotangent, channels)):
        part = slice(at, at + channels)
        ref[HALF : HALF + rows, HALF : HALF + cols, :] = source[...].astype(F32)
        for edge, place in ((up, 0), (down, HALF + rows)):
            band = edge[...].astype(F32)[:, part]
            for i in range(HALF):
                ref[place + i, HALF : HALF + cols, :] = band[i * cols : (i + 1) * cols]
        for edge, place in ((left, 0), (right, HALF + cols)):
            band = edge[:, part]
            for i in range(total):
                ref[i, place : place + HALF, :] = band[i * HALF : (i + 1) * HALF]
    tail = slice(total * HALF, total * HALF + total)
    source_col = iota((cols, wide), 0)
    target_col = iota((cols, wide), 1)
    marks = sum(
        nn(values.astype(BF16), ones_where(target_col == source_col + shift))
        for values, shift in (
            (left[tail, :cols], HALF - cols),
            (ext_ids[...], HALF),
            (right[tail, :cols], HALF + cols),
        )
    )
    masks = same_region(marks)
    bias = bias_ref[...]
    surface = to_windows(xs[...])
    grad = to_windows(cs[...]).astype(BF16)
    count = surface.shape[0]
    unit_one, inverse_one = norm(surface)
    normed_one = unit_one.astype(BF16)
    weights = [qkv_w[1, :, i * channels : (i + 1) * channels] for i in range(3)]
    query, key, value = (nn(normed_one, w).astype(BF16) for w in weights)
    key_t, value_t = (nt(w.T, normed_one).astype(BF16) for w in weights[1:])
    mix_t = attend_all(query, key, value_t, bias, masks, size, probs_s)
    middle = (surface + tn(mix_t, proj_w[1])).astype(BF16).astype(F32)
    unit_two, inverse_two = norm(middle)
    normed_two = unit_two.astype(BF16)
    acts, grad_pres, grad_norms = [], [], []
    for at in range(0, count, 2 * TOK):
        here = slice(at, at + 2 * TOK)
        pre = nn(normed_two[here], inner_w[1])
        cdf = 0.5 * (1.0 + lax.erf(pre * math.sqrt(0.5)))
        acts.append((pre * cdf).astype(BF16))
        slope = cdf + pre * (jnp.exp(-0.5 * pre * pre) * (1.0 / math.sqrt(2.0 * math.pi)))
        grad_pre = (slope * nn(grad[here], outer_w[1])).astype(BF16)
        grad_pres.append(grad_pre)
        grad_norms.append(nt(grad_pre, inner_w[1]))
    act = jnp.concatenate(acts, axis=0)
    grad_pre = jnp.concatenate(grad_pres, axis=0)
    grad_norm = jnp.concatenate(grad_norms, axis=0)
    grad_middle = (grad.astype(F32) + norm_back(unit_two, inverse_two, grad_norm)).astype(BF16)
    index = lax.axis_index("rows")
    last = lax.axis_size("rows") - 1
    per_band = wide // WIN
    raw = nt(grad_middle, proj_w[1])
    grad_mixes = []
    for w in range(count // TOK):
        row = w // per_band * WIN + (iota((TOK, channels), 0) >> 3)
        low = jnp.where(index == 0, HALF, 0)
        high = jnp.where(index == last, HALF + rows, total)
        part = jnp.where((row >= low) & (row < high), raw[w * TOK : (w + 1) * TOK], 0.0)
        grad_mixes.append(part.astype(BF16))

    def weigh(w, term):
        lane = iota((1, width), 1)
        row = w // per_band * WIN + ((lane >> 3) & (WIN - 1))
        col = w % per_band * WIN + (lane & (WIN - 1))
        own = (row >= HALF) & (row < HALF + rows) & (col >= HALF) & (col < HALF + cols)
        return term * jnp.where(own, 1.0, 0.0)

    grad_query, grad_key, grad_value, bias_sum = attend_all_back(
        query, key_t, value, probs_s, grad_mixes, size, weigh
    )
    grad_norm = (
        nt(grad_query.T, weights[0]) + nt(grad_key, weights[1]) + nt(grad_value, weights[2])
    )
    grad_surface = grad_middle.astype(F32) + norm_back(unit_one, inverse_one, grad_norm)
    xs[...] = from_windows(grad_surface, total, wide)
    grad_out[...] = to_windows(xs[HALF : HALF + rows, HALF : HALF + cols, :]).astype(BF16)
    own = own_windows(rows, cols, channels, HALF, HALF + rows)
    low = jnp.where(index == 0, 0, HALF)
    high = jnp.where(index == last, total, HALF + rows)
    normed_one = normed_one * own_windows(rows, cols, channels, low, high)
    count = lax.axis_size("cols")
    qkv = [nn(grad_query, normed_one), tn(grad_key, normed_one), tn(grad_value, normed_one)]
    blocks = joined(
        narrow_units(
            [jnp.concatenate(qkv, axis=0), nn(mix_t, grad_middle * own).T], count
        ),
        narrow_units([tn(grad_pre, normed_two * own)], count),
        wide_units(tn(grad * own, act), 2 * channels, count),
    )
    tails = [table_tail([fold_bias(bias_sum)], 2 * channels)]
    write_parts(sort_by(blocks, lax.axis_index("cols") & 1, 2), tails, (keep, send))


def third_kernel(
    grad_ref, middle_ref, act, slope, inner_w, outer_w, grad_out, keep, send
):
    count = grad_ref.shape[0]
    grad = grad_ref[...]
    unit, inverse = norm(middle_ref[...].astype(F32))
    grad_pres, grad_norms = [], []
    for at in range(0, count, 2 * TOK):
        here = slice(at, at + 2 * TOK)
        grad_pre = (slope[here] * nn(grad[here], outer_w[0])).astype(BF16)
        grad_pres.append(grad_pre)
        grad_norms.append(nt(grad_pre, inner_w[0]))
    grad_pre = jnp.concatenate(grad_pres, axis=0)
    grad_norm = jnp.concatenate(grad_norms, axis=0)
    grad_out[...] = (grad.astype(F32) + norm_back(unit, inverse, grad_norm)).astype(BF16)
    number = lax.axis_size("cols")
    blocks = joined(
        narrow_units([tn(grad_pre, unit.astype(BF16))], number),
        wide_units(tn(grad, act[...]), 2 * grad.shape[1], number),
    )
    write_parts(sort_by(blocks, lax.axis_index("cols") & 1, 2), [], (keep, send))


def fourth_kernel(
    tokens,
    grad_ref,
    query,
    key_t,
    value,
    probs_ref,
    mix_t,
    qkv_w,
    proj_w,
    after,
    token_grad,
    keep,
    send,
):
    rows, cols, channels = tokens.shape
    width = probs_ref.shape[2]
    size = channels // (width // TOK)
    count = rows * cols
    unit_one, inverse_one = norm(to_windows(tokens[...].astype(F32)))
    normed_one = unit_one.astype(BF16)
    grad_middle = grad_ref[...]
    grad_mix = nt(grad_middle, proj_w[0]).astype(BF16)
    grad_mixes = [grad_mix[at : at + TOK] for at in range(0, count, TOK)]
    grad_query, grad_key, grad_value, bias_sum = attend_all_back(
        query, key_t, value, probs_ref, grad_mixes, size, lambda w, term: term
    )
    weights = [qkv_w[0, :, i * channels : (i + 1) * channels] for i in range(3)]
    grad_norm = (
        nt(grad_query.T, weights[0]) + nt(grad_key, weights[1]) + nt(grad_value, weights[2])
    )
    grad_surface = grad_middle.astype(F32) + norm_back(unit_one, inverse_one, grad_norm)
    token_grad[...] = from_windows(grad_surface, rows, cols).astype(BF16)
    number = lax.axis_size("cols")
    qkv = [nn(grad_query, normed_one), tn(grad_key, normed_one), tn(grad_value, normed_one)]
    blocks = narrow_units(
        [jnp.concatenate(qkv, axis=0), nn(mix_t[...], grad_middle).T], number
    )
    tails = [table_tail([fold_wide(bias_sum)], 2 * channels)]
    write_parts(sort_by(blocks, lax.axis_index("cols") & 1, 2), tails, (keep, send))


def summed(refs):
    values = [ref[...].astype(F32) for ref in refs]
    if len(values) == 4:
        values = [values[i] for i in ORDERED]
    return tree_sum(values)


def cut(values, count):
    rows = values.shape[0] // count
    return [values[i * rows : (i + 1) * rows] for i in range(count)]


def ordered(parts):
    return [parts[i] for i in ARRIVAL] if len(parts) == 4 else parts


def join_kernel(count, bit, ways, tails, *refs):
    blocks = []
    table = None
    for n, tail in enumerate(tails):
        part = summed(refs[2 * n : 2 * n + 2])
        edge = part.shape[0] - tail
        blocks.append(cut(part[:edge], count))
        table = rows_table(part[edge:]) if tail else table
    place = (lax.axis_index("cols") >> bit) & (ways - 1)
    tail = [table_tail([table], part.shape[1])]
    parts = ordered(sort_by(joined(*blocks), place, ways))
    write_parts(parts, tail, refs[len(refs) - ways :])


def step_kernel(axis, count, bit, before, ways, tail, *refs):
    both = summed(refs[:before])
    edge = both.shape[0] - tail
    place = (lax.axis_index(axis) >> bit) & (ways - 1)
    parts = sort_by(cut(both[:edge], count), place, ways)
    write_parts(ordered(parts), [both[edge:]], refs[before:])


def padded(block):
    pad = jnp.zeros((block.shape[0], LANES - block.shape[1]), F32)
    return jnp.concatenate([block, pad], axis=1)


def dense(block, used):
    if used * 4 != LANES * 3:
        return padded(block)
    cut_at = block.shape[0] // 4
    side = jnp.concatenate(
        [block[3 * cut_at :, a : a + LANES // 4] for a in range(0, used, LANES // 4)], axis=0
    )
    return jnp.concatenate([block[: 3 * cut_at], side], axis=1)


def undense(block, used):
    if used * 4 != LANES * 3:
        return block
    cut_at = block.shape[0] // 3
    side = [block[i * cut_at : (i + 1) * cut_at, used:] for i in range(3)]
    return jnp.concatenate([block[:, :used], jnp.concatenate(side, axis=1)], axis=0)


def first_turn_kernel(channels, hidden, before, *refs):
    both = summed(refs[:before])
    two, ffn, table = refs[before:]
    count = lax.axis_size("rows")
    edge = both.shape[0] - 2 * WIN
    used = 2 * channels // count
    pieces = [
        row_pieces(unit, n in (1, 4), channels, hidden, count)
        for n, unit in enumerate(cut(both[:edge], 5))
    ]
    ffn[...] = padded(jnp.concatenate(joined(*pieces[:2]), axis=0))
    two[...] = jnp.concatenate([dense(b, used) for b in joined(*pieces[2:])], axis=0)
    table[...] = rows_table(both[edge:])


def merge_kernel(channels, hidden, before, ways, *refs):
    both = summed(refs[:before])
    two, ffn, table = refs[before : before + 3]
    count = lax.axis_size("rows")
    edge = both.shape[0] - 2 * WIN
    used = 2 * channels // count
    att = row_pieces(both[:edge], False, channels, hidden, count)
    one = [dense(b, used) for b in joined(att, cut(ffn[...][:, :used], count))]
    parts = sort_by(
        joined(one, cut(two[...], count)), lax.axis_index("rows") & (ways - 1), ways
    )
    tails = [table_tail([rows_table(both[edge:]), table[...]], LANES)]
    write_parts(ordered(parts), tails, refs[before + 3 :])


def last_kernel(sizes, scale, before, *refs):
    (qkv_cols, inner_cols, proj_cols), thin, broad = sizes
    qkv, proj, inner, outer, table = refs[before:]
    total = summed(refs[:before]) * scale
    edge = total.shape[0] - 4 * WIN
    heads = table.shape[0]
    onehot = offset_rows(table.shape[2])
    for b in range(2):
        both = undense(total[b * edge // 2 : (b + 1) * edge // 2], 2 * thin)
        low, mid, wide = cut(both, 3)
        low = jnp.concatenate([low[:, :thin], low[:, thin : 2 * thin]], axis=0)
        mid = jnp.concatenate([mid[:, :thin], mid[:, thin : 2 * thin]], axis=0)
        qkv[b] = low[:qkv_cols].T
        proj[b] = low[qkv_cols:]
        inner[b] = mid.T
        outer[b] = jnp.concatenate(
            [part[:, : 2 * thin] for part in cut(wide, broad // (2 * thin))], axis=1
        )
        sums = rows_table(total[edge + 2 * b * WIN : edge + 2 * (b + 1) * WIN])
        table[:, b] = sum(nt(part, onehot) for part in split(sums, 2))[:heads]


def call(kernel, outs, scratch, *operands, cost=0.2):
    return pl.pallas_call(
        kernel,
        out_shape=[jax.ShapeDtypeStruct(shape, kind) for shape, kind in outs],
        scratch_shapes=scratch,
        cost_estimate=pl.CostEstimate(
            flops=int(cost * 1e9), bytes_accessed=1024, transcendentals=0
        ),
        compiler_params=pltpu.CompilerParams(vmem_limit_bytes=VMEM_LIMIT),
    )(*operands)


def flip(values, axis, bit):
    count = lax.axis_size(axis)
    return lax.ppermute(values, axis, [(i, i ^ bit) for i in range(count)])


def swap_cols(values, offset):
    count = lax.axis_size("cols")
    pairs = []
    for i in range(offset, count, 2):
        j = (i + 1) % count
        pairs += [(i, j), (j, i)]
    return lax.ppermute(values, "cols", pairs)


def swap_rows(values, offset):
    count = lax.axis_size("rows")
    cols = lax.axis_size("cols")
    partner = {}
    for i in range(offset, count - 1, 2):
        partner[i], partner[i + 1] = i + 1, i
    pairs = []
    for r in range(count):
        for c in range(cols):
            target = (partner[r], c) if r in partner else (r, c ^ FILL)
            pairs.append((r * cols + c, target[0] * cols + target[1]))
    return lax.ppermute(values, ("rows", "cols"), pairs)


def spread_parts(parts, axis, bit):
    ways = len(parts)
    order = ARRIVAL if ways == 4 else range(ways)
    return [flip(part, axis, j << bit) if j else part for j, part in zip(order, parts)]


def bit_groups(bits, size):
    return [min(size, bits - at) for at in range(0, bits, size)]


def reduce_cols(pairs, tails, width, units, after=()):
    got = []
    for keep, send in pairs:
        got += [keep, flip(send, "cols", 1)]
    count = lax.axis_size("cols") // 2
    tail = 2 * WIN
    bit = 1
    kept = None
    for size in bit_groups(count.bit_length() - 1, 2):
        ways = 1 << size
        shape = ((count // ways * units + tail, width), BF16)
        if bit == 1:
            kernel = functools.partial(join_kernel, count, bit, ways, tails)
            got = got + list(after)
        else:
            kernel = functools.partial(step_kernel, "cols", count, bit, len(got), ways, tail)
        parts = call(kernel, [shape] * ways, [], *got)
        kept = parts[0] if kept is None else kept
        got = spread_parts(parts, "cols", bit)
        bit += size
        count //= ways
    return got, kept


def reduce_rows(got, others, channels, hidden, rows):
    count = lax.axis_size("rows")
    tail = 4 * WIN
    bit = 0
    for size in bit_groups(count.bit_length() - 1, 2):
        ways = 1 << size
        shape = ((count // ways * rows * 2 + tail, LANES), BF16)
        if bit == 0:
            kernel = functools.partial(merge_kernel, channels, hidden, len(got), ways)
            got = [*got, *others]
        else:
            kernel = functools.partial(step_kernel, "rows", count, bit, len(got), ways, tail)
        got = spread_parts(call(kernel, [shape] * ways, [], *got), "rows", bit)
        bit += size
        count //= ways
    return got


def local(
    tokens,
    region_ids,
    upper_rim,
    upper_ids,
    lower_rim,
    lower_ids,
    cotangent,
    qkv_weight,
    proj_weight,
    inner_weight,
    outer_weight,
    bias_table,
):
    rows, cols, channels = tokens.shape
    hidden = inner_weight.shape[2]
    length, heads = bias_table.shape[1:]
    outer_weight = jnp.swapaxes(outer_weight, 1, 2)
    bias_table = jnp.transpose(bias_table, (2, 0, 1))
    col_count = lax.axis_size("cols")
    row_count = lax.axis_size("rows")
    count = rows * cols
    width = heads * TOK
    total = rows + 2 * HALF
    flat = ((count, channels), BF16)
    band = (HALF * cols + 2 * WIN, 2 * channels)
    pair = ((TOK, width), F32)
    bias_one, bias_two = call(bias_kernel, [pair, pair], [], bias_table, cost=6.0)
    first_out, near, far, query, key, value, probs, mix, middle, pre, act = call(
        first_kernel,
        [
            ((rows, cols, channels), BF16),
            (band, BF16),
            (band, BF16),
            flat,
            flat,
            flat,
            ((count // TOK, TOK, width), F32),
            ((channels, count), BF16),
            flat,
            ((count, hidden), F32),
            ((count, hidden), BF16),
        ],
        [pltpu.VMEM(band, F32)],
        tokens,
        region_ids,
        cotangent,
        qkv_weight,
        proj_weight,
        inner_weight,
        outer_weight,
        bias_one,
        cost=3.0,
    )
    from_near = swap_rows(near, 0)
    from_far = swap_rows(far, 1)
    slope, key_t = call(
        side_kernel, [((count, hidden), F32), ((channels, count), BF16)], [], pre, key, cost=1.0
    )
    strip = (total * HALF + total, 2 * channels)
    up, down, near, far, ext_ids = call(
        edge_kernel,
        [
            ((HALF * cols, 2 * channels), BF16),
            ((HALF * cols, 2 * channels), BF16),
            (strip, BF16),
            (strip, BF16),
            ((total, cols), F32),
        ],
        [pltpu.VMEM(strip, F32), pltpu.VMEM((total, cols), F32)],
        first_out,
        cotangent,
        region_ids,
        upper_rim,
        upper_ids,
        lower_rim,
        lower_ids,
        from_near,
        from_far,
    )
    near = swap_cols(near, 0)
    far = swap_cols(far, 1)
    units = 4 * channels // col_count // 2
    slots = col_count // 2

    def packed(number, tail):
        return ((slots * number * units + tail, 2 * channels), BF16)

    grid = (total, cols + 2 * HALF, channels)
    grad_first, keep_two, send_two = call(
        second_kernel,
        [flat, packed(3, 2 * WIN), packed(3, 2 * WIN)],
        [
            pltpu.VMEM(grid, F32),
            pltpu.VMEM(grid, F32),
            pltpu.VMEM((grid[0] * grid[1] // TOK, TOK, width), F32),
        ],
        first_out,
        cotangent,
        up,
        down,
        near,
        far,
        ext_ids,
        bias_two,
        qkv_weight,
        proj_weight,
        inner_weight,
        outer_weight,
        key_t,
        cost=12.0,
    )
    grad_middle, keep_ffn, send_ffn = call(
        third_kernel,
        [flat, packed(2, 0), packed(2, 0)],
        [],
        grad_first,
        middle,
        act,
        slope,
        inner_weight,
        outer_weight,
        cost=1.0,
    )
    got, kept = reduce_cols(
        [(keep_ffn, send_ffn), (keep_two, send_two)], (0, 2 * WIN), 2 * channels, 5 * units
    )
    thin = channels // row_count
    piece = units * 3 // 4 * 3 if 8 * thin == 3 * LANES else units * 3
    others = call(
        functools.partial(first_turn_kernel, channels, hidden, len(got)),
        [
            ((row_count * piece, LANES), F32),
            ((row_count * 2 * units, LANES), F32),
            ((WIN, 2 * LANES), F32),
        ],
        [],
        *got,
        cost=TURN_COST,
    )
    token_grad, keep_one, send_one = call(
        fourth_kernel,
        [((rows, cols, channels), BF16), packed(1, 2 * WIN), packed(1, 2 * WIN)],
        [],
        tokens,
        grad_middle,
        query,
        key_t,
        value,
        probs,
        mix,
        qkv_weight,
        proj_weight,
        kept,
        cost=4.0,
    )
    got, _ = reduce_cols([(keep_one, send_one)], (2 * WIN,), 2 * channels, units)
    got = reduce_rows(got, others, channels, hidden, piece)
    broad = hidden // row_count
    sizes = (
        (3 * channels // col_count, hidden // col_count, channels // col_count),
        thin,
        broad,
    )
    qkv_grad, proj_grad, inner_grad, outer_grad, table_grad = call(
        functools.partial(last_kernel, sizes, 1.0 / (row_count * col_count), len(got)),
        [
            ((2, thin, sizes[0][0]), F32),
            ((2, sizes[0][2], thin), F32),
            ((2, thin, sizes[0][1]), F32),
            ((2, sizes[0][2], broad), F32),
            ((heads, 2, length), F32),
        ],
        [],
        *got,
    )
    proj_grad = jnp.swapaxes(proj_grad, 1, 2)
    outer_grad = jnp.swapaxes(outer_grad, 1, 2)
    table_grad = jnp.transpose(table_grad, (1, 2, 0))
    return token_grad, qkv_grad, proj_grad, inner_grad, outer_grad, table_grad


def solution(mesh):
    return jax.shard_map(
        local,
        mesh=mesh,
        in_specs=(
            P("rows", "cols", None),
            P("rows", "cols"),
            P(None, "cols", None),
            P(None, "cols"),
            P(None, "cols", None),
            P(None, "cols"),
            P("rows", "cols", None),
            P(),
            P(),
            P(),
            P(),
            P(),
        ),
        out_specs=(
            P("rows", "cols", None),
            P(None, "rows", "cols"),
            P(None, "rows", "cols"),
            P(None, "rows", "cols"),
            P(None, "rows", "cols"),
            P(),
        ),
        check_vma=False,
    )
```

```python
import functools
import math

import jax
import jax.numpy as jnp
from jax import lax
from jax.experimental import pallas as pl
from jax.experimental.pallas import tpu as pltpu
from jax.sharding import PartitionSpec as P

WIN = 8
HALF = 4
TOK = WIN * WIN
SPAN = 2 * WIN - 1
LANES = 128
EPS = 1e-05
MASKED = -1000000000.0
F32 = jnp.float32
BF16 = jnp.bfloat16
ARRIVAL = (0, 3, 2, 1)
ORDERED = (0, 3, 2, 1)
TURN_COST = 20.0
FILL = 1
VMEM_LIMIT = 40 * 1024 * 1024


def nn(left, right):
    return lax.dot_general(left, right, (((1,), (0,)), ((), ())), preferred_element_type=F32)


def nt(left, right):
    return lax.dot_general(left, right, (((1,), (1,)), ((), ())), preferred_element_type=F32)


def tn(left, right):
    return lax.dot_general(left, right, (((0,), (0,)), ((), ())), preferred_element_type=F32)


def iota(shape, dim):
    return lax.broadcasted_iota(jnp.int32, shape, dim)


def ones_where(condition):
    return jnp.where(condition, 1.0, 0.0).astype(BF16)


def norm(values):
    shifted = values - jnp.mean(values, axis=-1, keepdims=True)
    inverse = lax.rsqrt(jnp.mean(shifted * shifted, axis=-1, keepdims=True) + EPS)
    return shifted * inverse, inverse


def norm_back(unit, inverse, grad):
    mean_grad = jnp.mean(grad, axis=-1, keepdims=True)
    mean_unit = jnp.mean(grad * unit, axis=-1, keepdims=True)
    return inverse * (grad - mean_grad - unit * mean_unit)


def to_windows(grid):
    rows, cols, channels = grid.shape
    return jnp.concatenate(
        [
            grid[a : a + WIN, b : b + WIN].reshape(TOK, channels)
            for a in range(0, rows, WIN)
            for b in range(0, cols, WIN)
        ],
        axis=0,
    )


def from_windows(framed, rows, cols):
    per_band = cols // WIN
    bands = []
    for a in range(rows // WIN):
        pieces = [
            framed[(a * per_band + b) * TOK : (a * per_band + b + 1) * TOK].reshape(WIN, WIN, -1)
            for b in range(per_band)
        ]
        bands.append(jnp.concatenate(pieces, axis=1))
    return jnp.concatenate(bands, axis=0) if len(bands) > 1 else bands[0]


def lane_tiles(channels, size):
    tiles = []
    for start in range(0, channels, LANES):
        width = min(LANES, channels - start)
        tiles.append((start, width, start // size * TOK, (start + width) // size * TOK))
    return tiles


def spread(part, size):
    lane = iota((1, part.shape[1]), 1)
    copies = [
        part * ones_where((lane >= first) & (lane < first + size))
        for first in range(0, part.shape[1], size)
    ]
    return jnp.concatenate(copies, axis=0)


def paired(stacks, sides, size):
    both = []
    for n, part in enumerate(stacks):
        zeros = jnp.zeros(part.shape, part.dtype)
        both.append(jnp.concatenate([part, zeros] if n == 0 else [zeros, part], axis=0))
    wide = nn(sides, jnp.concatenate(both, axis=1))
    left = iota((size, LANES), 1) < TOK
    half = stacks[0].shape[1]
    rows = []
    for h in range(sides.shape[0] // size):
        at = h // 2 * LANES
        own = slice(h * size, (h + 1) * size)
        first = wide[own, at : at + LANES]
        second = wide[own, half + at : half + at + LANES]
        if h % 2 == 0:
            rows.append(jnp.where(left, first, pltpu.roll(second, TOK, 1)))
        else:
            rows.append(jnp.where(left, pltpu.roll(first, TOK, 1), second))
    return jnp.concatenate(rows, axis=0)


def pair_up(stacks, sides, size):
    wide = stacks[0].shape[1]
    return jnp.concatenate(
        [
            paired(
                [stack[:, at : at + LANES] for stack in stacks],
                sides[at // TOK * size : (at + LANES) // TOK * size],
                size,
            )
            for at in range(0, wide, LANES)
        ],
        axis=0,
    )


def attend(query, key, bias, same, size):
    scale = size ** (-0.5)
    parts = []
    for start, width, first, last in lane_tiles(query.shape[1], size):
        scores = nt(key[:, start : start + width], spread(query[:, start : start + width], size))
        for at in range(first, last, LANES):
            part = scores[:, at - first : at - first + LANES] * scale + bias[:, at : at + LANES]
            part = jnp.where(same, part, MASKED)
            exponent = jnp.exp(part - jnp.max(part, axis=0, keepdims=True))
            parts.append(exponent * (1.0 / jnp.sum(exponent, axis=0, keepdims=True)))
    return jnp.concatenate(parts, axis=1)


def attend_all(query, key, value_t, bias, masks, size, probs_ref):
    mixes = []
    for w in range(0, len(masks), 2):
        lows = []
        for v in (w, w + 1):
            at = slice(v * TOK, (v + 1) * TOK)
            probs = attend(query[at], key[at], bias, masks[v], size)
            probs_ref[v] = probs
            lows.append(probs.astype(BF16))
        mixes.append(pair_up(lows, value_t[:, w * TOK : (w + 2) * TOK], size).astype(BF16))
    return jnp.concatenate(mixes, axis=1)


def attend_back(query, value, probs, grad_mix, size):
    scale = size ** (-0.5)
    keys, values = [], []
    terms = []
    for start, width, first, last in lane_tiles(query.shape[1], size):
        part = slice(start, start + width)
        grad_heads = spread(grad_mix[:, part], size)
        chance = probs[:, first:last]
        grad_probs = nt(value[:, part], grad_heads)
        term = chance * (grad_probs - jnp.sum(grad_probs * chance, axis=0, keepdims=True))
        keys.append(nn(term.astype(BF16), spread(query[:, part], size)) * scale)
        values.append(nn(chance.astype(BF16), grad_heads))
        terms.append(term)
    return (
        jnp.concatenate(keys, axis=1).astype(BF16),
        jnp.concatenate(values, axis=1).astype(BF16),
        jnp.concatenate(terms, axis=1),
    )


def attend_all_back(query, key_t, value, probs_ref, grad_mixes, size, weigh):
    scale = size ** (-0.5)
    queries, keys, values = [], [], []
    bias_sum = None
    for w in range(0, len(grad_mixes), 2):
        lows = []
        for v in (w, w + 1):
            at = slice(v * TOK, (v + 1) * TOK)
            key, val, term = attend_back(query[at], value[at], probs_ref[v], grad_mixes[v], size)
            keys.append(key)
            values.append(val)
            lows.append(term.astype(BF16))
            term = weigh(v, term)
            bias_sum = term if bias_sum is None else bias_sum + term
        part = pair_up(lows, key_t[:, w * TOK : (w + 2) * TOK], size)
        queries.append((part * scale).astype(BF16))
    return (
        jnp.concatenate(queries, axis=1),
        jnp.concatenate(keys, axis=0),
        jnp.concatenate(values, axis=0),
        bias_sum,
    )


def same_region(ids):
    rows, cols = ids.shape
    masks = []
    row = iota((TOK, cols), 0)
    col = iota((TOK, cols), 1)
    lift = ones_where(iota((TOK, WIN), 0) // WIN == iota((TOK, WIN), 1))
    ones = jnp.ones((cols, LANES), BF16)
    for a in range(0, rows, WIN):
        band = ids[a : a + WIN].astype(BF16)
        lifted = nn(lift, band)
        for b in range(0, cols, WIN):
            picked = jnp.where(col == b + (row & (WIN - 1)), lifted, 0.0).astype(BF16)
            down = nn(picked, ones)
            tiled = nn(
                band,
                ones_where(iota((cols, LANES), 0) == b + (iota((cols, LANES), 1) & (WIN - 1))),
            )
            own = iota((WIN, LANES), 0) == ((iota((WIN, LANES), 1) // WIN) & (WIN - 1))
            across = jnp.sum(jnp.where(own, tiled, 0.0), axis=0, keepdims=True)
            masks.append(down == across)
    return masks


def split(values, count):
    parts = []
    for _ in range(count):
        low = values.astype(BF16)
        parts.append(low)
        values = values - low.astype(F32)
    return parts


def offset_rows(length):
    place = iota((length, 2 * LANES), 0)
    row = (place * 4370) >> 16
    return ones_where(iota((length, 2 * LANES), 1) == 2 * WIN * row + place - SPAN * row)


def offset_places():
    lane = iota((2 * LANES, LANES), 1)
    return ones_where(iota((2 * LANES, LANES), 0) == 2 * WIN * (lane >> 3) + (lane & (WIN - 1)))


def shifted(values, first, last):
    place = iota(values.shape, 0) & (WIN - 1)
    result = values
    for c in range(WIN):
        shift = (first + (last - first) // (WIN - 1) * c) % values.shape[1]
        if shift:
            result = jnp.where(place == c, pltpu.roll(values, shift, 1), result)
    return result


def expand_bias(table):
    heads, length = table.shape
    onehot = offset_rows(length)
    rows = sum(nn(part, onehot) for part in split(table, 3))
    base = jnp.concatenate(
        [jnp.broadcast_to(rows[h : h + 1], (WIN, 2 * LANES)) for h in range(heads)], axis=0
    )
    places = offset_places()
    spreaded = sum(nn(part, places) for part in split(shifted(base, 1 - WIN, 0), 3))
    left = iota((WIN, LANES), 1) < TOK
    columns = []
    for h in range(0, heads, 2):
        first = spreaded[h * WIN : (h + 1) * WIN]
        second = spreaded[(h + 1) * WIN : (h + 2) * WIN]
        pieces = []
        for r in range(WIN):
            back = LANES - WIN * (WIN - 1 - r)
            one = pltpu.roll(first, back % LANES, 1) if back % LANES else first
            two = pltpu.roll(second, (back + TOK) % LANES, 1)
            pieces.append(jnp.where(left, one, two))
        columns.append(jnp.concatenate(pieces, axis=0))
    return jnp.concatenate(columns, axis=1)


def fold_bias(grad):
    heads = grad.shape[1] // TOK
    left = iota((WIN, LANES), 1) < TOK
    rows = []
    for h in range(heads):
        at = h // 2 * LANES
        total = None
        for r in range(WIN):
            piece = grad[r * WIN : (r + 1) * WIN, at : at + LANES]
            piece = jnp.where(left, piece, 0.0) if h % 2 == 0 else jnp.where(left, 0.0, piece)
            shift = (WIN * (WIN - 1 - r) + h % 2 * TOK) % LANES
            piece = pltpu.roll(piece, shift, 1) if shift else piece
            total = piece if total is None else total + piece
        rows.append(total)
    places = offset_places()
    stacked = jnp.concatenate(rows, axis=0)
    folded = shifted(sum(nt(part, places) for part in split(stacked, 2)), WIN - 1, 0)
    sums = [
        jnp.sum(folded[h * WIN : (h + 1) * WIN], axis=0, keepdims=True) for h in range(heads)
    ]
    sums.append(jnp.zeros((WIN - heads, 2 * LANES), F32))
    return jnp.concatenate(sums, axis=0)


def wide_places():
    lane = iota((2 * LANES, WIN * LANES), 1)
    row = ((lane >> 3) & (WIN - 1)) - (lane >> 7) + WIN - 1
    return ones_where(iota((2 * LANES, WIN * LANES), 0) == 2 * WIN * row + (lane & (WIN - 1)))


def fold_wide(grad):
    heads = grad.shape[1] // TOK
    left = iota((WIN, LANES), 1) < TOK
    rows = []
    for h in range(heads):
        at = h // 2 * LANES
        pieces = []
        for r in range(WIN):
            piece = grad[r * WIN : (r + 1) * WIN, at : at + LANES]
            pieces.append(jnp.where(left, piece, 0.0) if h % 2 == 0 else jnp.where(left, 0.0, piece))
        rows.append(jnp.concatenate(pieces, axis=1))
    stacked = jnp.concatenate(rows, axis=0)
    places = wide_places()
    folded = sum(nt(part, places) for part in split(stacked, 2))
    place = iota(folded.shape, 0) & (WIN - 1)
    rolled = folded
    for c in range(WIN - 1):
        rolled = jnp.where(place == c, pltpu.roll(folded, WIN - 1 - c, 1), rolled)
    sums = [
        jnp.sum(rolled[h * WIN : (h + 1) * WIN], axis=0, keepdims=True) for h in range(heads)
    ]
    sums.append(jnp.zeros((WIN - heads, 2 * LANES), F32))
    return jnp.concatenate(sums, axis=0)


def table_rows(table, width):
    if width == LANES:
        return jnp.concatenate([table[:, :LANES], table[:, LANES:]], axis=0)
    return jnp.concatenate([table, jnp.zeros((WIN, width - 2 * LANES), F32)], axis=1)


def rows_table(rows):
    if rows.shape[1] == LANES:
        return jnp.concatenate([rows[:WIN], rows[WIN:]], axis=1)
    return rows[:WIN, : 2 * LANES]


def sort_by(blocks, place, ways):
    bit = 1
    while bit < ways:
        low = (place & bit) == 0
        blocks = [
            jnp.where(low, blocks[i], blocks[i ^ bit]) for i in range(len(blocks))
        ]
        bit *= 2
    return [blocks[i::ways] for i in range(ways)]


def tree_sum(values):
    while len(values) > 1:
        values = [values[i] + values[i + 1] for i in range(0, len(values), 2)]
    return values[0]


def write_parts(parts, tails, refs):
    for ref, part in zip(refs, parts):
        ref[...] = jnp.concatenate(part + tails, axis=0).astype(BF16)


def table_tail(tables, width):
    rows = jnp.concatenate([table_rows(table, width) for table in tables], axis=0)
    pad = -rows.shape[0] % (2 * WIN)
    if pad:
        rows = jnp.concatenate([rows, jnp.zeros((pad, width), F32)], axis=0)
    return rows


def narrow_units(terms, count):
    units = []
    for c in range(count):
        parts = []
        for term in terms:
            size = term.shape[0] // count
            parts.append(term[c * size : (c + 1) * size])
        block = jnp.concatenate(parts, axis=0) if len(parts) > 1 else parts[0]
        half = block.shape[0] // 2
        units.append(jnp.concatenate([block[:half], block[half:]], axis=1))
    return units


def wide_units(outer, width, count):
    units = []
    size = outer.shape[0] // count
    for c in range(count):
        wide = outer[c * size : (c + 1) * size]
        units.append(
            jnp.concatenate([wide[:, a : a + width] for a in range(0, wide.shape[1], width)], axis=0)
        )
    return units


def joined(*units):
    return [jnp.concatenate(parts, axis=0) for parts in zip(*units)]


def row_pieces(block, wide, channels, hidden, count):
    thin = channels // count
    broad = hidden // count
    if wide:
        size = block.shape[0] * block.shape[1] // hidden
        full = jnp.concatenate(
            [block[a : a + size] for a in range(0, block.shape[0], size)], axis=1
        )
        return [
            jnp.concatenate(
                [full[:, r * broad + a : r * broad + a + 2 * thin] for a in range(0, broad, 2 * thin)],
                axis=0,
            )
            for r in range(count)
        ]
    return [
        jnp.concatenate(
            [
                block[:, r * thin : (r + 1) * thin],
                block[:, channels + r * thin : channels + (r + 1) * thin],
            ],
            axis=1,
        )
        for r in range(count)
    ]


def bias_kernel(table, first):
    first[...] = expand_bias(table[:, 0])


def first_kernel(
    tokens,
    ids,
    cotangent,
    qkv_w,
    proj_w,
    inner_w,
    outer_w,
    bias_ref,
    first_out,
    near,
    far,
    query_out,
    key_out,
    value_out,
    probs_out,
    mix_out,
    middle_out,
    pre_out,
    act_out,
    edge,
):
    rows, cols, channels = tokens.shape
    size = channels // (bias_ref.shape[1] // TOK)
    count = rows * cols
    surface = to_windows(tokens[...].astype(F32))
    normed = norm(surface)[0].astype(BF16)
    bias = bias_ref[...]
    masks = same_region(ids[...].astype(F32))
    query, key, value = (
        nn(normed, qkv_w[0, :, i * channels : (i + 1) * channels]).astype(BF16) for i in range(3)
    )
    query_out[...] = query
    key_out[...] = key
    value_out[...] = value
    mix_t = attend_all(query, key, value.T, bias, masks, size, probs_out)
    mix_out[...] = mix_t
    middle = (surface + tn(mix_t, proj_w[0])).astype(BF16)
    middle_out[...] = middle
    normed = norm(middle.astype(F32))[0].astype(BF16)
    outs = []
    for at in range(0, count, 2 * TOK):
        pre = nn(normed[at : at + 2 * TOK], inner_w[0])
        pre_out[at : at + 2 * TOK] = pre
        act = (0.5 * pre * (1.0 + lax.erf(pre * math.sqrt(0.5)))).astype(BF16)
        act_out[at : at + 2 * TOK] = act
        outs.append(nt(act, outer_w[0]))
    result = (middle.astype(F32) + jnp.concatenate(outs, axis=0)).astype(BF16).astype(F32)
    grid = from_windows(result, rows, cols)
    first_out[...] = grid.astype(BF16)
    grads = cotangent[...].astype(F32)
    marks = ids[...].astype(F32)
    even = (lax.axis_index("rows") & 1) == 0
    for ref, down in ((near, even), (far, jnp.logical_not(even))):
        edge[...] = jnp.zeros(edge.shape, F32)
        for i in range(HALF):
            low = rows - HALF + i
            here = slice(i * cols, (i + 1) * cols)
            edge[here, :channels] = jnp.where(down, grid[low], grid[i])
            edge[here, channels:] = jnp.where(down, grads[low], grads[i])
        edge[HALF * cols : HALF * cols + HALF, :cols] = jnp.where(
            down, marks[rows - HALF :], marks[:HALF]
        )
        ref[...] = edge[...].astype(BF16)


def edge_kernel(
    first_out,
    cotangent,
    ids,
    upper_rim,
    upper_ids,
    lower_rim,
    lower_ids,
    from_near,
    from_far,
    up,
    down,
    near,
    far,
    ext_ids,
    edge,
    marks,
):
    rows, cols, channels = first_out.shape
    index = lax.axis_index("rows")
    at_top = index == 0
    at_bottom = index == lax.axis_size("rows") - 1
    grid = first_out[...].astype(F32)
    grads = cotangent[...].astype(F32)
    marks[HALF : HALF + rows, :] = ids[...].astype(F32)
    bands = []
    even = (index & 1) == 0
    got_near = from_near[...].astype(F32)
    got_far = from_far[...].astype(F32)
    for at_end, rim, rim_ids, got, target, place in (
        (at_top, upper_rim, upper_ids, jnp.where(even, got_far, got_near), up, 0),
        (at_bottom, lower_rim, lower_ids, jnp.where(even, got_near, got_far), down, HALF + rows),
    ):
        wide = HALF * cols
        tokens = jnp.where(at_end, rim[...].astype(F32).reshape(wide, channels), got[:wide, :channels])
        rest = jnp.where(at_end, 0.0, got[:wide, channels:])
        band = jnp.concatenate([tokens, rest], axis=1)
        target[...] = band.astype(BF16)
        marks[place : place + HALF, :] = jnp.where(
            at_end, rim_ids[...].astype(F32), got[wide : wide + HALF, :cols]
        )
        bands.append(band)
    ext_ids[...] = marks[...]
    total = rows + 2 * HALF
    even = (lax.axis_index("cols") & 1) == 0
    last = cols - HALF
    for ref, right in ((near, even), (far, jnp.logical_not(even))):
        edge[...] = jnp.zeros(edge.shape, F32)
        for i in range(total):
            here = slice(i * HALF, (i + 1) * HALF)
            if HALF <= i < HALF + rows:
                for values, part in ((grid, slice(0, channels)), (grads, slice(channels, None))):
                    row = values[i - HALF]
                    edge[here, part] = jnp.where(right, row[last:], row[:HALF])
            else:
                band, row = (bands[0], i) if i < HALF else (bands[1], i - HALF - rows)
                row = band[row * cols : (row + 1) * cols]
                edge[here, :] = jnp.where(right, row[last:], row[:HALF])
        edge[total * HALF : total * HALF + total, :cols] = marks[...]
        ref[...] = edge[...].astype(BF16)


def side_kernel(pre, key, table, slope, key_t, bias, onehot):
    onehot[...] = offset_rows(onehot.shape[0])
    bias[...] = expand_bias(table[:, 1])
    key_t[...] = key[...].T
    for at in range(0, pre.shape[0], TOK):
        x = pre[at : at + TOK]
        slope[at : at + TOK] = 0.5 * (1.0 + lax.erf(x * math.sqrt(0.5))) + x * (
            jnp.exp(-0.5 * x * x) * (1.0 / math.sqrt(2.0 * math.pi))
        )


def own_windows(rows, cols, channels, low, high):
    per_band = (cols + 2 * HALF) // WIN
    masks = []
    for a in range((rows + 2 * HALF) // WIN):
        for b in range(per_band):
            token = iota((TOK, channels), 0)
            row = a * WIN + (token >> 3)
            col = b * WIN + (token & (WIN - 1))
            masks.append((row >= low) & (row < high) & (col >= HALF) & (col < HALF + cols))
    return jnp.concatenate([ones_where(mask) for mask in masks], axis=0)


def second_kernel(
    first_out,
    cotangent,
    up,
    down,
    far,
    near,
    ext_ids,
    bias_ref,
    qkv_w,
    proj_w,
    inner_w,
    outer_w,
    after,
    grad_out,
    table_out,
    keep,
    send,
    xs,
    cs,
    probs_s,
):
    rows, cols, channels = first_out.shape
    total, wide = rows + 2 * HALF, cols + 2 * HALF
    width = bias_ref.shape[1]
    size = channels // (width // TOK)
    even = (lax.axis_index("cols") & 1) == 0
    got_near = near[...].astype(F32)
    got_far = far[...].astype(F32)
    left = jnp.where(even, got_far, got_near)
    right = jnp.where(even, got_near, got_far)
    for ref, source, at in ((xs, first_out, 0), (cs, cotangent, channels)):
        part = slice(at, at + channels)
        ref[HALF : HALF + rows, HALF : HALF + cols, :] = source[...].astype(F32)
        for edge, place in ((up, 0), (down, HALF + rows)):
            band = edge[...].astype(F32)[:, part]
            for i in range(HALF):
                ref[place + i, HALF : HALF + cols, :] = band[i * cols : (i + 1) * cols]
        for edge, place in ((left, 0), (right, HALF + cols)):
            band = edge[:, part]
            for i in range(total):
                ref[i, place : place + HALF, :] = band[i * HALF : (i + 1) * HALF]
    tail = slice(total * HALF, total * HALF + total)
    source_col = iota((cols, wide), 0)
    target_col = iota((cols, wide), 1)
    marks = sum(
        nn(values.astype(BF16), ones_where(target_col == source_col + shift))
        for values, shift in (
            (left[tail, :cols], HALF - cols),
            (ext_ids[...], HALF),
            (right[tail, :cols], HALF + cols),
        )
    )
    masks = same_region(marks)
    bias = bias_ref[...]
    surface = to_windows(xs[...])
    grad = to_windows(cs[...]).astype(BF16)
    count = surface.shape[0]
    unit_one, inverse_one = norm(surface)
    normed_one = unit_one.astype(BF16)
    weights = [qkv_w[1, :, i * channels : (i + 1) * channels] for i in range(3)]
    query, key, value = (nn(normed_one, w).astype(BF16) for w in weights)
    key_t, value_t = (nt(w.T, normed_one).astype(BF16) for w in weights[1:])
    mix_t = attend_all(query, key, value_t, bias, masks, size, probs_s)
    middle = (surface + tn(mix_t, proj_w[1])).astype(BF16).astype(F32)
    unit_two, inverse_two = norm(middle)
    normed_two = unit_two.astype(BF16)
    acts, grad_pres, grad_norms = [], [], []
    for at in range(0, count, 2 * TOK):
        here = slice(at, at + 2 * TOK)
        pre = nn(normed_two[here], inner_w[1])
        cdf = 0.5 * (1.0 + lax.erf(pre * math.sqrt(0.5)))
        acts.append((pre * cdf).astype(BF16))
        slope = cdf + pre * (jnp.exp(-0.5 * pre * pre) * (1.0 / math.sqrt(2.0 * math.pi)))
        grad_pre = (slope * nn(grad[here], outer_w[1])).astype(BF16)
        grad_pres.append(grad_pre)
        grad_norms.append(nt(grad_pre, inner_w[1]))
    act = jnp.concatenate(acts, axis=0)
    grad_pre = jnp.concatenate(grad_pres, axis=0)
    grad_norm = jnp.concatenate(grad_norms, axis=0)
    grad_middle = (grad.astype(F32) + norm_back(unit_two, inverse_two, grad_norm)).astype(BF16)
    index = lax.axis_index("rows")
    last = lax.axis_size("rows") - 1
    per_band = wide // WIN
    raw = nt(grad_middle, proj_w[1])
    grad_mixes = []
    for w in range(count // TOK):
        row = w // per_band * WIN + (iota((TOK, channels), 0) >> 3)
        low = jnp.where(index == 0, HALF, 0)
        high = jnp.where(index == last, HALF + rows, total)
        part = jnp.where((row >= low) & (row < high), raw[w * TOK : (w + 1) * TOK], 0.0)
        grad_mixes.append(part.astype(BF16))

    def weigh(w, term):
        lane = iota((1, width), 1)
        row = w // per_band * WIN + ((lane >> 3) & (WIN - 1))
        col = w % per_band * WIN + (lane & (WIN - 1))
        own = (row >= HALF) & (row < HALF + rows) & (col >= HALF) & (col < HALF + cols)
        return term * jnp.where(own, 1.0, 0.0)

    grad_query, grad_key, grad_value, bias_sum = attend_all_back(
        query, key_t, value, probs_s, grad_mixes, size, weigh
    )
    grad_norm = (
        nt(grad_query.T, weights[0]) + nt(grad_key, weights[1]) + nt(grad_value, weights[2])
    )
    grad_surface = grad_middle.astype(F32) + norm_back(unit_one, inverse_one, grad_norm)
    xs[...] = from_windows(grad_surface, total, wide)
    grad_out[...] = to_windows(xs[HALF : HALF + rows, HALF : HALF + cols, :]).astype(BF16)
    own = own_windows(rows, cols, channels, HALF, HALF + rows)
    low = jnp.where(index == 0, 0, HALF)
    high = jnp.where(index == last, total, HALF + rows)
    normed_one = normed_one * own_windows(rows, cols, channels, low, high)
    count = lax.axis_size("cols")
    qkv = [nn(grad_query, normed_one), tn(grad_key, normed_one), tn(grad_value, normed_one)]
    blocks = joined(
        narrow_units(
            [jnp.concatenate(qkv, axis=0), nn(mix_t, grad_middle * own).T], count
        ),
        narrow_units([tn(normed_two * own, grad_pre).T], count),
        wide_units(tn(grad * own, act), 2 * channels, count),
    )
    table_out[...] = fold_bias(bias_sum)
    write_parts(sort_by(blocks, lax.axis_index("cols") & 1, 2), [], (keep, send))


def third_kernel(
    grad_ref, middle_ref, act, slope, inner_w, outer_w, grad_out, keep, send
):
    count = grad_ref.shape[0]
    grad = grad_ref[...]
    unit, inverse = norm(middle_ref[...].astype(F32))
    grad_pres, grad_norms = [], []
    for at in range(0, count, 2 * TOK):
        here = slice(at, at + 2 * TOK)
        grad_pre = (slope[here] * nn(grad[here], outer_w[0])).astype(BF16)
        grad_pres.append(grad_pre)
        grad_norms.append(nt(grad_pre, inner_w[0]))
    grad_pre = jnp.concatenate(grad_pres, axis=0)
    grad_norm = jnp.concatenate(grad_norms, axis=0)
    grad_out[...] = (grad.astype(F32) + norm_back(unit, inverse, grad_norm)).astype(BF16)
    number = lax.axis_size("cols")
    blocks = joined(
        narrow_units([tn(grad_pre, unit.astype(BF16))], number),
        wide_units(tn(grad, act[...]), 2 * grad.shape[1], number),
    )
    write_parts(sort_by(blocks, lax.axis_index("cols") & 1, 2), [], (keep, send))


def fourth_kernel(
    grad_ref, query, key_t, value, probs_ref, proj_w, query_out, key_out, value_out, bias_out
):
    count, channels = grad_ref.shape
    width = probs_ref.shape[2]
    grad_mix = nt(grad_ref[...], proj_w[0]).astype(BF16)
    grad_mixes = [grad_mix[at : at + TOK] for at in range(0, count, TOK)]
    query_out[...], key_out[...], value_out[...], bias_out[...] = attend_all_back(
        query,
        key_t,
        value,
        probs_ref,
        grad_mixes,
        channels // (width // TOK),
        lambda w, term: term,
    )


def fifth_kernel(
    tokens,
    grad_ref,
    mix_t,
    grad_query,
    grad_key,
    grad_value,
    bias_sum,
    table_two,
    qkv_w,
    after,
    token_grad,
    keep,
    send,
):
    rows, cols, channels = tokens.shape
    unit, inverse = norm(to_windows(tokens[...].astype(F32)))
    normed = unit.astype(BF16)
    grad_middle = grad_ref[...]
    grads = [grad_query[...].T, grad_key[...], grad_value[...]]
    number = lax.axis_size("cols")
    qkv = [nn(grad_query[...], normed), tn(grads[1], normed), tn(grads[2], normed)]
    blocks = narrow_units(
        [jnp.concatenate(qkv, axis=0), nn(mix_t[...], grad_middle).T], number
    )
    tails = [table_tail([fold_wide(bias_sum[...]), table_two[...]], 2 * channels)]
    write_parts(sort_by(blocks, lax.axis_index("cols") & 1, 2), tails, (keep, send))
    grad_norm = sum(
        nt(grad, qkv_w[0, :, i * channels : (i + 1) * channels]) for i, grad in enumerate(grads)
    )
    grad_surface = grad_middle.astype(F32) + norm_back(unit, inverse, grad_norm)
    token_grad[...] = from_windows(grad_surface, rows, cols).astype(BF16)


def summed(refs):
    values = [ref[...].astype(F32) for ref in refs]
    if len(values) == 4:
        values = [values[i] for i in ORDERED]
    return tree_sum(values)


def cut(values, count):
    rows = values.shape[0] // count
    return [values[i * rows : (i + 1) * rows] for i in range(count)]


def ordered(parts):
    return [parts[i] for i in ARRIVAL] if len(parts) == 4 else parts


def join_kernel(count, bit, ways, tail, *refs):
    sources = refs[: len(refs) - ways]
    blocks = []
    rest = []
    for n in range(0, len(sources), 2):
        part = summed(sources[n : n + 2])
        edge = part.shape[0] - tail
        blocks.append(cut(part[:edge], count))
        rest += [part[edge:]] if tail else []
    place = (lax.axis_index("cols") >> bit) & (ways - 1)
    parts = ordered(sort_by(joined(*blocks), place, ways))
    write_parts(parts, rest, refs[len(refs) - ways :])


def step_kernel(axis, count, bit, before, ways, tail, *refs):
    both = summed(refs[:before])
    edge = both.shape[0] - tail
    place = (lax.axis_index(axis) >> bit) & (ways - 1)
    parts = sort_by(cut(both[:edge], count), place, ways)
    write_parts(ordered(parts), [both[edge:]] if tail else [], refs[before:])


def padded(block):
    pad = jnp.zeros((block.shape[0], LANES - block.shape[1]), F32)
    return jnp.concatenate([block, pad], axis=1)


def dense(block, used):
    if used * 4 != LANES * 3:
        return padded(block)
    cut_at = block.shape[0] // 4
    side = jnp.concatenate(
        [block[3 * cut_at :, a : a + LANES // 4] for a in range(0, used, LANES // 4)], axis=0
    )
    return jnp.concatenate([block[: 3 * cut_at], side], axis=1)


def undense(block, used):
    if used * 4 != LANES * 3:
        return block
    cut_at = block.shape[0] // 3
    side = [block[i * cut_at : (i + 1) * cut_at, used:] for i in range(3)]
    return jnp.concatenate([block[:, :used], jnp.concatenate(side, axis=1)], axis=0)


def first_turn_kernel(channels, hidden, before, *refs):
    both = summed(refs[:before])
    two, ffn = refs[before:]
    count = lax.axis_size("rows")
    used = 2 * channels // count
    pieces = [
        row_pieces(unit, n in (1, 4), channels, hidden, count)
        for n, unit in enumerate(cut(both, 5))
    ]
    ffn[...] = padded(jnp.concatenate(joined(*pieces[:2]), axis=0))
    two[...] = jnp.concatenate([dense(b, used) for b in joined(*pieces[2:])], axis=0)


def merge_kernel(channels, hidden, before, ways, *refs):
    both = summed(refs[:before])
    two, ffn = refs[before : before + 2]
    count = lax.axis_size("rows")
    edge = both.shape[0] - 2 * WIN
    used = 2 * channels // count
    att = row_pieces(both[:edge], False, channels, hidden, count)
    one = [dense(b, used) for b in joined(att, cut(ffn[...][:, :used], count))]
    parts = sort_by(
        joined(one, cut(two[...], count)), lax.axis_index("rows") & (ways - 1), ways
    )
    tables = [rows_table(both[edge + n * WIN : edge + (n + 1) * WIN]) for n in range(2)]
    write_parts(ordered(parts), [table_tail(tables, LANES)], refs[before + 2 :])


def last_kernel(sizes, scale, before, onehot_ref, *refs):
    (qkv_cols, inner_cols, proj_cols), thin, broad = sizes
    qkv, proj, inner, outer, table = refs[before:]
    total = summed(refs[:before]) * scale
    edge = total.shape[0] - 4 * WIN
    heads = table.shape[0]
    onehot = onehot_ref[...]
    for b in range(2):
        both = undense(total[b * edge // 2 : (b + 1) * edge // 2], 2 * thin)
        low, mid, wide = cut(both, 3)
        low = jnp.concatenate([low[:, :thin], low[:, thin : 2 * thin]], axis=0)
        mid = jnp.concatenate([mid[:, :thin], mid[:, thin : 2 * thin]], axis=0)
        qkv[b] = low[:qkv_cols].T
        proj[b] = low[qkv_cols:]
        inner[b] = mid.T
        outer[b] = jnp.concatenate(
            [part[:, : 2 * thin] for part in cut(wide, broad // (2 * thin))], axis=1
        )
        sums = rows_table(total[edge + 2 * b * WIN : edge + 2 * (b + 1) * WIN])
        table[:, b] = sum(nt(part, onehot) for part in split(sums, 2))[:heads]


def call(kernel, outs, scratch, *operands, cost=0.2):
    return pl.pallas_call(
        kernel,
        out_shape=[jax.ShapeDtypeStruct(shape, kind) for shape, kind in outs],
        scratch_shapes=scratch,
        cost_estimate=pl.CostEstimate(
            flops=int(cost * 1e9), bytes_accessed=1024, transcendentals=0
        ),
        compiler_params=pltpu.CompilerParams(vmem_limit_bytes=VMEM_LIMIT),
    )(*operands)


def flip(values, axis, bit):
    count = lax.axis_size(axis)
    return lax.ppermute(values, axis, [(i, i ^ bit) for i in range(count)])


def swap_cols(values, offset):
    count = lax.axis_size("cols")
    pairs = []
    for i in range(offset, count, 2):
        j = (i + 1) % count
        pairs += [(i, j), (j, i)]
    return lax.ppermute(values, "cols", pairs)


def swap_rows(values, offset):
    count = lax.axis_size("rows")
    cols = lax.axis_size("cols")
    partner = {}
    for i in range(offset, count - 1, 2):
        partner[i], partner[i + 1] = i + 1, i
    pairs = []
    for r in range(count):
        for c in range(cols):
            target = (partner[r], c) if r in partner else (r, c ^ FILL)
            pairs.append((r * cols + c, target[0] * cols + target[1]))
    return lax.ppermute(values, ("rows", "cols"), pairs)


def spread_parts(parts, axis, bit):
    ways = len(parts)
    order = ARRIVAL if ways == 4 else range(ways)
    return [flip(part, axis, j << bit) if j else part for j, part in zip(order, parts)]


def bit_groups(bits, size):
    return [min(size, bits - at) for at in range(0, bits, size)]


def reduce_cols(pairs, tail, width, units):
    got = []
    for keep, send in pairs:
        got += [keep, flip(send, "cols", 1)]
    count = lax.axis_size("cols") // 2
    bit = 1
    kept = None
    for size in bit_groups(count.bit_length() - 1, 2):
        ways = 1 << size
        shape = ((count // ways * units + tail, width), BF16)
        if bit == 1:
            kernel = functools.partial(join_kernel, count, bit, ways, tail)
        else:
            kernel = functools.partial(step_kernel, "cols", count, bit, len(got), ways, tail)
        parts = call(kernel, [shape] * ways, [], *got)
        kept = parts[0] if kept is None else kept
        got = spread_parts(parts, "cols", bit)
        bit += size
        count //= ways
    return got, kept


def reduce_rows(got, others, channels, hidden, rows):
    count = lax.axis_size("rows")
    tail = 4 * WIN
    bit = 0
    for size in bit_groups(count.bit_length() - 1, 2):
        ways = 1 << size
        shape = ((count // ways * rows * 2 + tail, LANES), BF16)
        if bit == 0:
            kernel = functools.partial(merge_kernel, channels, hidden, len(got), ways)
            got = [*got, *others]
        else:
            kernel = functools.partial(step_kernel, "rows", count, bit, len(got), ways, tail)
        got = spread_parts(call(kernel, [shape] * ways, [], *got), "rows", bit)
        bit += size
        count //= ways
    return got


def local(
    tokens,
    region_ids,
    upper_rim,
    upper_ids,
    lower_rim,
    lower_ids,
    cotangent,
    qkv_weight,
    proj_weight,
    inner_weight,
    outer_weight,
    bias_table,
):
    rows, cols, channels = tokens.shape
    hidden = inner_weight.shape[2]
    length, heads = bias_table.shape[1:]
    outer_weight = jnp.swapaxes(outer_weight, 1, 2)
    bias_table = jnp.transpose(bias_table, (2, 0, 1))
    col_count = lax.axis_size("cols")
    row_count = lax.axis_size("rows")
    count = rows * cols
    width = heads * TOK
    total = rows + 2 * HALF
    flat = ((count, channels), BF16)
    band = (HALF * cols + 2 * WIN, 2 * channels)
    pair = ((TOK, width), F32)
    (bias_one,) = call(bias_kernel, [pair], [], bias_table, cost=6.0)
    first_out, near, far, query, key, value, probs, mix, middle, pre, act = call(
        first_kernel,
        [
            ((rows, cols, channels), BF16),
            (band, BF16),
            (band, BF16),
            flat,
            flat,
            flat,
            ((count // TOK, TOK, width), F32),
            ((channels, count), BF16),
            flat,
            ((count, hidden), F32),
            ((count, hidden), BF16),
        ],
        [pltpu.VMEM(band, F32)],
        tokens,
        region_ids,
        cotangent,
        qkv_weight,
        proj_weight,
        inner_weight,
        outer_weight,
        bias_one,
        cost=3.0,
    )
    from_near = swap_rows(near, 0)
    from_far = swap_rows(far, 1)
    slope, key_t, bias_two, onehot = call(
        side_kernel,
        [((count, hidden), F32), ((channels, count), BF16), pair, ((length, 2 * LANES), BF16)],
        [],
        pre,
        key,
        bias_table,
        cost=1.0,
    )
    strip = (total * HALF + total, 2 * channels)
    up, down, near, far, ext_ids = call(
        edge_kernel,
        [
            ((HALF * cols, 2 * channels), BF16),
            ((HALF * cols, 2 * channels), BF16),
            (strip, BF16),
            (strip, BF16),
            ((total, cols), F32),
        ],
        [pltpu.VMEM(strip, F32), pltpu.VMEM((total, cols), F32)],
        first_out,
        cotangent,
        region_ids,
        upper_rim,
        upper_ids,
        lower_rim,
        lower_ids,
        from_near,
        from_far,
    )
    far = swap_cols(far, 1)
    near = swap_cols(near, 0)
    units = 4 * channels // col_count // 2
    slots = col_count // 2

    def packed(number, tail):
        return ((slots * number * units + tail, 2 * channels), BF16)

    grid = (total, cols + 2 * HALF, channels)
    grad_first, table_two, keep_two, send_two = call(
        second_kernel,
        [flat, ((WIN, 2 * LANES), F32), packed(3, 0), packed(3, 0)],
        [
            pltpu.VMEM(grid, F32),
            pltpu.VMEM(grid, F32),
            pltpu.VMEM((grid[0] * grid[1] // TOK, TOK, width), F32),
        ],
        first_out,
        cotangent,
        up,
        down,
        far,
        near,
        ext_ids,
        bias_two,
        qkv_weight,
        proj_weight,
        inner_weight,
        outer_weight,
        key_t,
        cost=12.0,
    )
    grad_middle, keep_ffn, send_ffn = call(
        third_kernel,
        [flat, packed(2, 0), packed(2, 0)],
        [],
        grad_first,
        middle,
        act,
        slope,
        inner_weight,
        outer_weight,
        cost=1.0,
    )
    got, kept = reduce_cols(
        [(keep_ffn, send_ffn), (keep_two, send_two)], 0, 2 * channels, 5 * units
    )
    thin = channels // row_count
    piece = units * 3 // 4 * 3 if 8 * thin == 3 * LANES else units * 3
    others = call(
        functools.partial(first_turn_kernel, channels, hidden, len(got)),
        [
            ((row_count * piece, LANES), F32),
            ((row_count * 2 * units, LANES), F32),
        ],
        [],
        *got,
        cost=TURN_COST,
    )
    grad_query, grad_key, grad_value, bias_sum = call(
        fourth_kernel,
        [((channels, count), BF16), flat, flat, pair],
        [],
        grad_middle,
        query,
        key_t,
        value,
        probs,
        proj_weight,
        cost=2.0,
    )
    token_grad, keep_one, send_one = call(
        fifth_kernel,
        [((rows, cols, channels), BF16), packed(1, 2 * WIN), packed(1, 2 * WIN)],
        [],
        tokens,
        grad_middle,
        mix,
        grad_query,
        grad_key,
        grad_value,
        bias_sum,
        table_two,
        qkv_weight,
        kept,
        cost=4.0,
    )
    got, _ = reduce_cols([(keep_one, send_one)], 2 * WIN, 2 * channels, units)
    got = reduce_rows(got, others, channels, hidden, piece)
    broad = hidden // row_count
    sizes = (
        (3 * channels // col_count, hidden // col_count, channels // col_count),
        thin,
        broad,
    )
    qkv_grad, proj_grad, inner_grad, outer_grad, table_grad = call(
        functools.partial(last_kernel, sizes, 1.0 / (row_count * col_count), len(got)),
        [
            ((2, thin, sizes[0][0]), F32),
            ((2, sizes[0][2], thin), F32),
            ((2, thin, sizes[0][1]), F32),
            ((2, sizes[0][2], broad), F32),
            ((heads, 2, length), F32),
        ],
        [],
        onehot,
        *got,
    )
    proj_grad = jnp.swapaxes(proj_grad, 1, 2)
    outer_grad = jnp.swapaxes(outer_grad, 1, 2)
    table_grad = jnp.transpose(table_grad, (1, 2, 0))
    return token_grad, qkv_grad, proj_grad, inner_grad, outer_grad, table_grad


def solution(mesh):
    return jax.shard_map(
        local,
        mesh=mesh,
        in_specs=(
            P("rows", "cols", None),
            P("rows", "cols"),
            P(None, "cols", None),
            P(None, "cols"),
            P(None, "cols", None),
            P(None, "cols"),
            P("rows", "cols", None),
            P(),
            P(),
            P(),
            P(),
            P(),
        ),
        out_specs=(
            P("rows", "cols", None),
            P(None, "rows", "cols"),
            P(None, "rows", "cols"),
            P(None, "rows", "cols"),
            P(None, "rows", "cols"),
            P(),
        ),
        check_vma=False,
    )
```

```python
import functools
import math

import jax
import jax.numpy as jnp
from jax import lax
from jax.experimental import pallas as pl
from jax.experimental.pallas import tpu as pltpu
from jax.sharding import PartitionSpec as P

WIN = 8
HALF = 4
TOK = WIN * WIN
SPAN = 2 * WIN - 1
LANES = 128
EPS = 1e-05
MASKED = -1000000000.0
F32 = jnp.float32
BF16 = jnp.bfloat16
ARRIVAL = (0, 3, 2, 1)
ORDERED = (0, 3, 2, 1)
TURN_COST = 20.0
FILL = 1
VMEM_LIMIT = 40 * 1024 * 1024


def nn(left, right):
    return lax.dot_general(left, right, (((1,), (0,)), ((), ())), preferred_element_type=F32)


def nt(left, right):
    return lax.dot_general(left, right, (((1,), (1,)), ((), ())), preferred_element_type=F32)


def tn(left, right):
    return lax.dot_general(left, right, (((0,), (0,)), ((), ())), preferred_element_type=F32)


def iota(shape, dim):
    return lax.broadcasted_iota(jnp.int32, shape, dim)


def ones_where(condition):
    return jnp.where(condition, 1.0, 0.0).astype(BF16)


def norm(values):
    shifted = values - jnp.mean(values, axis=-1, keepdims=True)
    inverse = lax.rsqrt(jnp.mean(shifted * shifted, axis=-1, keepdims=True) + EPS)
    return shifted * inverse, inverse


def norm_back(unit, inverse, grad):
    mean_grad = jnp.mean(grad, axis=-1, keepdims=True)
    mean_unit = jnp.mean(grad * unit, axis=-1, keepdims=True)
    return inverse * (grad - mean_grad - unit * mean_unit)


def to_windows(grid):
    rows, cols, channels = grid.shape
    return jnp.concatenate(
        [
            grid[a : a + WIN, b : b + WIN].reshape(TOK, channels)
            for a in range(0, rows, WIN)
            for b in range(0, cols, WIN)
        ],
        axis=0,
    )


def from_windows(framed, rows, cols):
    per_band = cols // WIN
    bands = []
    for a in range(rows // WIN):
        pieces = [
            framed[(a * per_band + b) * TOK : (a * per_band + b + 1) * TOK].reshape(WIN, WIN, -1)
            for b in range(per_band)
        ]
        bands.append(jnp.concatenate(pieces, axis=1))
    return jnp.concatenate(bands, axis=0) if len(bands) > 1 else bands[0]


def lane_tiles(channels, size):
    tiles = []
    for start in range(0, channels, LANES):
        width = min(LANES, channels - start)
        tiles.append((start, width, start // size * TOK, (start + width) // size * TOK))
    return tiles


def spread(part, size):
    lane = iota((1, part.shape[1]), 1)
    copies = [
        part * ones_where((lane >= first) & (lane < first + size))
        for first in range(0, part.shape[1], size)
    ]
    return jnp.concatenate(copies, axis=0)


def paired(stacks, sides, size):
    both = []
    for n, part in enumerate(stacks):
        zeros = jnp.zeros(part.shape, part.dtype)
        both.append(jnp.concatenate([part, zeros] if n == 0 else [zeros, part], axis=0))
    wide = nn(sides, jnp.concatenate(both, axis=1))
    left = iota((size, LANES), 1) < TOK
    half = stacks[0].shape[1]
    rows = []
    for h in range(sides.shape[0] // size):
        at = h // 2 * LANES
        own = slice(h * size, (h + 1) * size)
        first = wide[own, at : at + LANES]
        second = wide[own, half + at : half + at + LANES]
        if h % 2 == 0:
            rows.append(jnp.where(left, first, pltpu.roll(second, TOK, 1)))
        else:
            rows.append(jnp.where(left, pltpu.roll(first, TOK, 1), second))
    return jnp.concatenate(rows, axis=0)


def pair_up(stacks, sides, size):
    wide = stacks[0].shape[1]
    return jnp.concatenate(
        [
            paired(
                [stack[:, at : at + LANES] for stack in stacks],
                sides[at // TOK * size : (at + LANES) // TOK * size],
                size,
            )
            for at in range(0, wide, LANES)
        ],
        axis=0,
    )


def attend(query, key, bias, same, size):
    scale = size ** (-0.5)
    parts = []
    for start, width, first, last in lane_tiles(query.shape[1], size):
        scores = nt(key[:, start : start + width], spread(query[:, start : start + width], size))
        for at in range(first, last, LANES):
            part = scores[:, at - first : at - first + LANES] * scale + bias[:, at : at + LANES]
            part = jnp.where(same, part, MASKED)
            exponent = jnp.exp(part - jnp.max(part, axis=0, keepdims=True))
            parts.append(exponent * (1.0 / jnp.sum(exponent, axis=0, keepdims=True)))
    return jnp.concatenate(parts, axis=1)


def attend_all(query, key, value_t, bias, masks, size, probs_ref):
    mixes = []
    for w in range(0, len(masks), 2):
        lows = []
        for v in (w, w + 1):
            at = slice(v * TOK, (v + 1) * TOK)
            probs = attend(query[at], key[at], bias, masks[v], size)
            probs_ref[v] = probs
            lows.append(probs.astype(BF16))
        mixes.append(pair_up(lows, value_t[:, w * TOK : (w + 2) * TOK], size).astype(BF16))
    return jnp.concatenate(mixes, axis=1)


def attend_back(query, value, probs, grad_mix, size):
    scale = size ** (-0.5)
    keys, values = [], []
    terms = []
    for start, width, first, last in lane_tiles(query.shape[1], size):
        part = slice(start, start + width)
        grad_heads = spread(grad_mix[:, part], size)
        chance = probs[:, first:last]
        grad_probs = nt(value[:, part], grad_heads)
        term = chance * (grad_probs - jnp.sum(grad_probs * chance, axis=0, keepdims=True))
        keys.append(nn(term.astype(BF16), spread(query[:, part], size)) * scale)
        values.append(nn(chance.astype(BF16), grad_heads))
        terms.append(term)
    return (
        jnp.concatenate(keys, axis=1).astype(BF16),
        jnp.concatenate(values, axis=1).astype(BF16),
        jnp.concatenate(terms, axis=1),
    )


def attend_all_back(query, key_t, value, probs_ref, grad_mixes, size, weigh):
    scale = size ** (-0.5)
    queries, keys, values = [], [], []
    bias_sum = None
    for w in range(0, len(grad_mixes), 2):
        lows = []
        for v in (w, w + 1):
            at = slice(v * TOK, (v + 1) * TOK)
            key, val, term = attend_back(query[at], value[at], probs_ref[v], grad_mixes[v], size)
            keys.append(key)
            values.append(val)
            lows.append(term.astype(BF16))
            term = weigh(v, term)
            bias_sum = term if bias_sum is None else bias_sum + term
        part = pair_up(lows, key_t[:, w * TOK : (w + 2) * TOK], size)
        queries.append((part * scale).astype(BF16))
    return (
        jnp.concatenate(queries, axis=1),
        jnp.concatenate(keys, axis=0),
        jnp.concatenate(values, axis=0),
        bias_sum,
    )


def same_region(ids):
    rows, cols = ids.shape
    masks = []
    row = iota((TOK, cols), 0)
    col = iota((TOK, cols), 1)
    lift = ones_where(iota((TOK, WIN), 0) // WIN == iota((TOK, WIN), 1))
    ones = jnp.ones((cols, LANES), BF16)
    for a in range(0, rows, WIN):
        band = ids[a : a + WIN].astype(BF16)
        lifted = nn(lift, band)
        for b in range(0, cols, WIN):
            picked = jnp.where(col == b + (row & (WIN - 1)), lifted, 0.0).astype(BF16)
            down = nn(picked, ones)
            tiled = nn(
                band,
                ones_where(iota((cols, LANES), 0) == b + (iota((cols, LANES), 1) & (WIN - 1))),
            )
            own = iota((WIN, LANES), 0) == ((iota((WIN, LANES), 1) // WIN) & (WIN - 1))
            across = jnp.sum(jnp.where(own, tiled, 0.0), axis=0, keepdims=True)
            masks.append(down == across)
    return masks


def split(values, count):
    parts = []
    for _ in range(count):
        low = values.astype(BF16)
        parts.append(low)
        values = values - low.astype(F32)
    return parts


def offset_rows(length):
    place = iota((length, 2 * LANES), 0)
    row = (place * 4370) >> 16
    return ones_where(iota((length, 2 * LANES), 1) == 2 * WIN * row + place - SPAN * row)


def offset_places():
    lane = iota((2 * LANES, LANES), 1)
    return ones_where(iota((2 * LANES, LANES), 0) == 2 * WIN * (lane >> 3) + (lane & (WIN - 1)))


def shifted(values, first, last):
    place = iota(values.shape, 0) & (WIN - 1)
    result = values
    for c in range(WIN):
        shift = (first + (last - first) // (WIN - 1) * c) % values.shape[1]
        if shift:
            result = jnp.where(place == c, pltpu.roll(values, shift, 1), result)
    return result


def expand_bias(table):
    heads, length = table.shape
    onehot = offset_rows(length)
    rows = sum(nn(part, onehot) for part in split(table, 3))
    base = jnp.concatenate(
        [jnp.broadcast_to(rows[h : h + 1], (WIN, 2 * LANES)) for h in range(heads)], axis=0
    )
    places = offset_places()
    spreaded = sum(nn(part, places) for part in split(shifted(base, 1 - WIN, 0), 3))
    left = iota((WIN, LANES), 1) < TOK
    columns = []
    for h in range(0, heads, 2):
        first = spreaded[h * WIN : (h + 1) * WIN]
        second = spreaded[(h + 1) * WIN : (h + 2) * WIN]
        pieces = []
        for r in range(WIN):
            back = LANES - WIN * (WIN - 1 - r)
            one = pltpu.roll(first, back % LANES, 1) if back % LANES else first
            two = pltpu.roll(second, (back + TOK) % LANES, 1)
            pieces.append(jnp.where(left, one, two))
        columns.append(jnp.concatenate(pieces, axis=0))
    return jnp.concatenate(columns, axis=1)


def fold_bias(grad):
    heads = grad.shape[1] // TOK
    left = iota((WIN, LANES), 1) < TOK
    rows = []
    for h in range(heads):
        at = h // 2 * LANES
        total = None
        for r in range(WIN):
            piece = grad[r * WIN : (r + 1) * WIN, at : at + LANES]
            piece = jnp.where(left, piece, 0.0) if h % 2 == 0 else jnp.where(left, 0.0, piece)
            shift = (WIN * (WIN - 1 - r) + h % 2 * TOK) % LANES
            piece = pltpu.roll(piece, shift, 1) if shift else piece
            total = piece if total is None else total + piece
        rows.append(total)
    places = offset_places()
    stacked = jnp.concatenate(rows, axis=0)
    folded = shifted(sum(nt(part, places) for part in split(stacked, 2)), WIN - 1, 0)
    sums = [
        jnp.sum(folded[h * WIN : (h + 1) * WIN], axis=0, keepdims=True) for h in range(heads)
    ]
    sums.append(jnp.zeros((WIN - heads, 2 * LANES), F32))
    return jnp.concatenate(sums, axis=0)


def wide_places():
    lane = iota((2 * LANES, WIN * LANES), 1)
    row = ((lane >> 3) & (WIN - 1)) - (lane >> 7) + WIN - 1
    return ones_where(iota((2 * LANES, WIN * LANES), 0) == 2 * WIN * row + (lane & (WIN - 1)))


def fold_wide(grad):
    heads = grad.shape[1] // TOK
    left = iota((WIN, LANES), 1) < TOK
    rows = []
    for h in range(heads):
        at = h // 2 * LANES
        pieces = []
        for r in range(WIN):
            piece = grad[r * WIN : (r + 1) * WIN, at : at + LANES]
            pieces.append(jnp.where(left, piece, 0.0) if h % 2 == 0 else jnp.where(left, 0.0, piece))
        rows.append(jnp.concatenate(pieces, axis=1))
    stacked = jnp.concatenate(rows, axis=0)
    places = wide_places()
    folded = sum(nt(part, places) for part in split(stacked, 2))
    place = iota(folded.shape, 0) & (WIN - 1)
    rolled = folded
    for c in range(WIN - 1):
        rolled = jnp.where(place == c, pltpu.roll(folded, WIN - 1 - c, 1), rolled)
    sums = [
        jnp.sum(rolled[h * WIN : (h + 1) * WIN], axis=0, keepdims=True) for h in range(heads)
    ]
    sums.append(jnp.zeros((WIN - heads, 2 * LANES), F32))
    return jnp.concatenate(sums, axis=0)


def table_rows(table, width):
    if width == LANES:
        return jnp.concatenate([table[:, :LANES], table[:, LANES:]], axis=0)
    return jnp.concatenate([table, jnp.zeros((WIN, width - 2 * LANES), F32)], axis=1)


def rows_table(rows):
    if rows.shape[1] == LANES:
        return jnp.concatenate([rows[:WIN], rows[WIN:]], axis=1)
    return rows[:WIN, : 2 * LANES]


def sort_by(blocks, place, ways):
    bit = 1
    while bit < ways:
        low = (place & bit) == 0
        blocks = [
            jnp.where(low, blocks[i], blocks[i ^ bit]) for i in range(len(blocks))
        ]
        bit *= 2
    return [blocks[i::ways] for i in range(ways)]


def tree_sum(values):
    while len(values) > 1:
        values = [values[i] + values[i + 1] for i in range(0, len(values), 2)]
    return values[0]


def write_parts(parts, tails, refs):
    for ref, part in zip(refs, parts):
        ref[...] = jnp.concatenate(part + tails, axis=0).astype(BF16)


def table_tail(tables, width):
    rows = jnp.concatenate([table_rows(table, width) for table in tables], axis=0)
    pad = -rows.shape[0] % (2 * WIN)
    if pad:
        rows = jnp.concatenate([rows, jnp.zeros((pad, width), F32)], axis=0)
    return rows


def narrow_units(terms, count):
    units = []
    for c in range(count):
        parts = []
        for term in terms:
            size = term.shape[0] // count
            parts.append(term[c * size : (c + 1) * size])
        block = jnp.concatenate(parts, axis=0) if len(parts) > 1 else parts[0]
        half = block.shape[0] // 2
        units.append(jnp.concatenate([block[:half], block[half:]], axis=1))
    return units


def wide_units(outer, width, count):
    units = []
    size = outer.shape[0] // count
    for c in range(count):
        wide = outer[c * size : (c + 1) * size]
        units.append(
            jnp.concatenate([wide[:, a : a + width] for a in range(0, wide.shape[1], width)], axis=0)
        )
    return units


def joined(*units):
    return [jnp.concatenate(parts, axis=0) for parts in zip(*units)]


def row_pieces(block, wide, channels, hidden, count):
    thin = channels // count
    broad = hidden // count
    if wide:
        size = block.shape[0] * block.shape[1] // hidden
        full = jnp.concatenate(
            [block[a : a + size] for a in range(0, block.shape[0], size)], axis=1
        )
        return [
            jnp.concatenate(
                [full[:, r * broad + a : r * broad + a + 2 * thin] for a in range(0, broad, 2 * thin)],
                axis=0,
            )
            for r in range(count)
        ]
    return [
        jnp.concatenate(
            [
                block[:, r * thin : (r + 1) * thin],
                block[:, channels + r * thin : channels + (r + 1) * thin],
            ],
            axis=1,
        )
        for r in range(count)
    ]


def bias_kernel(table, first):
    first[...] = expand_bias(table[:, 0])


def first_kernel(
    tokens,
    ids,
    qkv_w,
    proj_w,
    bias_ref,
    query_out,
    key_out,
    value_out,
    probs_out,
    mix_out,
    middle_out,
):
    rows, cols, channels = tokens.shape
    size = channels // (bias_ref.shape[1] // TOK)
    count = rows * cols
    surface = to_windows(tokens[...].astype(F32))
    normed = norm(surface)[0].astype(BF16)
    bias = bias_ref[...]
    masks = same_region(ids[...].astype(F32))
    query, key, value = (
        nn(normed, qkv_w[0, :, i * channels : (i + 1) * channels]).astype(BF16) for i in range(3)
    )
    query_out[...] = query
    key_out[...] = key
    value_out[...] = value
    mix_t = attend_all(query, key, value.T, bias, masks, size, probs_out)
    mix_out[...] = mix_t
    middle = (surface + tn(mix_t, proj_w[0])).astype(BF16)
    middle_out[...] = middle


def feed_kernel(
    middle_ref, ids, cotangent, inner_w, outer_w, first_out, near, far, pre_out, act_out, edge
):
    rows, cols, channels = first_out.shape
    count = rows * cols
    middle = middle_ref[...]
    normed = norm(middle.astype(F32))[0].astype(BF16)
    outs = []
    for at in range(0, count, 2 * TOK):
        pre = nn(normed[at : at + 2 * TOK], inner_w[0])
        pre_out[at : at + 2 * TOK] = pre
        act = (0.5 * pre * (1.0 + lax.erf(pre * math.sqrt(0.5)))).astype(BF16)
        act_out[at : at + 2 * TOK] = act
        outs.append(nt(act, outer_w[0]))
    result = (middle.astype(F32) + jnp.concatenate(outs, axis=0)).astype(BF16).astype(F32)
    grid = from_windows(result, rows, cols)
    first_out[...] = grid.astype(BF16)
    grads = cotangent[...].astype(F32)
    marks = ids[...].astype(F32)
    even = (lax.axis_index("rows") & 1) == 0
    for ref, down in ((near, even), (far, jnp.logical_not(even))):
        edge[...] = jnp.zeros(edge.shape, F32)
        for i in range(HALF):
            low = rows - HALF + i
            here = slice(i * cols, (i + 1) * cols)
            edge[here, :channels] = jnp.where(down, grid[low], grid[i])
            edge[here, channels:] = jnp.where(down, grads[low], grads[i])
        edge[HALF * cols : HALF * cols + HALF, :cols] = jnp.where(
            down, marks[rows - HALF :], marks[:HALF]
        )
        ref[...] = edge[...].astype(BF16)


def edge_kernel(
    first_out,
    cotangent,
    ids,
    upper_rim,
    upper_ids,
    lower_rim,
    lower_ids,
    from_near,
    from_far,
    up,
    down,
    near,
    far,
    ext_ids,
    edge,
    marks,
):
    rows, cols, channels = first_out.shape
    index = lax.axis_index("rows")
    at_top = index == 0
    at_bottom = index == lax.axis_size("rows") - 1
    grid = first_out[...].astype(F32)
    grads = cotangent[...].astype(F32)
    marks[HALF : HALF + rows, :] = ids[...].astype(F32)
    bands = []
    even = (index & 1) == 0
    got_near = from_near[...].astype(F32)
    got_far = from_far[...].astype(F32)
    for at_end, rim, rim_ids, got, target, place in (
        (at_top, upper_rim, upper_ids, jnp.where(even, got_far, got_near), up, 0),
        (at_bottom, lower_rim, lower_ids, jnp.where(even, got_near, got_far), down, HALF + rows),
    ):
        wide = HALF * cols
        tokens = jnp.where(at_end, rim[...].astype(F32).reshape(wide, channels), got[:wide, :channels])
        rest = jnp.where(at_end, 0.0, got[:wide, channels:])
        band = jnp.concatenate([tokens, rest], axis=1)
        target[...] = band.astype(BF16)
        marks[place : place + HALF, :] = jnp.where(
            at_end, rim_ids[...].astype(F32), got[wide : wide + HALF, :cols]
        )
        bands.append(band)
    ext_ids[...] = marks[...]
    total = rows + 2 * HALF
    even = (lax.axis_index("cols") & 1) == 0
    last = cols - HALF
    for ref, right in ((near, even), (far, jnp.logical_not(even))):
        edge[...] = jnp.zeros(edge.shape, F32)
        for i in range(total):
            here = slice(i * HALF, (i + 1) * HALF)
            if HALF <= i < HALF + rows:
                for values, part in ((grid, slice(0, channels)), (grads, slice(channels, None))):
                    row = values[i - HALF]
                    edge[here, part] = jnp.where(right, row[last:], row[:HALF])
            else:
                band, row = (bands[0], i) if i < HALF else (bands[1], i - HALF - rows)
                row = band[row * cols : (row + 1) * cols]
                edge[here, :] = jnp.where(right, row[last:], row[:HALF])
        edge[total * HALF : total * HALF + total, :cols] = marks[...]
        ref[...] = edge[...].astype(BF16)


def side_kernel(pre, key, table, slope, key_t, bias, onehot):
    onehot[...] = offset_rows(onehot.shape[0])
    bias[...] = expand_bias(table[:, 1])
    key_t[...] = key[...].T
    for at in range(0, pre.shape[0], TOK):
        x = pre[at : at + TOK]
        slope[at : at + TOK] = 0.5 * (1.0 + lax.erf(x * math.sqrt(0.5))) + x * (
            jnp.exp(-0.5 * x * x) * (1.0 / math.sqrt(2.0 * math.pi))
        )


def own_windows(rows, cols, channels, low, high):
    per_band = (cols + 2 * HALF) // WIN
    masks = []
    for a in range((rows + 2 * HALF) // WIN):
        for b in range(per_band):
            token = iota((TOK, channels), 0)
            row = a * WIN + (token >> 3)
            col = b * WIN + (token & (WIN - 1))
            masks.append((row >= low) & (row < high) & (col >= HALF) & (col < HALF + cols))
    return jnp.concatenate([ones_where(mask) for mask in masks], axis=0)


def second_kernel(
    first_out,
    cotangent,
    up,
    down,
    far,
    near,
    ext_ids,
    bias_ref,
    qkv_w,
    proj_w,
    inner_w,
    outer_w,
    after,
    grad_out,
    table_out,
    keep,
    send,
    xs,
    cs,
    probs_s,
):
    rows, cols, channels = first_out.shape
    total, wide = rows + 2 * HALF, cols + 2 * HALF
    width = bias_ref.shape[1]
    size = channels // (width // TOK)
    even = (lax.axis_index("cols") & 1) == 0
    got_near = near[...].astype(F32)
    got_far = far[...].astype(F32)
    left = jnp.where(even, got_far, got_near)
    right = jnp.where(even, got_near, got_far)
    for ref, source, at in ((xs, first_out, 0), (cs, cotangent, channels)):
        part = slice(at, at + channels)
        ref[HALF : HALF + rows, HALF : HALF + cols, :] = source[...].astype(F32)
        for edge, place in ((up, 0), (down, HALF + rows)):
            band = edge[...].astype(F32)[:, part]
            for i in range(HALF):
                ref[place + i, HALF : HALF + cols, :] = band[i * cols : (i + 1) * cols]
        for edge, place in ((left, 0), (right, HALF + cols)):
            band = edge[:, part]
            for i in range(total):
                ref[i, place : place + HALF, :] = band[i * HALF : (i + 1) * HALF]
    tail = slice(total * HALF, total * HALF + total)
    source_col = iota((cols, wide), 0)
    target_col = iota((cols, wide), 1)
    marks = sum(
        nn(values.astype(BF16), ones_where(target_col == source_col + shift))
        for values, shift in (
            (left[tail, :cols], HALF - cols),
            (ext_ids[...], HALF),
            (right[tail, :cols], HALF + cols),
        )
    )
    masks = same_region(marks)
    bias = bias_ref[...]
    surface = to_windows(xs[...])
    grad = to_windows(cs[...]).astype(BF16)
    count = surface.shape[0]
    unit_one, inverse_one = norm(surface)
    normed_one = unit_one.astype(BF16)
    weights = [qkv_w[1, :, i * channels : (i + 1) * channels] for i in range(3)]
    query, key, value = (nn(normed_one, w).astype(BF16) for w in weights)
    key_t, value_t = (nt(w.T, normed_one).astype(BF16) for w in weights[1:])
    mix_t = attend_all(query, key, value_t, bias, masks, size, probs_s)
    middle = (surface + tn(mix_t, proj_w[1])).astype(BF16).astype(F32)
    unit_two, inverse_two = norm(middle)
    normed_two = unit_two.astype(BF16)
    acts, grad_pres, grad_norms = [], [], []
    for at in range(0, count, 2 * TOK):
        here = slice(at, at + 2 * TOK)
        pre = nn(normed_two[here], inner_w[1])
        cdf = 0.5 * (1.0 + lax.erf(pre * math.sqrt(0.5)))
        acts.append((pre * cdf).astype(BF16))
        slope = cdf + pre * (jnp.exp(-0.5 * pre * pre) * (1.0 / math.sqrt(2.0 * math.pi)))
        grad_pre = (slope * nn(grad[here], outer_w[1])).astype(BF16)
        grad_pres.append(grad_pre)
        grad_norms.append(nt(grad_pre, inner_w[1]))
    act = jnp.concatenate(acts, axis=0)
    grad_pre = jnp.concatenate(grad_pres, axis=0)
    grad_norm = jnp.concatenate(grad_norms, axis=0)
    grad_middle = (grad.astype(F32) + norm_back(unit_two, inverse_two, grad_norm)).astype(BF16)
    index = lax.axis_index("rows")
    last = lax.axis_size("rows") - 1
    per_band = wide // WIN
    raw = nt(grad_middle, proj_w[1])
    grad_mixes = []
    for w in range(count // TOK):
        row = w // per_band * WIN + (iota((TOK, channels), 0) >> 3)
        low = jnp.where(index == 0, HALF, 0)
        high = jnp.where(index == last, HALF + rows, total)
        part = jnp.where((row >= low) & (row < high), raw[w * TOK : (w + 1) * TOK], 0.0)
        grad_mixes.append(part.astype(BF16))

    def weigh(w, term):
        lane = iota((1, width), 1)
        row = w // per_band * WIN + ((lane >> 3) & (WIN - 1))
        col = w % per_band * WIN + (lane & (WIN - 1))
        own = (row >= HALF) & (row < HALF + rows) & (col >= HALF) & (col < HALF + cols)
        return term * jnp.where(own, 1.0, 0.0)

    grad_query, grad_key, grad_value, bias_sum = attend_all_back(
        query, key_t, value, probs_s, grad_mixes, size, weigh
    )
    grad_norm = (
        nt(grad_query.T, weights[0]) + nt(grad_key, weights[1]) + nt(grad_value, weights[2])
    )
    grad_surface = grad_middle.astype(F32) + norm_back(unit_one, inverse_one, grad_norm)
    xs[...] = from_windows(grad_surface, total, wide)
    grad_out[...] = to_windows(xs[HALF : HALF + rows, HALF : HALF + cols, :]).astype(BF16)
    own = own_windows(rows, cols, channels, HALF, HALF + rows)
    low = jnp.where(index == 0, 0, HALF)
    high = jnp.where(index == last, total, HALF + rows)
    normed_one = normed_one * own_windows(rows, cols, channels, low, high)
    count = lax.axis_size("cols")
    qkv = [nn(grad_query, normed_one), tn(grad_key, normed_one), tn(grad_value, normed_one)]
    blocks = joined(
        narrow_units(
            [jnp.concatenate(qkv, axis=0), nn(mix_t, grad_middle * own).T], count
        ),
        narrow_units([tn(normed_two * own, grad_pre).T], count),
        wide_units(tn(grad * own, act), 2 * channels, count),
    )
    table_out[...] = fold_bias(bias_sum)
    write_parts(sort_by(blocks, lax.axis_index("cols") & 1, 2), [], (keep, send))


def third_kernel(
    grad_ref, middle_ref, act, slope, inner_w, outer_w, grad_out, keep, send
):
    count = grad_ref.shape[0]
    grad = grad_ref[...]
    unit, inverse = norm(middle_ref[...].astype(F32))
    grad_pres, grad_norms = [], []
    for at in range(0, count, 2 * TOK):
        here = slice(at, at + 2 * TOK)
        grad_pre = (slope[here] * nn(grad[here], outer_w[0])).astype(BF16)
        grad_pres.append(grad_pre)
        grad_norms.append(nt(grad_pre, inner_w[0]))
    grad_pre = jnp.concatenate(grad_pres, axis=0)
    grad_norm = jnp.concatenate(grad_norms, axis=0)
    grad_out[...] = (grad.astype(F32) + norm_back(unit, inverse, grad_norm)).astype(BF16)
    number = lax.axis_size("cols")
    blocks = joined(
        narrow_units([tn(grad_pre, unit.astype(BF16))], number),
        wide_units(tn(grad, act[...]), 2 * grad.shape[1], number),
    )
    write_parts(sort_by(blocks, lax.axis_index("cols") & 1, 2), [], (keep, send))


def fourth_kernel(
    grad_ref, query, key_t, value, probs_ref, proj_w, query_out, key_out, value_out, bias_out
):
    count, channels = grad_ref.shape
    width = probs_ref.shape[2]
    grad_mix = nt(grad_ref[...], proj_w[0]).astype(BF16)
    grad_mixes = [grad_mix[at : at + TOK] for at in range(0, count, TOK)]
    query_out[...], key_out[...], value_out[...], bias_out[...] = attend_all_back(
        query,
        key_t,
        value,
        probs_ref,
        grad_mixes,
        channels // (width // TOK),
        lambda w, term: term,
    )


def fifth_kernel(
    tokens,
    grad_ref,
    mix_t,
    grad_query,
    grad_key,
    grad_value,
    bias_sum,
    table_two,
    qkv_w,
    after,
    token_grad,
    keep,
    send,
):
    rows, cols, channels = tokens.shape
    unit, inverse = norm(to_windows(tokens[...].astype(F32)))
    normed = unit.astype(BF16)
    grad_middle = grad_ref[...]
    grads = [grad_query[...].T, grad_key[...], grad_value[...]]
    number = lax.axis_size("cols")
    qkv = [nn(grad_query[...], normed), tn(grads[1], normed), tn(grads[2], normed)]
    blocks = narrow_units(
        [jnp.concatenate(qkv, axis=0), nn(mix_t[...], grad_middle).T], number
    )
    tails = [table_tail([fold_wide(bias_sum[...]), table_two[...]], 2 * channels)]
    write_parts(sort_by(blocks, lax.axis_index("cols") & 1, 2), tails, (keep, send))
    grad_norm = sum(
        nt(grad, qkv_w[0, :, i * channels : (i + 1) * channels]) for i, grad in enumerate(grads)
    )
    grad_surface = grad_middle.astype(F32) + norm_back(unit, inverse, grad_norm)
    token_grad[...] = from_windows(grad_surface, rows, cols).astype(BF16)


def summed(refs):
    values = [ref[...].astype(F32) for ref in refs]
    if len(values) == 4:
        values = [values[i] for i in ORDERED]
    return tree_sum(values)


def cut(values, count):
    rows = values.shape[0] // count
    return [values[i * rows : (i + 1) * rows] for i in range(count)]


def ordered(parts):
    return [parts[i] for i in ARRIVAL] if len(parts) == 4 else parts


def join_kernel(count, bit, ways, tail, *refs):
    sources = refs[: len(refs) - ways]
    blocks = []
    rest = []
    for n in range(0, len(sources), 2):
        part = summed(sources[n : n + 2])
        edge = part.shape[0] - tail
        blocks.append(cut(part[:edge], count))
        rest += [part[edge:]] if tail else []
    place = (lax.axis_index("cols") >> bit) & (ways - 1)
    parts = ordered(sort_by(joined(*blocks), place, ways))
    write_parts(parts, rest, refs[len(refs) - ways :])


def step_kernel(axis, count, bit, before, ways, tail, *refs):
    both = summed(refs[:before])
    edge = both.shape[0] - tail
    place = (lax.axis_index(axis) >> bit) & (ways - 1)
    parts = sort_by(cut(both[:edge], count), place, ways)
    write_parts(ordered(parts), [both[edge:]] if tail else [], refs[before:])


def padded(block):
    pad = jnp.zeros((block.shape[0], LANES - block.shape[1]), F32)
    return jnp.concatenate([block, pad], axis=1)


def dense(block, used):
    if used * 4 != LANES * 3:
        return padded(block)
    cut_at = block.shape[0] // 4
    side = jnp.concatenate(
        [block[3 * cut_at :, a : a + LANES // 4] for a in range(0, used, LANES // 4)], axis=0
    )
    return jnp.concatenate([block[: 3 * cut_at], side], axis=1)


def undense(block, used):
    if used * 4 != LANES * 3:
        return block
    cut_at = block.shape[0] // 3
    side = [block[i * cut_at : (i + 1) * cut_at, used:] for i in range(3)]
    return jnp.concatenate([block[:, :used], jnp.concatenate(side, axis=1)], axis=0)


def first_turn_kernel(channels, hidden, before, *refs):
    both = summed(refs[:before])
    two, ffn = refs[before:]
    count = lax.axis_size("rows")
    used = 2 * channels // count
    pieces = [
        row_pieces(unit, n in (1, 4), channels, hidden, count)
        for n, unit in enumerate(cut(both, 5))
    ]
    ffn[...] = padded(jnp.concatenate(joined(*pieces[:2]), axis=0))
    two[...] = jnp.concatenate([dense(b, used) for b in joined(*pieces[2:])], axis=0)


def merge_kernel(channels, hidden, before, ways, *refs):
    both = summed(refs[:before])
    two, ffn = refs[before : before + 2]
    count = lax.axis_size("rows")
    edge = both.shape[0] - 2 * WIN
    used = 2 * channels // count
    att = row_pieces(both[:edge], False, channels, hidden, count)
    one = [dense(b, used) for b in joined(att, cut(ffn[...][:, :used], count))]
    parts = sort_by(
        joined(one, cut(two[...], count)), lax.axis_index("rows") & (ways - 1), ways
    )
    tables = [rows_table(both[edge + n * WIN : edge + (n + 1) * WIN]) for n in range(2)]
    write_parts(ordered(parts), [table_tail(tables, LANES)], refs[before + 2 :])


def last_kernel(sizes, scale, before, onehot_ref, *refs):
    (qkv_cols, inner_cols, proj_cols), thin, broad = sizes
    qkv, proj, inner, outer, table = refs[before:]
    total = summed(refs[:before]) * scale
    edge = total.shape[0] - 4 * WIN
    heads = table.shape[0]
    onehot = onehot_ref[...]
    for b in range(2):
        both = undense(total[b * edge // 2 : (b + 1) * edge // 2], 2 * thin)
        low, mid, wide = cut(both, 3)
        low = jnp.concatenate([low[:, :thin], low[:, thin : 2 * thin]], axis=0)
        mid = jnp.concatenate([mid[:, :thin], mid[:, thin : 2 * thin]], axis=0)
        qkv[b] = low[:qkv_cols].T
        proj[b] = low[qkv_cols:]
        inner[b] = mid.T
        outer[b] = jnp.concatenate(
            [part[:, : 2 * thin] for part in cut(wide, broad // (2 * thin))], axis=1
        )
        sums = rows_table(total[edge + 2 * b * WIN : edge + 2 * (b + 1) * WIN])
        table[:, b] = sum(nt(part, onehot) for part in split(sums, 2))[:heads]


def call(kernel, outs, scratch, *operands, cost=0.2):
    return pl.pallas_call(
        kernel,
        out_shape=[jax.ShapeDtypeStruct(shape, kind) for shape, kind in outs],
        scratch_shapes=scratch,
        cost_estimate=pl.CostEstimate(
            flops=int(cost * 1e9), bytes_accessed=1024, transcendentals=0
        ),
        compiler_params=pltpu.CompilerParams(vmem_limit_bytes=VMEM_LIMIT),
    )(*operands)


def flip(values, axis, bit):
    count = lax.axis_size(axis)
    return lax.ppermute(values, axis, [(i, i ^ bit) for i in range(count)])


def swap_cols(values, offset):
    count = lax.axis_size("cols")
    pairs = []
    for i in range(offset, count, 2):
        j = (i + 1) % count
        pairs += [(i, j), (j, i)]
    return lax.ppermute(values, "cols", pairs)


def swap_rows(values, offset):
    count = lax.axis_size("rows")
    cols = lax.axis_size("cols")
    partner = {}
    for i in range(offset, count - 1, 2):
        partner[i], partner[i + 1] = i + 1, i
    pairs = []
    for r in range(count):
        for c in range(cols):
            target = (partner[r], c) if r in partner else (r, c ^ FILL)
            pairs.append((r * cols + c, target[0] * cols + target[1]))
    return lax.ppermute(values, ("rows", "cols"), pairs)


def spread_parts(parts, axis, bit):
    ways = len(parts)
    order = ARRIVAL if ways == 4 else range(ways)
    return [flip(part, axis, j << bit) if j else part for j, part in zip(order, parts)]


def bit_groups(bits, size):
    return [min(size, bits - at) for at in range(0, bits, size)]


def reduce_cols(pairs, tail, width, units):
    got = []
    for keep, send in pairs:
        got += [keep, flip(send, "cols", 1)]
    count = lax.axis_size("cols") // 2
    bit = 1
    kept = None
    for size in bit_groups(count.bit_length() - 1, 2):
        ways = 1 << size
        shape = ((count // ways * units + tail, width), BF16)
        if bit == 1:
            kernel = functools.partial(join_kernel, count, bit, ways, tail)
        else:
            kernel = functools.partial(step_kernel, "cols", count, bit, len(got), ways, tail)
        parts = call(kernel, [shape] * ways, [], *got)
        kept = parts[0] if kept is None else kept
        got = spread_parts(parts, "cols", bit)
        bit += size
        count //= ways
    return got, kept


def reduce_rows(got, others, channels, hidden, rows):
    count = lax.axis_size("rows")
    tail = 4 * WIN
    bit = 0
    for size in bit_groups(count.bit_length() - 1, 2):
        ways = 1 << size
        shape = ((count // ways * rows * 2 + tail, LANES), BF16)
        if bit == 0:
            kernel = functools.partial(merge_kernel, channels, hidden, len(got), ways)
            got = [*got, *others]
        else:
            kernel = functools.partial(step_kernel, "rows", count, bit, len(got), ways, tail)
        got = spread_parts(call(kernel, [shape] * ways, [], *got), "rows", bit)
        bit += size
        count //= ways
    return got


def local(
    tokens,
    region_ids,
    upper_rim,
    upper_ids,
    lower_rim,
    lower_ids,
    cotangent,
    qkv_weight,
    proj_weight,
    inner_weight,
    outer_weight,
    bias_table,
):
    rows, cols, channels = tokens.shape
    hidden = inner_weight.shape[2]
    length, heads = bias_table.shape[1:]
    outer_weight = jnp.swapaxes(outer_weight, 1, 2)
    bias_table = jnp.transpose(bias_table, (2, 0, 1))
    col_count = lax.axis_size("cols")
    row_count = lax.axis_size("rows")
    count = rows * cols
    width = heads * TOK
    total = rows + 2 * HALF
    flat = ((count, channels), BF16)
    band = (HALF * cols + 2 * WIN, 2 * channels)
    pair = ((TOK, width), F32)
    (bias_one,) = call(bias_kernel, [pair], [], bias_table, cost=6.0)
    query, key, value, probs, mix, middle = call(
        first_kernel,
        [flat, flat, flat, ((count // TOK, TOK, width), F32), ((channels, count), BF16), flat],
        [],
        tokens,
        region_ids,
        qkv_weight,
        proj_weight,
        bias_one,
        cost=2.0,
    )
    first_out, near, far, pre, act = call(
        feed_kernel,
        [
            ((rows, cols, channels), BF16),
            (band, BF16),
            (band, BF16),
            ((count, hidden), F32),
            ((count, hidden), BF16),
        ],
        [pltpu.VMEM(band, F32)],
        middle,
        region_ids,
        cotangent,
        inner_weight,
        outer_weight,
        cost=1.0,
    )
    from_near = swap_rows(near, 0)
    from_far = swap_rows(far, 1)
    slope, key_t, bias_two, onehot = call(
        side_kernel,
        [((count, hidden), F32), ((channels, count), BF16), pair, ((length, 2 * LANES), BF16)],
        [],
        pre,
        key,
        bias_table,
        cost=1.0,
    )
    strip = (total * HALF + total, 2 * channels)
    up, down, near, far, ext_ids = call(
        edge_kernel,
        [
            ((HALF * cols, 2 * channels), BF16),
            ((HALF * cols, 2 * channels), BF16),
            (strip, BF16),
            (strip, BF16),
            ((total, cols), F32),
        ],
        [pltpu.VMEM(strip, F32), pltpu.VMEM((total, cols), F32)],
        first_out,
        cotangent,
        region_ids,
        upper_rim,
        upper_ids,
        lower_rim,
        lower_ids,
        from_near,
        from_far,
    )
    far = swap_cols(far, 1)
    near = swap_cols(near, 0)
    units = 4 * channels // col_count // 2
    slots = col_count // 2

    def packed(number, tail):
        return ((slots * number * units + tail, 2 * channels), BF16)

    grid = (total, cols + 2 * HALF, channels)
    grad_first, table_two, keep_two, send_two = call(
        second_kernel,
        [flat, ((WIN, 2 * LANES), F32), packed(3, 0), packed(3, 0)],
        [
            pltpu.VMEM(grid, F32),
            pltpu.VMEM(grid, F32),
            pltpu.VMEM((grid[0] * grid[1] // TOK, TOK, width), F32),
        ],
        first_out,
        cotangent,
        up,
        down,
        far,
        near,
        ext_ids,
        bias_two,
        qkv_weight,
        proj_weight,
        inner_weight,
        outer_weight,
        key_t,
        cost=12.0,
    )
    grad_middle, keep_ffn, send_ffn = call(
        third_kernel,
        [flat, packed(2, 0), packed(2, 0)],
        [],
        grad_first,
        middle,
        act,
        slope,
        inner_weight,
        outer_weight,
        cost=1.0,
    )
    got, kept = reduce_cols(
        [(keep_ffn, send_ffn), (keep_two, send_two)], 0, 2 * channels, 5 * units
    )
    thin = channels // row_count
    piece = units * 3 // 4 * 3 if 8 * thin == 3 * LANES else units * 3
    others = call(
        functools.partial(first_turn_kernel, channels, hidden, len(got)),
        [
            ((row_count * piece, LANES), F32),
            ((row_count * 2 * units, LANES), F32),
        ],
        [],
        *got,
        cost=TURN_COST,
    )
    grad_query, grad_key, grad_value, bias_sum = call(
        fourth_kernel,
        [((channels, count), BF16), flat, flat, pair],
        [],
        grad_middle,
        query,
        key_t,
        value,
        probs,
        proj_weight,
        cost=2.0,
    )
    token_grad, keep_one, send_one = call(
        fifth_kernel,
        [((rows, cols, channels), BF16), packed(1, 2 * WIN), packed(1, 2 * WIN)],
        [],
        tokens,
        grad_middle,
        mix,
        grad_query,
        grad_key,
        grad_value,
        bias_sum,
        table_two,
        qkv_weight,
        kept,
        cost=4.0,
    )
    got, _ = reduce_cols([(keep_one, send_one)], 2 * WIN, 2 * channels, units)
    got = reduce_rows(got, others, channels, hidden, piece)
    broad = hidden // row_count
    sizes = (
        (3 * channels // col_count, hidden // col_count, channels // col_count),
        thin,
        broad,
    )
    qkv_grad, proj_grad, inner_grad, outer_grad, table_grad = call(
        functools.partial(last_kernel, sizes, 1.0 / (row_count * col_count), len(got)),
        [
            ((2, thin, sizes[0][0]), F32),
            ((2, sizes[0][2], thin), F32),
            ((2, thin, sizes[0][1]), F32),
            ((2, sizes[0][2], broad), F32),
            ((heads, 2, length), F32),
        ],
        [],
        onehot,
        *got,
    )
    proj_grad = jnp.swapaxes(proj_grad, 1, 2)
    outer_grad = jnp.swapaxes(outer_grad, 1, 2)
    table_grad = jnp.transpose(table_grad, (1, 2, 0))
    return token_grad, qkv_grad, proj_grad, inner_grad, outer_grad, table_grad


def solution(mesh):
    return jax.shard_map(
        local,
        mesh=mesh,
        in_specs=(
            P("rows", "cols", None),
            P("rows", "cols"),
            P(None, "cols", None),
            P(None, "cols"),
            P(None, "cols", None),
            P(None, "cols"),
            P("rows", "cols", None),
            P(),
            P(),
            P(),
            P(),
            P(),
        ),
        out_specs=(
            P("rows", "cols", None),
            P(None, "rows", "cols"),
            P(None, "rows", "cols"),
            P(None, "rows", "cols"),
            P(None, "rows", "cols"),
            P(),
        ),
        check_vma=False,
    )
```
